32 devices in a mesh: paths: 32 (over z, y, x, core).
Axes of the slice: x: 2, y: 2, z: 4, core: 2. Of those that a mesh axis runs over, the one named last changes fastest.
Arguments:
- params: float32 [256, 4], replicated, may hold values from -0.9 to 2, as said below
- increments: bfloat16 [2, 64, 4096], P(None, None, 'paths'), may hold values from -5 to 5
- w_in: bfloat16 [6, 1024], replicated, may hold values from -2.5 to 2.5
- b_in: float32 [1024], replicated, may hold values from -3 to 3
- w_mid: bfloat16 [1024, 1024], replicated, may hold values from -0.1875 to 0.1875
- b_mid: float32 [1024], replicated, may hold values from -3 to 3
- w_out: bfloat16 [1024], replicated, may hold values from -0.1875 to 0.1875
- b_out: float32 [1], replicated, may hold values from -3 to 3
Outputs:
- prices: float32 [256, 88], P('paths')
- direction_w_in: float32 [6, 1024], replicated
- direction_b_in: float32 [1024], replicated
- direction_w_mid: float32 [1024, 1024], replicated
- direction_b_mid: float32 [1024], replicated
- direction_w_out: float32 [1024], replicated
- direction_b_out: float32 [1], replicated
The draws below stay inside these ranges and needn't reach their ends.
Inputs may be any that keep to these rules, and one draw needn't show every extreme that they name: `params`: each row holds a Hurst index in [0.05, 0.45], a vol-of-vol in [0.8, 2.0], a correlation in [-0.9, -0.3] and an initial forward variance in [0.01, 0.15].
All inputs are finite; a program needn't handle non-finite values.
Results may differ from the reference program's by a relative error of at most 0.0003.
The reference program's roundings to bfloat16 on the way count: a program that leaves them out, or rounds other values in their place, can miss the bound.
Values sent between devices are 32-bit elements; how exact they have to be, the bound alone decides.
No kernel may reach another device: no remote copies, remote signals or barrier semaphores. Data moves between devices by JAX's collectives and lax.ppermute only.
A program may use at most 64 MiB of HBM per device.

```python
import jax
import jax.numpy as jnp
from jax import lax

STEPS = 64
MATS = 8
STRIKES = 11
INPUTS = 6
WIDTH = 1024
PAIRS = 88
SETS = 256
PATHS = 4096


def draw_params(key, part):
    uniform_draw = jax.random.uniform(key, (SETS, 4), jnp.float32)
    hurst = 0.05 + 0.4 * uniform_draw[:, 0]
    vol_of_vol = 0.8 + 1.2 * uniform_draw[:, 1]
    correl = -0.9 + 0.6 * uniform_draw[:, 2]
    rising = 1.0 + 2.0 * jnp.arange(SETS, dtype=jnp.float32) / SETS
    forward_var = 0.01 * jnp.exp(jnp.log(5.0) * uniform_draw[:, 3]) * rising
    return jnp.stack([hurst, vol_of_vol, correl, forward_var], axis=1).astype(jnp.float32)


def level_of(stream_key, extent, shards, low, top_value):
    def one(dim, blocks):
        draws = jax.random.uniform(jax.random.fold_in(jax.random.fold_in(stream_key, 6), dim), (blocks,), jnp.float32, low / len(shards), top_value / len(shards))
        return jnp.repeat(jnp.exp(draws), extent[dim] // blocks).reshape((-1,) + (1,) * (len(extent) - dim - 1))

    gain = one(*shards[0])
    for cut in shards[1:]:
        gain = gain * one(*cut)
    return gain


def normal_values(stream_key, dims, spread, reach, split=(), kind=jnp.bfloat16):
    level = level_of(stream_key, dims, split, -0.22, 0.18) if split else 1.0
    values = jax.random.normal(stream_key, dims, jnp.float32) * spread * level
    return jnp.minimum(jnp.maximum(values, -reach), reach).astype(kind)


def setup_inputs(seed: int = 0) -> dict:
    arg_keys = jax.random.split(jax.random.key(seed), 9)
    params = draw_params(jax.random.fold_in(arg_keys[8], 71), 0)
    increments = normal_values(arg_keys[1], (2, STEPS, PATHS), 1.0, 5.0, ((2, 32),))
    w_in = normal_values(arg_keys[2], (INPUTS, WIDTH), INPUTS ** -0.5, 2.5)
    b_in = normal_values(arg_keys[3], (WIDTH,), 0.5, 3.0, (), jnp.float32)
    w_mid = normal_values(arg_keys[4], (WIDTH, WIDTH), WIDTH ** -0.5, 0.1875)
    b_mid = normal_values(arg_keys[5], (WIDTH,), 0.5, 3.0, (), jnp.float32)
    w_out = normal_values(arg_keys[6], (WIDTH,), WIDTH ** -0.5, 0.1875)
    b_out = normal_values(arg_keys[7], (1,), 0.5, 3.0, (), jnp.float32)
    return {"params": params, "increments": increments, "w_in": w_in, "b_in": b_in, "w_mid": w_mid, "b_mid": b_mid, "w_out": w_out, "b_out": b_out}


EPSILON = 1e-06

def strike_grid():
    tenors = (jnp.arange(MATS, dtype=jnp.float32) + 1.0) / MATS
    offsets = jnp.arange(STRIKES, dtype=jnp.float32) - (STRIKES - 1) / 2.0
    log_strike = 0.05 * offsets[None, :] * jnp.sqrt(tenors)[:, None]
    return (tenors, log_strike)

def payoff_sums(block_params, increments):
    count = block_params.shape[0]
    paths_here = increments.shape[2]
    hurst = block_params[:, 0]
    vol_of_vol = block_params[:, 1]
    correl = block_params[:, 2]
    forward_var = block_params[:, 3]
    delta_t = 1.0 / STEPS
    position = jnp.arange(STEPS, dtype=jnp.float32)
    lag = position[:, None] - position[None, :]
    lag_high = jnp.maximum(lag, 1.0)
    exponent = (hurst + 0.5)[:, None, None]
    powers = jnp.power(lag_high[None], exponent) - jnp.power(lag_high[None] - 1.0, exponent)
    front = jnp.sqrt(2.0 * hurst) * jnp.power(delta_t, hurst) / (hurst + 0.5)
    kernel = jnp.where((lag >= 1.0)[None], powers * front[:, None, None], 0.0).astype(jnp.bfloat16)
    drive = jnp.dot(kernel.reshape(count * STEPS, STEPS), increments[0], preferred_element_type=jnp.float32)
    drive = drive.reshape(count, STEPS, paths_here)
    times = position * delta_t
    compensator = 0.5 * vol_of_vol[:, None] * vol_of_vol[:, None] * jnp.power(times[None, :], 2.0 * hurst[:, None])
    variance = forward_var[:, None, None] * jnp.exp(vol_of_vol[:, None, None] * drive - compensator[:, :, None])
    first_noise = increments[0].astype(jnp.float32)
    second_noise = increments[1].astype(jnp.float32)
    shock = correl[:, None, None] * first_noise[None] + jnp.sqrt(1.0 - correl * correl)[:, None, None] * second_noise[None]
    moves = jnp.sqrt(variance * delta_t) * shock - 0.5 * delta_t * variance
    log_spot = jnp.cumsum(moves.reshape(count, MATS, STEPS // MATS, paths_here).sum(axis=2), axis=1)
    tenors, log_strike = strike_grid()
    spot = jnp.exp(log_spot)
    gains = jnp.maximum(spot[:, :, None, :] - jnp.exp(log_strike)[None, :, :, None], 0.0)
    return lax.optimization_barrier(jnp.sum(gains, axis=3)).reshape(count, PAIRS)

def features(set_rows):
    count = set_rows.shape[0]
    tenors, log_strike = strike_grid()
    scaled = set_rows * jnp.array([4.0, 1.0, 1.0, 20.0], dtype=jnp.float32)
    per_pair = jnp.stack([4.0 * log_strike.reshape(PAIRS), jnp.repeat(tenors, STRIKES)], axis=1)
    left = jnp.broadcast_to(scaled[:, None, :], (count, PAIRS, 4))
    right = jnp.broadcast_to(per_pair[None], (count, PAIRS, 2))
    return jnp.concatenate([left, right], axis=2).reshape(count * PAIRS, 6).astype(jnp.bfloat16)

def silu_slope(value):
    logistic = jax.nn.sigmoid(value)
    return logistic * (1.0 + value * (1.0 - logistic))

def contract_rows(left, right):
    return lax.dot_general(left, right, (((0,), (0,)), ((), ())), preferred_element_type=jnp.float32)

def local_terms(inputs, target, w_in, b_in, w_mid, b_mid, w_out, b_out, inv_sets):
    raw_in = jnp.dot(inputs, w_in, preferred_element_type=jnp.float32) + b_in
    hidden_in = jax.nn.silu(raw_in).astype(jnp.bfloat16)
    raw_mid = jnp.dot(hidden_in, w_mid, preferred_element_type=jnp.float32) + b_mid
    hidden_mid = jax.nn.silu(raw_mid).astype(jnp.bfloat16)
    predicted = jnp.dot(hidden_mid, w_out, preferred_element_type=jnp.float32) + b_out[0]
    slope = (predicted - target) * inv_sets
    grad_out = lax.optimization_barrier(jnp.sum(hidden_mid.astype(jnp.float32) * slope[:, None], axis=0))
    grad_bout = lax.optimization_barrier(jnp.sum(slope, keepdims=True))
    delta_mid = (slope[:, None] * w_out.astype(jnp.float32)[None, :] * silu_slope(raw_mid)).astype(jnp.bfloat16)
    grad_bmid = lax.optimization_barrier(jnp.sum(delta_mid.astype(jnp.float32), axis=0))
    backward = lax.dot_general(delta_mid, w_mid, (((1,), (1,)), ((), ())), preferred_element_type=jnp.float32)
    delta_in = (backward * silu_slope(raw_in)).astype(jnp.bfloat16)
    grad_in = contract_rows(inputs, delta_in)
    grad_bin = lax.optimization_barrier(jnp.sum(delta_in.astype(jnp.float32), axis=0))
    return ((grad_in, grad_bin, grad_bmid, grad_out, grad_bout), hidden_in, delta_mid)

def directions(grad_w, grad_b):
    entries = grad_w.size + grad_b.size
    mean_square = (jnp.sum(grad_w * grad_w) + jnp.sum(grad_b * grad_b)) / entries
    factor = lax.rsqrt(mean_square + EPSILON)
    return (grad_w * factor, grad_b * factor)

def reference(params, increments, w_in, b_in, w_mid, b_mid, w_out, b_out):
    groups = params.reshape(SETS // 8, 8, 4)
    sums = lax.map(lambda group: payoff_sums(group, increments), groups)
    prices = sums.reshape(SETS, PAIRS) / PATHS
    inv_sets = 1.0 / SETS
    width = w_mid.shape[0]

    def accumulate(carry, element):
        group, target = element
        small, hidden_in, delta_mid = local_terms(features(group), target.reshape(-1), w_in, b_in, w_mid, b_mid, w_out, b_out, inv_sets)
        totals = small + (contract_rows(hidden_in, delta_mid),)
        return (tuple((value + extra for value, extra in zip(carry, totals))), None)
    initial = (jnp.zeros((6, width), jnp.float32), jnp.zeros((width,), jnp.float32), jnp.zeros((width,), jnp.float32), jnp.zeros((width,), jnp.float32), jnp.zeros((1,), jnp.float32), jnp.zeros((width, width), jnp.float32))
    totals, unused = lax.scan(accumulate, initial, (groups, prices.reshape(SETS // 8, 8, PAIRS)))
    grad_in, grad_bin, grad_bmid, grad_out, grad_bout, grad_mid = totals
    direction_w_in, direction_b_in = directions(grad_in, grad_bin)
    direction_w_mid, direction_b_mid = directions(grad_mid, grad_bmid)
    direction_w_out, direction_b_out = directions(grad_out, grad_bout)
    return (prices, direction_w_in, direction_b_in, direction_w_mid, direction_b_mid, direction_w_out, direction_b_out)
```

```python
import math

import jax
import jax.numpy as jnp
import numpy as np
from jax import lax
from jax.experimental import pallas as pl
from jax.experimental.pallas import tpu as pltpu
from jax.sharding import PartitionSpec as P

STEPS = 64
MATS = 8
STRIKES = 11
PAIRS = 88
WIDTH = 1024
LANES = 128
SMALL_ROWS = 10
EPSILON = 1e-06


TENORS = (np.arange(MATS, dtype=np.float32) + np.float32(1.0)) / np.float32(MATS)
OFFSETS = np.arange(STRIKES, dtype=np.float32) - np.float32((STRIKES - 1) / 2.0)
LOG_STRIKE = np.float32(0.05) * OFFSETS[None, :] * np.sqrt(TENORS)[:, None]
STRIKE = np.exp(LOG_STRIKE).astype(np.float32)
SET_BLOCK = 256
LOG2E = 1.4426950408889634


def strike_grid():
    return (jnp.asarray(TENORS), jnp.asarray(LOG_STRIKE))


def bf16_pieces(value):
    high = value.astype(jnp.bfloat16)
    rest = value - high.astype(jnp.float32)
    mid = rest.astype(jnp.bfloat16)
    low = (rest - mid.astype(jnp.float32)).astype(jnp.bfloat16)
    return high, mid, low


def pricing_kernel(strike_ref, params_ref, inc_ref, out_ref, lags_ref, noise_ref, comp_ref, pay_ref):
    sets = params_ref.shape[1]
    paths = inc_ref.shape[2]
    hurst = params_ref[0:1, :]
    vol_of_vol = params_ref[1:2, :]
    correl = params_ref[2:3, :]
    forward_var = params_ref[3:4, :]
    delta_t = 1.0 / STEPS

    lag = (LANES - lax.broadcasted_iota(jnp.int32, (LANES, 1), 0)).astype(jnp.float32)
    exponent = hurst + 0.5
    here = jnp.exp2(exponent * jnp.log2(lag))
    before = jnp.exp2(exponent * jnp.log2(jnp.maximum(lag - 1.0, 1.0)))
    before = jnp.where(lag > 1.5, before, 0.0)
    front = jnp.sqrt(2.0 * hurst) * jnp.exp2(hurst * math.log2(delta_t)) / exponent
    weights = jnp.where(lag < STEPS - 0.5, (here - before) * front, 0.0).astype(jnp.bfloat16)

    half_scale = vol_of_vol * (0.5 * LOG2E)
    step = lax.broadcasted_iota(jnp.int32, (STEPS, 1), 0).astype(jnp.float32)
    powers = jnp.exp2(2.0 * hurst * jnp.log2(jnp.maximum(step, 1.0) * delta_t))
    comp_ref[...] = jnp.where(step > 0.5, powers * (0.25 * LOG2E * vol_of_vol * vol_of_vol), 0.0)

    root = jnp.sqrt(forward_var * delta_t)
    back = 2.0 / root
    growth = (0.5 * LOG2E) * forward_var * delta_t
    noise_weights = jnp.concatenate(
        [
            jnp.broadcast_to(piece.astype(jnp.float32), (8, sets))
            for value in (correl * back, jnp.sqrt(1.0 - correl * correl) * back)
            for piece in bf16_pieces(value)
        ]
        + [jnp.zeros((LANES - 48, sets), jnp.float32)],
        axis=0,
    ).astype(jnp.bfloat16)

    first = inc_ref[0].astype(jnp.float32)
    second = inc_ref[1].astype(jnp.float32)
    lags_ref[...] = jnp.concatenate([first, jnp.zeros((LANES - STEPS, paths), jnp.float32)], 0).T
    for m in range(MATS):
        rows = slice(8 * m, 8 * m + 8)
        block = jnp.concatenate(
            [first[rows]] * 3 + [second[rows]] * 3 + [jnp.zeros((LANES - 48, paths), jnp.float32)], 0
        )
        noise_ref[m] = block.T.astype(jnp.bfloat16)
    lane = lax.broadcasted_iota(jnp.int32, (paths, LANES), 1)

    def maturity(m, total):
        noise = noise_ref[m]
        for k in range(8):
            i = 8 * m + k
            window = lags_ref[...] if k == 0 else pltpu.roll(lags_ref[...], LANES - k, 1)
            drive = jnp.dot(
                window.astype(jnp.bfloat16), weights, preferred_element_type=jnp.float32
            )
            picked = jnp.where(lane % 8 == k, noise.astype(jnp.float32), 0.0).astype(jnp.bfloat16)
            shock = jnp.dot(picked, noise_weights, preferred_element_type=jnp.float32)
            root_variance = jnp.exp2(drive * half_scale - comp_ref[pl.ds(i, 1), :])
            total = total + root_variance * (shock - root_variance)
        lags_ref[...] = pltpu.roll(lags_ref[...], LANES - 8, 1)
        spot = jnp.exp2(total * growth)
        for j in range(STRIKES):
            strike = strike_ref[m, j]
            gains = jnp.maximum(spot, strike).reshape(paths // 8, 8, sets).sum(axis=0)
            gains = gains - strike * (paths // 8)
            pay_ref[pl.ds(m * STRIKES + j, 1), :] = jnp.sum(gains, axis=0, keepdims=True)
        return total

    lax.fori_loop(0, MATS, maturity, jnp.zeros((paths, sets), jnp.float32))
    out_ref[...] = pay_ref[...].T[:, :PAIRS]


def payoff_sums(params, increments):
    count = params.shape[0]
    paths = increments.shape[2]
    sets = math.gcd(count, SET_BLOCK)
    return pl.pallas_call(
        pricing_kernel,
        grid=(count // sets,),
        in_specs=[
            pl.BlockSpec(memory_space=pltpu.SMEM),
            pl.BlockSpec((4, sets), lambda b: (0, b)),
            pl.BlockSpec((2, STEPS, paths), lambda b: (0, 0, 0)),
        ],
        out_specs=pl.BlockSpec((sets, PAIRS), lambda b: (b, 0)),
        out_shape=jax.ShapeDtypeStruct((count, PAIRS), jnp.float32),
        scratch_shapes=[
            pltpu.VMEM((paths, LANES), jnp.float32),
            pltpu.VMEM((MATS, paths, LANES), jnp.bfloat16),
            pltpu.VMEM((STEPS, sets), jnp.float32),
            pltpu.VMEM((LANES, sets), jnp.float32),
        ],
        compiler_params=pltpu.CompilerParams(vmem_limit_bytes=32 * 1024 * 1024),
        name="pricing",
    )(jnp.asarray(STRIKE), params.T, increments)


def features(set_rows):
    count = set_rows.shape[0]
    tenors, log_strike = strike_grid()
    scaled = set_rows * jnp.array([4.0, 1.0, 1.0, 20.0], dtype=jnp.float32)
    per_pair = jnp.stack([4.0 * log_strike.reshape(PAIRS), jnp.repeat(tenors, STRIKES)], axis=1)
    left = jnp.broadcast_to(scaled[:, None, :], (count, PAIRS, 4))
    right = jnp.broadcast_to(per_pair[None], (count, PAIRS, 2))
    return jnp.concatenate([left, right], axis=2).reshape(count * PAIRS, 6).astype(jnp.bfloat16)


def silu_slope(value):
    logistic = jax.nn.sigmoid(value)
    return logistic * (1.0 + value * (1.0 - logistic))


def contract_rows(left, right):
    return lax.dot_general(
        left, right, (((0,), (0,)), ((), ())), preferred_element_type=jnp.float32
    )


def block_gradients(inputs, target, w_in, b_in, w_mid, b_mid, w_out, b_out, inv_sets, block, cols):
    def own(array, axis):
        return lax.dynamic_slice_in_dim(array, block * cols, cols, axis)

    raw_in = jnp.dot(inputs, w_in, preferred_element_type=jnp.float32) + b_in
    hidden_in = jax.nn.silu(raw_in).astype(jnp.bfloat16)
    raw_mid = jnp.dot(hidden_in, w_mid, preferred_element_type=jnp.float32) + b_mid
    hidden_mid = jax.nn.silu(raw_mid).astype(jnp.bfloat16)
    predicted = jnp.dot(hidden_mid, w_out, preferred_element_type=jnp.float32) + b_out[0]
    slope = (predicted - target) * inv_sets
    grad_out = jnp.sum(own(hidden_mid, 1).astype(jnp.float32) * slope[:, None], axis=0)
    grad_bout = jnp.broadcast_to(jnp.sum(slope), (cols,))
    delta_mid = (slope[:, None] * w_out.astype(jnp.float32)[None, :] * silu_slope(raw_mid)).astype(
        jnp.bfloat16
    )
    own_mid = own(delta_mid, 1)
    grad_bmid = jnp.sum(own_mid.astype(jnp.float32), axis=0)
    backward = lax.dot_general(
        delta_mid, own(w_mid, 0), (((1,), (1,)), ((), ())), preferred_element_type=jnp.float32
    )
    delta_in = (backward * silu_slope(own(raw_in, 1))).astype(jnp.bfloat16)
    grad_in = contract_rows(inputs, delta_in)
    grad_bin = jnp.sum(delta_in.astype(jnp.float32), axis=0)
    small = jnp.concatenate(
        [grad_in, grad_bin[None], grad_bmid[None], grad_out[None], grad_bout[None]], axis=0
    )
    return contract_rows(hidden_in, own_mid), small


def swap(array, bit, devices):
    return lax.ppermute(array, "paths", [(i, i ^ bit) for i in range(devices)])


def pick(array, index):
    return lax.dynamic_index_in_dim(array, index, 0, keepdims=False)


def on_device(params, increments, w_in, b_in, w_mid, b_mid, w_out, b_out):
    devices = lax.axis_size("paths")
    top = devices // 2
    groups = devices // 4
    total_paths = increments.shape[2] * devices
    set_count = params.shape[0]
    set_dev = set_count // devices
    owner = lax.axis_index("paths")
    core = owner % 2
    high = owner // top
    group = (owner // 2) % groups

    sums = payoff_sums(params, increments).reshape(devices, set_dev, PAIRS)
    parts = lax.all_to_all(sums, "paths", 0, 0, tiled=True)
    prices = jnp.sum(parts, axis=0) / total_paths
    other = swap(prices, 1, devices)
    pair = jnp.stack([jnp.where(core == 0, prices, other), jnp.where(core == 0, other, prices)])
    far = swap(pair, top, devices)
    quad = jnp.stack([jnp.where(high == 0, pair, far), jnp.where(high == 0, far, pair)])

    rows = pick(params.reshape(2, groups, 2 * set_dev, 4).swapaxes(0, 1), group).reshape(-1, 4)
    cols = WIDTH // 4
    block = 2 * high + core
    big, small = block_gradients(
        features(rows), quad.reshape(-1), w_in, b_in, w_mid, b_mid, w_out, b_out,
        1.0 / set_count, block, cols,
    )
    piece_rows = WIDTH // groups
    big = big.reshape(groups, piece_rows, 2, LANES).swapaxes(1, 2)
    small = small.reshape(2 * SMALL_ROWS, LANES)
    small = jnp.pad(small, ((0, 8 * groups - 2 * SMALL_ROWS), (0, 0))).reshape(groups, 8, LANES)
    held = jnp.concatenate([big.reshape(groups, 2 * piece_rows, LANES), small], axis=1)

    bit = groups // 2
    while bit:
        mine = (group // bit) % 2
        halves = held.reshape((2, held.shape[0] // 2) + held.shape[1:])
        held = pick(halves, mine) + swap(pick(halves, 1 - mine), 2 * bit, devices)
        bit //= 2

    gathered = held.reshape((1,) + held.shape[1:])
    bit = top
    while bit:
        came = swap(gathered, bit, devices)
        first = (owner // bit) % 2 == 0
        pair = jnp.stack([jnp.where(first, gathered, came), jnp.where(first, came, gathered)])
        if bit == top:
            gathered = pair.reshape((-1,) + pair.shape[2:])
        else:
            gathered = jnp.swapaxes(pair, 0, 1).reshape((-1,) + pair.shape[2:])
        bit //= 2
    whole = gathered.reshape(2, groups, 2, 2 * piece_rows + 8, LANES)
    big = whole[:, :, :, : 2 * piece_rows].reshape(2, groups, 2, 2, piece_rows, LANES)
    grad_mid = big.transpose(1, 4, 0, 2, 3, 5).reshape(WIDTH, WIDTH)
    small = whole[:, :, :, 2 * piece_rows :].transpose(1, 3, 0, 2, 4)
    small = small.reshape(groups * 8, 2, 2, LANES)[: 2 * SMALL_ROWS]
    small = small.reshape(SMALL_ROWS, 2, 2, 2, LANES).transpose(0, 2, 3, 1, 4)
    small = small.reshape(SMALL_ROWS, WIDTH)

    def directions(grad_w, grad_b):
        entries = grad_w.size + grad_b.size
        mean_square = (jnp.sum(grad_w * grad_w) + jnp.sum(grad_b * grad_b)) / entries
        factor = lax.rsqrt(mean_square + EPSILON)
        return (grad_w * factor, grad_b * factor)

    direction_w_mid, direction_b_mid = directions(grad_mid, small[7])
    direction_w_in, direction_b_in = directions(small[:6], small[6])
    direction_w_out, direction_b_out = directions(small[8], small[9, :1])
    return (
        prices.reshape(set_dev, PAIRS),
        direction_w_in,
        direction_b_in,
        direction_w_mid,
        direction_b_mid,
        direction_w_out,
        direction_b_out,
    )


def solution(mesh):
    in_specs = (P(), P(None, None, "paths"), P(), P(), P(), P(), P(), P())
    out_specs = (P("paths", None), P(), P(), P(), P(), P(), P())
    return jax.shard_map(
        on_device, mesh=mesh, in_specs=in_specs, out_specs=out_specs, check_vma=False
    )
```

```python
import functools
import math

import jax
import jax.numpy as jnp
import numpy as np
from jax import lax
from jax.experimental import pallas as pl
from jax.experimental.pallas import tpu as pltpu
from jax.sharding import PartitionSpec as P

STEPS = 64
MATS = 8
STRIKES = 11
PAIRS = 88
WIDTH = 1024
LANES = 128
FEATURE_ROWS = 16
ROW_TILE = 256
EPSILON = 1e-06


TENORS = (np.arange(MATS, dtype=np.float32) + np.float32(1.0)) / np.float32(MATS)
OFFSETS = np.arange(STRIKES, dtype=np.float32) - np.float32((STRIKES - 1) / 2.0)
LOG_STRIKE = np.float32(0.05) * OFFSETS[None, :] * np.sqrt(TENORS)[:, None]
STRIKE = np.exp(LOG_STRIKE).astype(np.float32)
SET_BLOCK = 256
LOG2E = 1.4426950408889634


def bf16_pieces(value):
    high = value.astype(jnp.bfloat16)
    rest = value - high.astype(jnp.float32)
    mid = rest.astype(jnp.bfloat16)
    low = (rest - mid.astype(jnp.float32)).astype(jnp.bfloat16)
    return high, mid, low


def pricing_kernel(strike_ref, params_ref, inc_ref, out_ref, lags_ref, noise_ref, comp_ref, pay_ref):
    sets = params_ref.shape[1]
    paths = inc_ref.shape[2]
    hurst = params_ref[0:1, :]
    vol_of_vol = params_ref[1:2, :]
    correl = params_ref[2:3, :]
    forward_var = params_ref[3:4, :]
    delta_t = 1.0 / STEPS

    lag = (LANES - lax.broadcasted_iota(jnp.int32, (LANES, 1), 0)).astype(jnp.float32)
    exponent = hurst + 0.5
    here = jnp.exp2(exponent * jnp.log2(lag))
    before = jnp.exp2(exponent * jnp.log2(jnp.maximum(lag - 1.0, 1.0)))
    before = jnp.where(lag > 1.5, before, 0.0)
    front = jnp.sqrt(2.0 * hurst) * jnp.exp2(hurst * math.log2(delta_t)) / exponent
    weights = jnp.where(lag < STEPS - 0.5, (here - before) * front, 0.0).astype(jnp.bfloat16)

    half_scale = vol_of_vol * (0.5 * LOG2E)
    step = lax.broadcasted_iota(jnp.int32, (STEPS, 1), 0).astype(jnp.float32)
    powers = jnp.exp2(2.0 * hurst * jnp.log2(jnp.maximum(step, 1.0) * delta_t))
    comp_ref[...] = jnp.where(step > 0.5, powers * (0.25 * LOG2E * vol_of_vol * vol_of_vol), 0.0)

    root = jnp.sqrt(forward_var * delta_t)
    back = 2.0 / root
    growth = (0.5 * LOG2E) * forward_var * delta_t
    noise_weights = jnp.concatenate(
        [
            jnp.broadcast_to(piece.astype(jnp.float32), (8, sets))
            for value in (correl * back, jnp.sqrt(1.0 - correl * correl) * back)
            for piece in bf16_pieces(value)
        ]
        + [jnp.zeros((LANES - 48, sets), jnp.float32)],
        axis=0,
    ).astype(jnp.bfloat16)

    first = inc_ref[0].astype(jnp.float32)
    second = inc_ref[1].astype(jnp.float32)
    lags_ref[...] = jnp.concatenate([first, jnp.zeros((LANES - STEPS, paths), jnp.float32)], 0).T
    for m in range(MATS):
        rows = slice(8 * m, 8 * m + 8)
        block = jnp.concatenate(
            [first[rows]] * 3 + [second[rows]] * 3 + [jnp.zeros((LANES - 48, paths), jnp.float32)], 0
        )
        noise_ref[m] = block.T.astype(jnp.bfloat16)
    lane = lax.broadcasted_iota(jnp.int32, (paths, LANES), 1)

    def maturity(m, total):
        noise = noise_ref[m]
        for k in range(8):
            i = 8 * m + k
            window = lags_ref[...] if k == 0 else pltpu.roll(lags_ref[...], LANES - k, 1)
            drive = jnp.dot(
                window.astype(jnp.bfloat16), weights, preferred_element_type=jnp.float32
            )
            picked = jnp.where(lane % 8 == k, noise.astype(jnp.float32), 0.0).astype(jnp.bfloat16)
            shock = jnp.dot(picked, noise_weights, preferred_element_type=jnp.float32)
            root_variance = jnp.exp2(drive * half_scale - comp_ref[pl.ds(i, 1), :])
            total = total + root_variance * (shock - root_variance)
        lags_ref[...] = pltpu.roll(lags_ref[...], LANES - 8, 1)
        spot = jnp.exp2(total * growth)
        for j in range(STRIKES):
            strike = strike_ref[m, j]
            gains = jnp.maximum(spot, strike).reshape(paths // 8, 8, sets).sum(axis=0)
            gains = gains - strike * (paths // 8)
            pay_ref[pl.ds(m * STRIKES + j, 1), :] = jnp.sum(gains, axis=0, keepdims=True)
        return total

    lax.fori_loop(0, MATS, maturity, jnp.zeros((paths, sets), jnp.float32))
    out_ref[...] = pay_ref[...].T[:, :PAIRS]


def payoff_sums(params, increments):
    count = params.shape[1]
    paths = increments.shape[2]
    sets = math.gcd(count, SET_BLOCK)
    return pl.pallas_call(
        pricing_kernel,
        grid=(count // sets,),
        in_specs=[
            pl.BlockSpec(memory_space=pltpu.SMEM),
            pl.BlockSpec((4, sets), lambda b: (0, b)),
            pl.BlockSpec((2, STEPS, paths), lambda b: (0, 0, 0)),
        ],
        out_specs=pl.BlockSpec((sets, PAIRS), lambda b: (b, 0)),
        out_shape=jax.ShapeDtypeStruct((count, PAIRS), jnp.float32),
        scratch_shapes=[
            pltpu.VMEM((paths, LANES), jnp.float32),
            pltpu.VMEM((MATS, paths, LANES), jnp.bfloat16),
            pltpu.VMEM((STEPS, sets), jnp.float32),
            pltpu.VMEM((LANES, sets), jnp.float32),
        ],
        compiler_params=pltpu.CompilerParams(vmem_limit_bytes=32 * 1024 * 1024),
        name="pricing",
    )(jnp.asarray(STRIKE), params, increments)


def row_maps(sets):
    row = np.arange(sets * PAIRS, dtype=np.int32)
    return np.stack([row % PAIRS, PAIRS + row // PAIRS])


def feature_base(sets):
    base = np.zeros((FEATURE_ROWS, LANES), np.float32)
    base[4, :PAIRS] = (np.float32(4.0) * LOG_STRIKE).reshape(PAIRS)
    base[5, :PAIRS] = np.repeat(TENORS, STRIKES)
    base[6:9, PAIRS : PAIRS + sets] = 1.0
    return base


def dot(left, right):
    return jnp.dot(left, right, preferred_element_type=jnp.float32)


def dot_rows(left, right):
    return lax.dot_general(
        left, right, (((1,), (1,)), ((), ())), preferred_element_type=jnp.float32
    )


def network_kernel(
    inv_sets, place_ref, maps_ref, feat_ref, sums_ref, w_in_ref, b_in_ref, w_mid_ref, b_mid_ref,
    w_out_ref, b_out_ref, out_ref, left_ref, win_ref, turned_ref, bias_ref, read_ref, grad_ref,
    small_ref, slope_ref, hidden_ref,
):
    block = place_ref[0]
    sets = sums_ref.shape[0]
    rows = maps_ref.shape[1]
    cols = WIDTH // 4
    own = pl.ds(pl.multiple_of(block * cols, cols), cols)
    groups = out_ref.shape[0]
    piece_rows = WIDTH // groups
    bf16 = jnp.bfloat16

    left_ref[...] = jnp.zeros_like(left_ref)
    left_ref[0:FEATURE_ROWS, :] = feat_ref[...]
    for p, piece in enumerate(bf16_pieces(sums_ref[...])):
        first = FEATURE_ROWS + p * sets
        left_ref[first : first + sets, :PAIRS] = piece.astype(jnp.float32)
    left = left_ref[...].astype(bf16)

    weights_in = w_in_ref[...].astype(jnp.float32)
    bias_in = [piece.astype(jnp.float32) for piece in bf16_pieces(b_in_ref[...])]
    pad = jnp.zeros((FEATURE_ROWS - weights_in.shape[0] - 3, WIDTH), jnp.float32)
    win_ref[...] = (0.5 * jnp.concatenate([weights_in] + bias_in + [pad], 0)).T.astype(bf16)
    turned_ref[...] = (0.5 * w_mid_ref[...].astype(jnp.float32)).T.astype(bf16)
    bias_ref[...] = jnp.broadcast_to((0.5 * b_mid_ref[...]).T, bias_ref.shape)
    read_ref[...] = jnp.broadcast_to((0.5 * w_out_ref[...].astype(jnp.float32)).T, read_ref.shape)
    grad_ref[...] = jnp.zeros_like(grad_ref)
    small_ref[...] = jnp.zeros_like(small_ref)
    slope_ref[...] = jnp.zeros_like(slope_ref)
    readout = jnp.broadcast_to(w_out_ref[...].astype(jnp.float32), (16, WIDTH)).astype(bf16)

    def tile(t, carry):
        here = pl.ds(pl.multiple_of(t * ROW_TILE, ROW_TILE), ROW_TILE)
        pair, group_set = maps_ref[0:1, here], maps_ref[1:2, here]
        code = lax.broadcasted_iota(jnp.int32, (LANES, ROW_TILE), 0)
        hot = jnp.where((code == pair) | (code == group_set), 1.0, 0.0).astype(bf16)
        looked = dot(left, hot)
        feat = looked[:FEATURE_ROWS].astype(bf16)
        target = looked[FEATURE_ROWS : FEATURE_ROWS + sets]
        for p in (1, 2):
            first = FEATURE_ROWS + p * sets
            target = target + looked[first : first + sets]
        member = lax.broadcasted_iota(jnp.int32, (sets, ROW_TILE), 0) + PAIRS
        target = jnp.sum(jnp.where(member == group_set, target, 0.0), axis=0, keepdims=True)

        half_in = dot(win_ref[...], feat)
        hidden_in = (half_in + half_in * jnp.tanh(half_in)).astype(bf16)
        half_mid = dot(turned_ref[...], hidden_in) + bias_ref[...]
        wave = jnp.tanh(half_mid)
        rise = 1.0 + wave
        hidden_mid = (half_mid * rise).astype(bf16)
        hidden_ref[...] = hidden_mid
        predicted = dot(readout, hidden_mid)[0:1] + b_out_ref[0]
        slope = (predicted - target) * inv_sets
        slope_ref[...] += slope
        curve = read_ref[...] * (rise * (1.0 + half_mid * (1.0 - wave)))
        delta_mid = (slope * curve).astype(bf16)
        backward = dot(w_mid_ref[own, :], delta_mid)
        own_half = dot(win_ref[own, :], feat)
        own_wave = jnp.tanh(own_half)
        own_curve = (0.5 * (1.0 + own_wave)) * (1.0 + own_half * (1.0 - own_wave))
        delta_in = (backward * own_curve).astype(bf16)
        own_curve_mid = slope * own_rows(curve, block, cols)
        own_delta = own_curve_mid.astype(bf16)
        grad_ref[...] += dot_rows(hidden_in, own_delta)
        pieces = [piece.astype(jnp.float32) for piece in bf16_pieces(slope)]
        lines = jnp.concatenate(
            [feat.astype(jnp.float32)] + pieces + [jnp.zeros((13, ROW_TILE), jnp.float32)], 0
        ).astype(bf16)
        small_ref[:, 0:cols] += dot_rows(lines, delta_in)
        small_ref[:, cols : 2 * cols] += dot_rows(lines, own_delta)
        small_ref[:, 2 * cols :] += dot_rows(lines, hidden_ref[own, :])
        return carry

    lax.fori_loop(0, rows // ROW_TILE, tile, 0)

    extra = [small_ref[0:7, 0:cols], small_ref[6:7, cols : 2 * cols]]
    extra.append(jnp.sum(small_ref[16:19, 2 * cols :], axis=0, keepdims=True))
    total = jnp.sum(slope_ref[...], axis=1, keepdims=True)
    extra.append(jnp.broadcast_to(total, (1, cols)))
    extra.append(jnp.zeros((6, cols), jnp.float32))
    extra = jnp.concatenate(extra, 0)
    for j in range(groups):
        for h in range(2):
            lanes = slice(h * LANES, (h + 1) * LANES)
            out_ref[j, h * piece_rows : (h + 1) * piece_rows, :] = grad_ref[
                j * piece_rows : (j + 1) * piece_rows, lanes
            ]
        if j < 4:
            lanes = slice((j % 2) * LANES, (j % 2 + 1) * LANES)
            out_ref[j, 2 * piece_rows :, :] = extra[8 * (j // 2) : 8 * (j // 2) + 8, lanes]
        else:
            out_ref[j, 2 * piece_rows :, :] = jnp.zeros((8, LANES), jnp.float32)


def own_rows(value, block, cols):
    part = value[0:cols]
    for b in range(1, 4):
        part = jnp.where(block == b, value[b * cols : (b + 1) * cols], part)
    return part


def block_gradients(rows, sums, w_in, b_in, w_mid, b_mid, w_out, b_out, inv_sets, block, groups):
    sets = rows.shape[1]
    cols = WIDTH // 4
    scale = jnp.array([[4.0], [1.0], [1.0], [20.0]], jnp.float32)
    feat = jnp.pad(rows * scale, ((0, FEATURE_ROWS - 4), (PAIRS, LANES - PAIRS - sets)))
    vmem = pl.BlockSpec(memory_space=pltpu.VMEM)
    smem = pl.BlockSpec(memory_space=pltpu.SMEM)
    return pl.pallas_call(
        functools.partial(network_kernel, inv_sets),
        in_specs=[smem] + [vmem] * 8 + [smem],
        out_specs=vmem,
        out_shape=jax.ShapeDtypeStruct((groups, 2 * (WIDTH // groups) + 8, LANES), jnp.float32),
        scratch_shapes=[
            pltpu.VMEM((FEATURE_ROWS + 3 * sets, LANES), jnp.float32),
            pltpu.VMEM((WIDTH, FEATURE_ROWS), jnp.bfloat16),
            pltpu.VMEM((WIDTH, WIDTH), jnp.bfloat16),
            pltpu.VMEM((WIDTH, ROW_TILE), jnp.float32),
            pltpu.VMEM((WIDTH, ROW_TILE), jnp.float32),
            pltpu.VMEM((WIDTH, cols), jnp.float32),
            pltpu.VMEM((32, 3 * cols), jnp.float32),
            pltpu.VMEM((1, ROW_TILE), jnp.float32),
            pltpu.VMEM((WIDTH, ROW_TILE), jnp.bfloat16),
        ],
        compiler_params=pltpu.CompilerParams(vmem_limit_bytes=48 * 1024 * 1024),
        name="network",
    )(
        block.reshape(1), jnp.asarray(row_maps(sets)), feat + feature_base(sets), sums, w_in,
        b_in.reshape(1, -1), w_mid, b_mid.reshape(1, -1), w_out.reshape(1, -1), b_out,
    )


def scaling_kernel(
    pieces_ref, w_in_ref, b_in_ref, w_mid_ref, b_mid_ref, w_out_ref, b_out_ref, small_ref
):
    groups = pieces_ref.shape[1]
    piece_rows = WIDTH // groups
    for high in range(2):
        for core in range(2):
            for j in range(4):
                start = (2 * high + core) * (WIDTH // 4) + (j % 2) * LANES
                small_ref[8 * (j // 2) : 8 * (j // 2) + 8, start : start + LANES] = pieces_ref[
                    high, j, core, 2 * piece_rows :, :
                ]
    small = small_ref[...]
    squares = jnp.sum(small * small, axis=1, keepdims=True)
    bias_out = small_ref[9:10, 0:1]
    last = bias_out * bias_out

    def factor(total, entries):
        return lax.rsqrt(total / entries + EPSILON)

    def add(j, total):
        for high in range(2):
            for core in range(2):
                part = pieces_ref[high, j, core, 0 : 2 * piece_rows, :]
                total = total + jnp.sum((part * part).reshape(-1, 8, LANES), axis=0)
        return total

    total = lax.fori_loop(0, groups, add, jnp.zeros((8, LANES), jnp.float32))
    total = jnp.sum(jnp.sum(total, axis=1, keepdims=True), axis=0, keepdims=True)
    scale_mid = factor(total + squares[7:8], WIDTH * WIDTH + WIDTH)
    scale_in = factor(jnp.sum(squares[0:7], axis=0, keepdims=True), 7 * WIDTH)
    scale_out = factor(squares[8:9] + last, WIDTH + 1)
    w_in_ref[...] = small[0:6] * scale_in
    b_in_ref[...] = small[6:7] * scale_in
    b_mid_ref[...] = small[7:8] * scale_mid
    w_out_ref[...] = small[8:9] * scale_out
    b_out_ref[...] = bias_out * scale_out

    def place(j, carry):
        rows = pl.ds(pl.multiple_of(j * piece_rows, 8), piece_rows)
        for high in range(2):
            for core in range(2):
                for h in range(2):
                    start = (2 * high + core) * (WIDTH // 4) + h * LANES
                    part = pieces_ref[high, j, core, h * piece_rows : (h + 1) * piece_rows, :]
                    w_mid_ref[rows, start : start + LANES] = part * scale_mid
        return carry

    lax.fori_loop(0, groups, place, 0)


def scaled(pieces):
    vmem = pl.BlockSpec(memory_space=pltpu.VMEM)
    shapes = [(6, WIDTH), (1, WIDTH), (WIDTH, WIDTH), (1, WIDTH), (1, WIDTH), (1, 1)]
    return pl.pallas_call(
        scaling_kernel,
        in_specs=[vmem],
        out_specs=[vmem] * 6,
        out_shape=[jax.ShapeDtypeStruct(shape, jnp.float32) for shape in shapes],
        scratch_shapes=[pltpu.VMEM((16, WIDTH), jnp.float32)],
        compiler_params=pltpu.CompilerParams(vmem_limit_bytes=32 * 1024 * 1024),
        name="scaling",
    )(pieces)


def swap(array, bit, devices):
    return lax.ppermute(array, "paths", [(i, i ^ bit) for i in range(devices)])


def pick(array, index):
    return lax.dynamic_index_in_dim(array, index, 0, keepdims=False)


def on_device(params, increments, w_in, b_in, w_mid, b_mid, w_out, b_out):
    devices = lax.axis_size("paths")
    top = devices // 2
    groups = devices // 4
    total_paths = increments.shape[2] * devices
    set_count = params.shape[0]
    set_dev = set_count // devices
    owner = lax.axis_index("paths")
    core = owner % 2
    high = owner // top
    group = (owner // 2) % groups
    block = 2 * high + core
    turned = params.T

    sums = payoff_sums(turned, increments)
    sums = sums + swap(sums, 1, devices)
    sums = sums.reshape(2, groups, 2 * set_dev, PAIRS).swapaxes(0, 1)
    sums = jnp.broadcast_to(sums[None], (2,) + sums.shape).reshape(top, 4 * set_dev, PAIRS)
    lanes = [[2 * chip + c for chip in range(top)] for c in range(2)]
    parts = lax.all_to_all(sums, "paths", 0, 0, axis_index_groups=lanes, tiled=True)
    sums = jnp.sum(parts, axis=0) / total_paths
    prices = pick(sums.reshape(4, set_dev, PAIRS), block)

    rows = pick(turned.reshape(4, 2, groups, 2 * set_dev).transpose(2, 0, 1, 3), group)
    held = block_gradients(
        rows.reshape(4, 4 * set_dev), sums, w_in, b_in, w_mid, b_mid, w_out, b_out,
        1.0 / set_count, block, groups,
    )

    bit = groups // 2
    while bit:
        mine = (group // bit) % 2
        halves = held.reshape((2, held.shape[0] // 2) + held.shape[1:])
        held = pick(halves, mine) + swap(pick(halves, 1 - mine), 2 * bit, devices)
        bit //= 2

    gathered = held.reshape((1,) + held.shape[1:])
    bit = top
    while bit:
        came = swap(gathered, bit, devices)
        first = (owner // bit) % 2 == 0
        pair = jnp.stack([jnp.where(first, gathered, came), jnp.where(first, came, gathered)])
        if bit == top:
            gathered = pair.reshape((-1,) + pair.shape[2:])
        else:
            gathered = jnp.swapaxes(pair, 0, 1).reshape((-1,) + pair.shape[2:])
        bit //= 2
    result = scaled(gathered.reshape((2, groups, 2) + gathered.shape[1:]))
    direction_w_in, direction_b_in, direction_w_mid, direction_b_mid, direction_w_out, direction_b_out = result
    return (
        prices,
        direction_w_in,
        direction_b_in.reshape(WIDTH),
        direction_w_mid,
        direction_b_mid.reshape(WIDTH),
        direction_w_out.reshape(WIDTH),
        direction_b_out.reshape(1),
    )


def solution(mesh):
    in_specs = (P(), P(None, None, "paths"), P(), P(), P(), P(), P(), P())
    out_specs = (P("paths", None), P(), P(), P(), P(), P(), P())
    return jax.shard_map(
        on_device, mesh=mesh, in_specs=in_specs, out_specs=out_specs, check_vma=False
    )
```

```python
import functools
import math

import jax
import jax.numpy as jnp
import numpy as np
from jax import lax
from jax.experimental import pallas as pl
from jax.experimental.pallas import tpu as pltpu
from jax.sharding import PartitionSpec as P

STEPS = 64
MATS = 8
STRIKES = 11
PAIRS = 88
WIDTH = 1024
LANES = 128
FEATURE_ROWS = 16
ROW_TILE = 256
CHUNK = 256
CHUNKS = [slice(start, start + CHUNK) for start in range(0, WIDTH, CHUNK)]
EPSILON = 1e-06


TENORS = (np.arange(MATS, dtype=np.float32) + np.float32(1.0)) / np.float32(MATS)
OFFSETS = np.arange(STRIKES, dtype=np.float32) - np.float32((STRIKES - 1) / 2.0)
LOG_STRIKE = np.float32(0.05) * OFFSETS[None, :] * np.sqrt(TENORS)[:, None]
STRIKE = np.exp(LOG_STRIKE).astype(np.float32)
SET_BLOCK = 256
LOG2E = 1.4426950408889634


def bf16_pieces(value):
    high = value.astype(jnp.bfloat16)
    rest = value - high.astype(jnp.float32)
    mid = rest.astype(jnp.bfloat16)
    low = (rest - mid.astype(jnp.float32)).astype(jnp.bfloat16)
    return high, mid, low


def pricing_kernel(strike_ref, params_ref, inc_ref, out_ref, lags_ref, noise_ref, comp_ref, pay_ref):
    sets = params_ref.shape[1]
    paths = inc_ref.shape[2]
    hurst = params_ref[0:1, :]
    vol_of_vol = params_ref[1:2, :]
    correl = params_ref[2:3, :]
    forward_var = params_ref[3:4, :]
    delta_t = 1.0 / STEPS

    lag = (LANES - lax.broadcasted_iota(jnp.int32, (LANES, 1), 0)).astype(jnp.float32)
    exponent = hurst + 0.5
    here = jnp.exp2(exponent * jnp.log2(lag))
    before = jnp.exp2(exponent * jnp.log2(jnp.maximum(lag - 1.0, 1.0)))
    before = jnp.where(lag > 1.5, before, 0.0)
    front = jnp.sqrt(2.0 * hurst) * jnp.exp2(hurst * math.log2(delta_t)) / exponent
    weights = jnp.where(lag < STEPS - 0.5, (here - before) * front, 0.0).astype(jnp.bfloat16)

    half_scale = vol_of_vol * (0.5 * LOG2E)
    step = lax.broadcasted_iota(jnp.int32, (STEPS, 1), 0).astype(jnp.float32)
    powers = jnp.exp2(2.0 * hurst * jnp.log2(jnp.maximum(step, 1.0) * delta_t))
    comp_ref[...] = jnp.where(step > 0.5, powers * (0.25 * LOG2E * vol_of_vol * vol_of_vol), 0.0)

    root = jnp.sqrt(forward_var * delta_t)
    back = 2.0 / root
    growth = (0.5 * LOG2E) * forward_var * delta_t
    noise_weights = jnp.concatenate(
        [
            jnp.broadcast_to(piece.astype(jnp.float32), (8, sets))
            for value in (correl * back, jnp.sqrt(1.0 - correl * correl) * back)
            for piece in bf16_pieces(value)
        ]
        + [jnp.zeros((LANES - 48, sets), jnp.float32)],
        axis=0,
    ).astype(jnp.bfloat16)

    first = inc_ref[0].astype(jnp.float32)
    second = inc_ref[1].astype(jnp.float32)
    lags_ref[...] = jnp.concatenate([first, jnp.zeros((LANES - STEPS, paths), jnp.float32)], 0).T
    for m in range(MATS):
        rows = slice(8 * m, 8 * m + 8)
        block = jnp.concatenate(
            [first[rows]] * 3 + [second[rows]] * 3 + [jnp.zeros((LANES - 48, paths), jnp.float32)], 0
        )
        noise_ref[m] = block.T.astype(jnp.bfloat16)
    lane = lax.broadcasted_iota(jnp.int32, (paths, LANES), 1)

    def maturity(m, total):
        noise = noise_ref[m]
        for k in range(8):
            i = 8 * m + k
            window = lags_ref[...] if k == 0 else pltpu.roll(lags_ref[...], LANES - k, 1)
            drive = jnp.dot(
                window.astype(jnp.bfloat16), weights, preferred_element_type=jnp.float32
            )
            picked = jnp.where(lane % 8 == k, noise.astype(jnp.float32), 0.0).astype(jnp.bfloat16)
            shock = jnp.dot(picked, noise_weights, preferred_element_type=jnp.float32)
            root_variance = jnp.exp2(drive * half_scale - comp_ref[pl.ds(i, 1), :])
            total = total + root_variance * (shock - root_variance)
        lags_ref[...] = pltpu.roll(lags_ref[...], LANES - 8, 1)
        spot = jnp.exp2(total * growth)
        for j in range(STRIKES):
            strike = strike_ref[m, j]
            gains = jnp.maximum(spot, strike).reshape(paths // 8, 8, sets).sum(axis=0)
            gains = gains - strike * (paths // 8)
            pay_ref[pl.ds(m * STRIKES + j, 1), :] = jnp.sum(gains, axis=0, keepdims=True)
        return total

    lax.fori_loop(0, MATS, maturity, jnp.zeros((paths, sets), jnp.float32))
    out_ref[...] = pay_ref[...].T[:, :PAIRS]


def payoff_sums(params, increments):
    count = params.shape[1]
    paths = increments.shape[2]
    sets = math.gcd(count, SET_BLOCK)
    return pl.pallas_call(
        pricing_kernel,
        grid=(count // sets,),
        in_specs=[
            pl.BlockSpec(memory_space=pltpu.SMEM),
            pl.BlockSpec((4, sets), lambda b: (0, b)),
            pl.BlockSpec((2, STEPS, paths), lambda b: (0, 0, 0)),
        ],
        out_specs=pl.BlockSpec((sets, PAIRS), lambda b: (b, 0)),
        out_shape=jax.ShapeDtypeStruct((count, PAIRS), jnp.float32),
        scratch_shapes=[
            pltpu.VMEM((paths, LANES), jnp.float32),
            pltpu.VMEM((MATS, paths, LANES), jnp.bfloat16),
            pltpu.VMEM((STEPS, sets), jnp.float32),
            pltpu.VMEM((LANES, sets), jnp.float32),
        ],
        compiler_params=pltpu.CompilerParams(vmem_limit_bytes=32 * 1024 * 1024),
        name="pricing",
    )(jnp.asarray(STRIKE), params, increments)


def row_maps(sets):
    row = np.arange(sets * PAIRS, dtype=np.int32)
    return np.stack([row % PAIRS, PAIRS + row // PAIRS])


def feature_base(sets):
    base = np.zeros((FEATURE_ROWS, LANES), np.float32)
    base[4, :PAIRS] = (np.float32(4.0) * LOG_STRIKE).reshape(PAIRS)
    base[5, :PAIRS] = np.repeat(TENORS, STRIKES)
    base[6:9, PAIRS : PAIRS + sets] = 1.0
    return base


def dot(left, right):
    return jnp.dot(left, right, preferred_element_type=jnp.float32)


def dot_rows(left, right):
    return lax.dot_general(
        left, right, (((1,), (1,)), ((), ())), preferred_element_type=jnp.float32
    )


def network_kernel(
    inv_sets, place_ref, maps_ref, feat_ref, sums_ref, w_in_ref, b_in_ref, w_mid_ref, b_mid_ref,
    w_out_ref, b_out_ref, keep_a, send_a, keep_b, send_b, left_ref, win_ref, turned_ref, bias_ref, read_ref, grad_ref,
    small_ref, slope_ref, delta_ref, extra_ref, even_hidden, odd_hidden, even_feat, odd_feat, even_gap,
    odd_gap, even_mixed, odd_mixed, even_curve, odd_curve,
):
    block = place_ref[0]
    sets = sums_ref.shape[0]
    tiles = maps_ref.shape[1] // ROW_TILE
    cols = WIDTH // 4
    own = pl.ds(pl.multiple_of(block * cols, cols), cols)
    groups = 2 * keep_a.shape[0]
    piece_rows = WIDTH // groups
    bf16 = jnp.bfloat16
    even = (even_hidden, even_feat, even_gap, even_mixed, even_curve)
    odd = (odd_hidden, odd_feat, odd_gap, odd_mixed, odd_curve)

    left_ref[...] = jnp.zeros_like(left_ref)
    left_ref[0:FEATURE_ROWS, :] = feat_ref[...]
    for p, piece in enumerate(bf16_pieces(sums_ref[...])):
        first = FEATURE_ROWS + p * sets
        left_ref[first : first + sets, :PAIRS] = piece.astype(jnp.float32)
    left = left_ref[...].astype(bf16)

    weights_in = w_in_ref[...].astype(jnp.float32)
    bias_in = [piece.astype(jnp.float32) for piece in bf16_pieces(b_in_ref[...])]
    pad = jnp.zeros((FEATURE_ROWS - weights_in.shape[0] - 3, WIDTH), jnp.float32)
    win_ref[...] = (0.5 * jnp.concatenate([weights_in] + bias_in + [pad], 0)).T.astype(bf16)
    turned_ref[...] = (0.5 * w_mid_ref[...].astype(jnp.float32)).T.astype(bf16)
    bias_ref[...] = jnp.broadcast_to((0.5 * b_mid_ref[...]).T, bias_ref.shape)
    read_ref[...] = jnp.broadcast_to((0.5 * w_out_ref[...].astype(jnp.float32)).T, read_ref.shape)
    grad_ref[...] = jnp.zeros_like(grad_ref)
    small_ref[...] = jnp.zeros_like(small_ref)
    slope_ref[...] = jnp.zeros_like(slope_ref)
    readout = jnp.broadcast_to(w_out_ref[...].astype(jnp.float32), (16, WIDTH)).astype(bf16)

    def tile(t, last, coming):
        if coming is not None:
            hidden, feat_tile, gap_ref, mixed, curve = coming
            here = pl.ds(pl.multiple_of(t * ROW_TILE, ROW_TILE), ROW_TILE)
            pair, group_set = maps_ref[0:1, here], maps_ref[1:2, here]
            code = lax.broadcasted_iota(jnp.int32, (LANES, ROW_TILE), 0)
            hot = jnp.where((code == pair) | (code == group_set), 1.0, 0.0).astype(bf16)
            looked = dot(left, hot)
            feat = looked[:FEATURE_ROWS].astype(bf16)
            feat_tile[...] = feat
            target = looked[FEATURE_ROWS : FEATURE_ROWS + sets]
            for p in (1, 2):
                first = FEATURE_ROWS + p * sets
                target = target + looked[first : first + sets]
            member = lax.broadcasted_iota(jnp.int32, (sets, ROW_TILE), 0) + PAIRS
            target = jnp.sum(jnp.where(member == group_set, target, 0.0), axis=0, keepdims=True)
        if last is not None:
            old_hidden, old_feat, old_gap, old_mixed, old_curve = last
            slope = old_gap[...] * inv_sets
            slope_ref[...] += slope
            pieces = [piece.astype(jnp.float32) for piece in bf16_pieces(slope)]
            lines = jnp.concatenate(
                [old_feat[...].astype(jnp.float32)]
                + pieces
                + [jnp.zeros((13, ROW_TILE), jnp.float32)],
                0,
            ).astype(bf16)
            for c in CHUNKS:
                delta_ref[c, :] = (slope * old_curve[c, :]).astype(bf16)
            own_half = dot(win_ref[own, :], old_feat[...])
            own_delta = delta_ref[own, :]
        if coming is not None:
            for c in CHUNKS:
                half_in = dot(win_ref[c, :], feat)
                hidden[c, :] = (half_in + half_in * jnp.tanh(half_in)).astype(bf16)
        if last is not None:
            backward = dot(w_mid_ref[own, :], delta_ref[...])
            own_wave = jnp.tanh(own_half)
            own_curve = (0.5 * (1.0 + own_wave)) * (1.0 + own_half * (1.0 - own_wave))
        for c in CHUNKS:
            if coming is not None:
                half_mid = dot(turned_ref[c, :], hidden[...]) + bias_ref[c, :]
            if last is not None:
                grad_ref[c, :] += dot_rows(old_hidden[c, :], own_delta)
            if coming is not None:
                wave = jnp.tanh(half_mid)
                turn = half_mid * wave
                mixed[c, :] = (half_mid + turn).astype(bf16)
                curve[c, :] = (1.0 + wave) * (1.0 + half_mid - turn) * read_ref[c, :]
        if last is not None:
            delta_in = (backward * own_curve).astype(bf16)
            small_ref[0:cols, :] += dot_rows(delta_in, lines)
            small_ref[cols : 2 * cols, :] += dot_rows(own_delta, lines)
            small_ref[2 * cols :, :] += dot_rows(old_mixed[own, :], lines)
        if coming is not None:
            predicted = dot(readout, mixed[...])[0:1] + b_out_ref[0]
            gap_ref[...] = predicted - target

    tile(0, None, even)

    def two_tiles(u, carry):
        tile(2 * u + 1, even, odd)
        tile(2 * u + 2, odd, even)
        return carry

    lax.fori_loop(0, (tiles - 1) // 2, two_tiles, 0)
    if tiles % 2 == 0:
        tile(tiles - 1, even, odd)
        tile(tiles, odd, None)
    else:
        tile(tiles, even, None)

    lines = small_ref[...].T
    extra = [lines[0:7, 0:cols], lines[6:7, cols : 2 * cols]]
    extra.append(jnp.sum(lines[16:19, 2 * cols :], axis=0, keepdims=True))
    total = jnp.sum(slope_ref[...], axis=1, keepdims=True)
    extra.append(jnp.broadcast_to(total, (1, cols)))
    extra.append(jnp.zeros((6, cols), jnp.float32))
    extra = jnp.concatenate(extra, 0)
    extra_ref[...] = jnp.zeros_like(extra_ref)
    for j in range(4):
        lanes = slice((j % 2) * LANES, (j % 2 + 1) * LANES)
        extra_ref[j] = extra[8 * (j // 2) : 8 * (j // 2) + 8, lanes]
    low, top = place_ref[1], place_ref[2]
    for i in range(groups // 2):
        for a_ref, b_ref, flip in ((keep_a, keep_b, 0), (send_a, send_b, 1)):
            j = 2 * i + (low ^ flip)
            piece = pl.ds(pl.multiple_of(j * piece_rows, piece_rows), piece_rows)
            a_ref[i, 0:piece_rows, :] = grad_ref[piece, 0:LANES]
            a_ref[i, piece_rows:, :] = extra_ref[j]
            j = i + (top ^ flip) * (groups // 2)
            piece = pl.ds(pl.multiple_of(j * piece_rows, piece_rows), piece_rows)
            b_ref[i] = grad_ref[piece, LANES:]


def block_gradients(rows, sums, w_in, b_in, w_mid, b_mid, w_out, b_out, inv_sets, place, groups):
    sets = rows.shape[1]
    cols = WIDTH // 4
    scale = jnp.array([[4.0], [1.0], [1.0], [20.0]], jnp.float32)
    feat = jnp.pad(rows * scale, ((0, FEATURE_ROWS - 4), (PAIRS, LANES - PAIRS - sets)))
    vmem = pl.BlockSpec(memory_space=pltpu.VMEM)
    smem = pl.BlockSpec(memory_space=pltpu.SMEM)
    return pl.pallas_call(
        functools.partial(network_kernel, inv_sets),
        in_specs=[smem] + [vmem] * 8 + [smem],
        out_specs=[vmem] * 4,
        out_shape=[
            jax.ShapeDtypeStruct((groups // 2, WIDTH // groups + more, LANES), jnp.float32)
            for more in (8, 8, 0, 0)
        ],
        scratch_shapes=[
            pltpu.VMEM((FEATURE_ROWS + 3 * sets, LANES), jnp.float32),
            pltpu.VMEM((WIDTH, FEATURE_ROWS), jnp.bfloat16),
            pltpu.VMEM((WIDTH, WIDTH), jnp.bfloat16),
            pltpu.VMEM((WIDTH, ROW_TILE), jnp.float32),
            pltpu.VMEM((WIDTH, ROW_TILE), jnp.float32),
            pltpu.VMEM((WIDTH, cols), jnp.float32),
            pltpu.VMEM((3 * cols, 32), jnp.float32),
            pltpu.VMEM((1, ROW_TILE), jnp.float32),
            pltpu.VMEM((WIDTH, ROW_TILE), jnp.bfloat16),
            pltpu.VMEM((max(groups, 4), 8, LANES), jnp.float32),
        ]
        + [
            pltpu.VMEM(shape, kind)
            for shape, kind in (
                ((WIDTH, ROW_TILE), jnp.bfloat16),
                ((FEATURE_ROWS, ROW_TILE), jnp.bfloat16),
                ((1, ROW_TILE), jnp.float32),
                ((WIDTH, ROW_TILE), jnp.bfloat16),
                ((WIDTH, ROW_TILE), jnp.float32),
            )
            for _ in range(2)
        ],
        compiler_params=pltpu.CompilerParams(vmem_limit_bytes=48 * 1024 * 1024),
        name="network",
    )(
        place, jnp.asarray(row_maps(sets)), feat + feature_base(sets), sums, w_in,
        b_in.reshape(1, -1), w_mid, b_mid.reshape(1, -1), w_out.reshape(1, -1), b_out,
    )


def scaling_kernel(layout, groups, owner_ref, *refs):
    blocks = refs[: len(layout)]
    w_in_ref, b_in_ref, w_mid_ref, b_mid_ref, w_out_ref, b_out_ref, extra_ref, small_ref = refs[
        len(layout) :
    ]
    piece_rows = WIDTH // groups
    cols = WIDTH // 4
    owner = owner_ref[0]
    parts = []
    for ref, (masks, contents) in zip(blocks, layout):
        for i, mask in enumerate(masks):
            device = owner ^ mask
            index = (device >> 1) & (groups - 1)
            column = 2 * (device // (2 * groups)) + (device & 1)
            start = 0
            for content in contents:
                if content == "extra":
                    extra_ref[index, column] = ref[i, start : start + 8, :]
                    start += 8
                else:
                    parts.append((ref, i, start, index, column, content == "right"))
                    start += piece_rows

    total = jnp.zeros((8, LANES), jnp.float32)
    for ref, i, start, index, column, right in parts:
        part = ref[i, start : start + piece_rows, :]
        total = total + jnp.sum((part * part).reshape(-1, 8, LANES), axis=0)
    for column in range(4):
        for j in range(4):
            first = column * cols + (j % 2) * LANES
            small_ref[8 * (j // 2) : 8 * (j // 2) + 8, first : first + LANES] = extra_ref[j, column]
    small = small_ref[...]
    squares = jnp.sum(small * small, axis=1, keepdims=True)
    bias_out = small_ref[9:10, 0:1]
    last = bias_out * bias_out

    def factor(total, entries):
        return lax.rsqrt(total / entries + EPSILON)

    total = jnp.sum(jnp.sum(total, axis=1, keepdims=True), axis=0, keepdims=True)
    scale_mid = factor(total + squares[7:8], WIDTH * WIDTH + WIDTH)
    scale_in = factor(jnp.sum(squares[0:7], axis=0, keepdims=True), 7 * WIDTH)
    scale_out = factor(squares[8:9] + last, WIDTH + 1)
    w_in_ref[...] = small[0:6] * scale_in
    b_in_ref[...] = small[6:7] * scale_in
    b_mid_ref[...] = small[7:8] * scale_mid
    w_out_ref[...] = small[8:9] * scale_out
    b_out_ref[...] = bias_out * scale_out
    for ref, i, start, index, column, right in parts:
        rows = pl.ds(pl.multiple_of(index * piece_rows, piece_rows), piece_rows)
        first = pl.multiple_of(column * cols + (LANES if right else 0), LANES)
        part = ref[i, start : start + piece_rows, :]
        w_mid_ref[rows, pl.ds(first, LANES)] = part * scale_mid


def scaled(owner, groups, received):
    vmem = pl.BlockSpec(memory_space=pltpu.VMEM)
    shapes = [(6, WIDTH), (1, WIDTH), (WIDTH, WIDTH), (1, WIDTH), (1, WIDTH), (1, 1)]
    layout = [(masks, contents) for _, masks, contents in received]
    return pl.pallas_call(
        functools.partial(scaling_kernel, layout, groups),
        in_specs=[pl.BlockSpec(memory_space=pltpu.SMEM)] + [vmem] * len(received),
        out_specs=[vmem] * 6,
        out_shape=[jax.ShapeDtypeStruct(shape, jnp.float32) for shape in shapes],
        scratch_shapes=[
            pltpu.VMEM((max(groups, 4), 4, 8, LANES), jnp.float32),
            pltpu.VMEM((16, WIDTH), jnp.float32),
        ],
        compiler_params=pltpu.CompilerParams(vmem_limit_bytes=32 * 1024 * 1024),
        name="scaling",
    )(owner.reshape(1), *[array for array, _, _ in received])


def swap(array, bit, devices):
    return lax.ppermute(array, "paths", [(i, i ^ bit) for i in range(devices)])


def pick(array, index):
    return lax.dynamic_index_in_dim(array, index, 0, keepdims=False)


def halved(part, left, bit, group, devices):
    axis = len(left) - 1 - left.index(bit)
    shape = part.shape[1:]
    cube = part.reshape((2,) * len(left) + shape)
    mine = (group >> bit) % 2
    keep = lax.dynamic_index_in_dim(cube, mine, axis, keepdims=False)
    send = lax.dynamic_index_in_dim(cube, 1 - mine, axis, keepdims=False)
    send, keep = send.reshape((-1,) + shape), keep.reshape((-1,) + shape)
    return keep + swap(send, 2 << bit, devices)


def on_device(params, increments, w_in, b_in, w_mid, b_mid, w_out, b_out):
    devices = lax.axis_size("paths")
    top = devices // 2
    groups = devices // 4
    total_paths = increments.shape[2] * devices
    set_count = params.shape[0]
    set_dev = set_count // devices
    owner = lax.axis_index("paths")
    core = owner % 2
    high = owner // top
    group = (owner // 2) % groups
    block = 2 * high + core
    turned = params.T

    sums = payoff_sums(turned, increments)
    sums = sums.reshape(2, groups, 2 * set_dev, PAIRS).swapaxes(0, 1)
    sums = sums.reshape(groups, 4 * set_dev, PAIRS)
    lanes = [[2 * j + c + top * h for j in range(groups)] for h in range(2) for c in range(2)]
    sums = jnp.sum(lax.all_to_all(sums, "paths", 0, 0, axis_index_groups=lanes, tiled=True), axis=0)
    sums = sums + swap(sums, 1, devices)
    sums = (sums + swap(sums, top, devices)) / total_paths
    prices = pick(sums.reshape(4, set_dev, PAIRS), block)

    rows = pick(turned.reshape(4, 2, groups, 2 * set_dev).transpose(2, 0, 1, 3), group)
    place = jnp.stack([block, group % 2, group // (groups // 2)])
    keep_a, send_a, keep_b, send_b = block_gradients(
        rows.reshape(4, 4 * set_dev), sums, w_in, b_in, w_mid, b_mid, w_out, b_out,
        1.0 / set_count, place, groups,
    )

    bits = [bit for bit in range(groups.bit_length() - 1)]
    part_a = keep_a + swap(send_a, 2, devices)
    part_b = keep_b + swap(send_b, top // 2, devices)
    left_a, left_b = bits[1:], bits[:-1]
    while left_a:
        part_a = halved(part_a, left_a, left_a[0], group, devices)
        part_b = halved(part_b, left_b, left_b[0], group, devices)
        left_a, left_b = left_a[1:], left_b[1:]

    own = jnp.concatenate([part_a, part_b], axis=1)
    far = (0, top // 2, top, top + top // 2)
    whole = jnp.concatenate([own] + [swap(own, mask, devices) for mask in far[1:]], axis=0)
    received = [(whole, far, ("left", "extra", "right"))]
    split = part_a.shape[1]
    held_a, held_b = whole[:, :split], whole[:, split:]
    order = [2 << bit for bit in bits[:-1]]
    masks_a = masks_b = far
    for bit_a, bit_b in zip(order, order[1:] + order[:1]):
        came_a, came_b = swap(held_a, bit_a, devices), swap(held_b, bit_b, devices)
        new_a = tuple(mask ^ bit_a for mask in masks_a)
        new_b = tuple(mask ^ bit_b for mask in masks_b)
        received += [(came_a, new_a, ("left", "extra")), (came_b, new_b, ("right",))]
        if bit_a != order[-1]:
            held_a = jnp.concatenate([held_a, came_a], axis=0)
            held_b = jnp.concatenate([held_b, came_b], axis=0)
        masks_a, masks_b = masks_a + new_a, masks_b + new_b
    received += [
        (swap(array, 1, devices), tuple(mask ^ 1 for mask in masks), contents)
        for array, masks, contents in received
    ]
    result = scaled(owner, groups, received)
    direction_w_in, direction_b_in, direction_w_mid, direction_b_mid, direction_w_out, direction_b_out = result
    return (
        prices,
        direction_w_in,
        direction_b_in.reshape(WIDTH),
        direction_w_mid,
        direction_b_mid.reshape(WIDTH),
        direction_w_out.reshape(WIDTH),
        direction_b_out.reshape(1),
    )


def solution(mesh):
    in_specs = (P(), P(None, None, "paths"), P(), P(), P(), P(), P(), P())
    out_specs = (P("paths", None), P(), P(), P(), P(), P(), P())
    return jax.shard_map(
        on_device, mesh=mesh, in_specs=in_specs, out_specs=out_specs, check_vma=False
    )
```

```python
import functools
import math

import jax
import jax.numpy as jnp
import numpy as np
from jax import lax
from jax.experimental import pallas as pl
from jax.experimental.pallas import tpu as pltpu
from jax.sharding import PartitionSpec as P

STEPS = 64
MATS = 8
STRIKES = 11
PAIRS = 88
WIDTH = 1024
LANES = 128
FEATURE_ROWS = 16
ROW_TILE = 256
FORWARD_VMEM = 24 * 1024 * 1024
BACKWARD_VMEM = 24 * 1024 * 1024
CHUNK = 256
CHUNKS = [slice(start, start + CHUNK) for start in range(0, WIDTH, CHUNK)]
EPSILON = 1e-06


TENORS = (np.arange(MATS, dtype=np.float32) + np.float32(1.0)) / np.float32(MATS)
OFFSETS = np.arange(STRIKES, dtype=np.float32) - np.float32((STRIKES - 1) / 2.0)
LOG_STRIKE = np.float32(0.05) * OFFSETS[None, :] * np.sqrt(TENORS)[:, None]
SET_BLOCK = 256
LOG2E = 1.4426950408889634


def bf16_pieces(value):
    high = value.astype(jnp.bfloat16)
    rest = value - high.astype(jnp.float32)
    mid = rest.astype(jnp.bfloat16)
    low = (rest - mid.astype(jnp.float32)).astype(jnp.bfloat16)
    return high, mid, low


def pricing_kernel(params_ref, inc_ref, out_ref, lags_ref, noise_ref, comp_ref, pay_ref):
    sets = params_ref.shape[1]
    paths = inc_ref.shape[2]
    hurst = params_ref[0:1, :]
    vol_of_vol = params_ref[1:2, :]
    correl = params_ref[2:3, :]
    forward_var = params_ref[3:4, :]
    delta_t = 1.0 / STEPS

    lag = (LANES - lax.broadcasted_iota(jnp.int32, (LANES, 1), 0)).astype(jnp.float32)
    exponent = hurst + 0.5
    here = jnp.exp2(exponent * jnp.log2(lag))
    before = jnp.exp2(exponent * jnp.log2(jnp.maximum(lag - 1.0, 1.0)))
    before = jnp.where(lag > 1.5, before, 0.0)
    front = jnp.sqrt(2.0 * hurst) * jnp.exp2(hurst * math.log2(delta_t)) / exponent
    weights = jnp.where(lag < STEPS - 0.5, (here - before) * front, 0.0).astype(jnp.bfloat16)

    half_scale = vol_of_vol * (0.5 * LOG2E)
    step = lax.broadcasted_iota(jnp.int32, (STEPS, 1), 0).astype(jnp.float32)
    powers = jnp.exp2(2.0 * hurst * jnp.log2(jnp.maximum(step, 1.0) * delta_t))
    comp_ref[...] = jnp.where(step > 0.5, powers * (0.25 * LOG2E * vol_of_vol * vol_of_vol), 0.0)

    root = jnp.sqrt(forward_var * delta_t)
    back = 2.0 / root
    growth = (0.5 * LOG2E) * forward_var * delta_t
    noise_weights = jnp.concatenate(
        [
            jnp.broadcast_to(piece.astype(jnp.float32), (8, sets))
            for value in (correl * back, jnp.sqrt(1.0 - correl * correl) * back)
            for piece in bf16_pieces(value)
        ]
        + [jnp.zeros((LANES - 48, sets), jnp.float32)],
        axis=0,
    ).astype(jnp.bfloat16)

    first = inc_ref[0].astype(jnp.float32)
    second = inc_ref[1].astype(jnp.float32)
    lags_ref[...] = jnp.concatenate([first, jnp.zeros((LANES - STEPS, paths), jnp.float32)], 0).T
    for m in range(MATS):
        rows = slice(8 * m, 8 * m + 8)
        block = jnp.concatenate(
            [first[rows]] * 3 + [second[rows]] * 3 + [jnp.zeros((LANES - 48, paths), jnp.float32)], 0
        )
        noise_ref[m] = block.T.astype(jnp.bfloat16)
    lane = lax.broadcasted_iota(jnp.int32, (paths, LANES), 1)

    def maturity(m, total):
        noise = noise_ref[m]
        for k in range(8):
            i = 8 * m + k
            window = lags_ref[...] if k == 0 else pltpu.roll(lags_ref[...], LANES - k, 1)
            drive = jnp.dot(
                window.astype(jnp.bfloat16), weights, preferred_element_type=jnp.float32
            )
            picked = jnp.where(lane % 8 == k, noise.astype(jnp.float32), 0.0).astype(jnp.bfloat16)
            shock = jnp.dot(picked, noise_weights, preferred_element_type=jnp.float32)
            root_variance = jnp.exp2(drive * half_scale - comp_ref[pl.ds(i, 1), :])
            total = total + root_variance * (shock - root_variance)
        lags_ref[...] = pltpu.roll(lags_ref[...], LANES - 8, 1)
        spot = jnp.exp2(total * growth)
        tenor = jnp.full((8, sets), 1.0, jnp.float32) * ((m + 1).astype(jnp.float32) / MATS)
        spread = jnp.sqrt(tenor)
        for j in range(STRIKES):
            strike = jnp.exp((0.05 * (j - (STRIKES - 1) / 2.0)) * spread)
            gains = jnp.maximum(spot.reshape(paths // 8, 8, sets), strike[None]).sum(axis=0)
            gains = gains - strike * (paths // 8)
            pay_ref[pl.ds(m * STRIKES + j, 1), :] = jnp.sum(gains, axis=0, keepdims=True)
        return total

    lax.fori_loop(0, MATS, maturity, jnp.zeros((paths, sets), jnp.float32))
    out_ref[...] = pay_ref[...].T[:, :PAIRS]


def payoff_sums(params, increments):
    count = params.shape[1]
    paths = increments.shape[2]
    sets = math.gcd(count, SET_BLOCK)
    return pl.pallas_call(
        pricing_kernel,
        grid=(count // sets,),
        in_specs=[
            pl.BlockSpec((4, sets), lambda b: (0, b)),
            pl.BlockSpec((2, STEPS, paths), lambda b: (0, 0, 0)),
        ],
        out_specs=pl.BlockSpec((sets, PAIRS), lambda b: (b, 0)),
        out_shape=jax.ShapeDtypeStruct((count, PAIRS), jnp.float32),
        scratch_shapes=[
            pltpu.VMEM((paths, LANES), jnp.float32),
            pltpu.VMEM((MATS, paths, LANES), jnp.bfloat16),
            pltpu.VMEM((STEPS, sets), jnp.float32),
            pltpu.VMEM((LANES, sets), jnp.float32),
        ],
        compiler_params=pltpu.CompilerParams(vmem_limit_bytes=32 * 1024 * 1024),
        name="pricing",
    )(in_hbm(params), in_hbm(increments))


def in_hbm(array):
    return pltpu.with_memory_space_constraint(array, pltpu.HBM)


def dot(left, right):
    return jnp.dot(left, right, preferred_element_type=jnp.float32)


def dot_rows(left, right):
    return lax.dot_general(
        left, right, (((1,), (1,)), ((), ())), preferred_element_type=jnp.float32
    )


def one_hot(t, sets):
    row = t * ROW_TILE + lax.broadcasted_iota(jnp.int32, (1, ROW_TILE), 1)
    group_set = ((row.astype(jnp.float32) + 0.5) * (1.0 / PAIRS)).astype(jnp.int32)
    pair = row - PAIRS * group_set
    code = lax.broadcasted_iota(jnp.int32, (LANES, ROW_TILE), 0)
    hot = jnp.where((code == pair) | (code == group_set + PAIRS), 1.0, 0.0)
    return hot.astype(jnp.bfloat16), group_set


def feature_table(params_ref, group, sets):
    set_count = params_ref.shape[1]
    lane = lax.broadcasted_iota(jnp.int32, (1, LANES), 1)
    maturity = ((lane.astype(jnp.float32) + 0.5) * (1.0 / STRIKES)).astype(jnp.int32)
    offset = (lane - STRIKES * maturity).astype(jnp.float32) - (STRIKES - 1) / 2.0
    spread = jnp.zeros((1, LANES), jnp.float32)
    for m in range(MATS):
        spread = jnp.where(maturity == m, float(np.sqrt(TENORS)[m]), spread)
    strikes = jnp.where(lane < PAIRS, 4.0 * (0.05 * offset * spread), 0.0)
    tenors = jnp.where(lane < PAIRS, (maturity.astype(jnp.float32) + 1.0) / MATS, 0.0)
    ones = jnp.where((lane >= PAIRS) & (lane < PAIRS + sets), 1.0, 0.0)
    wide = jnp.concatenate([params_ref[...], jnp.zeros((4, set_count), jnp.float32)], 0)
    half = sets // 2
    own = jnp.zeros((8, LANES), jnp.float32)
    for high in range(2):
        first = PAIRS + high * half
        start = high * (set_count // 2) + group * half
        moved = pltpu.roll(wide, lax.rem(first + set_count - start, set_count), 1)[:, :LANES]
        own = jnp.where((lane >= first) & (lane < first + half), moved, own)
    scale = [own[0:1] * 4.0, own[1:2], own[2:3], own[3:4] * 20.0]
    pad = jnp.zeros((FEATURE_ROWS - 9, LANES), jnp.float32)
    return jnp.concatenate(scale + [strikes, tenors, ones, ones, ones, pad], 0)


def prepare_kernel(
    w_in_hbm, b_in_hbm, w_mid_hbm, win_ref, turned_ref, w_in_ref, b_in_ref, w_mid_ref, sems
):
    copies = [
        pltpu.make_async_copy(source, target, sems.at[i])
        for i, (source, target) in enumerate(
            ((w_in_hbm, w_in_ref), (b_in_hbm, b_in_ref), (w_mid_hbm, w_mid_ref))
        )
    ]
    for copy in copies:
        copy.start()
    for copy in copies:
        copy.wait()
    weights_in = w_in_ref[...].astype(jnp.float32)
    bias_in = [piece.astype(jnp.float32) for piece in bf16_pieces(b_in_ref[...])]
    pad = jnp.zeros((FEATURE_ROWS - weights_in.shape[0] - 3, WIDTH), jnp.float32)
    win = (0.5 * jnp.concatenate([weights_in] + bias_in + [pad], 0)).T
    win_ref[...] = win.astype(jnp.bfloat16)
    turned_ref[...] = (0.5 * w_mid_ref[...].astype(jnp.float32)).T.astype(jnp.bfloat16)


def prepare(w_in, b_in, w_mid):
    vmem = pl.BlockSpec(memory_space=pltpu.VMEM)
    hbm = pl.BlockSpec(memory_space=pltpu.HBM)
    return pl.pallas_call(
        prepare_kernel,
        in_specs=[hbm] * 3,
        out_specs=[vmem] * 2,
        out_shape=[
            jax.ShapeDtypeStruct((WIDTH, FEATURE_ROWS), jnp.bfloat16),
            jax.ShapeDtypeStruct((WIDTH, WIDTH), jnp.bfloat16),
        ],
        scratch_shapes=[
            pltpu.VMEM(w_in.shape, jnp.bfloat16),
            pltpu.VMEM((1, WIDTH), jnp.float32),
            pltpu.VMEM((WIDTH, WIDTH), jnp.bfloat16),
            pltpu.SemaphoreType.DMA((3,)),
        ],
        compiler_params=pltpu.CompilerParams(vmem_limit_bytes=16 * 1024 * 1024),
        name="prepare",
    )(in_hbm(w_in), in_hbm(b_in.reshape(1, -1)), in_hbm(w_mid))


def forward_kernel(
    sets, owner_ref, params_ref, b_mid_ref, w_out_ref, win_ref, turned_ref,
    hidden_out, curve_out, own_curve_out, mixed_out, feat_out, pred_out, bias_ref, read_ref,
    even_hidden, odd_hidden, even_mixed, odd_mixed,
):
    bf16 = jnp.bfloat16
    tiles = hidden_out.shape[1] // ROW_TILE
    cols = WIDTH // 4
    owner = owner_ref[0]
    devices = params_ref.shape[1] * 4 // sets
    block = 2 * (owner // (devices // 2)) + owner % 2
    group = (owner // 2) % (devices // 4)
    own = pl.ds(pl.multiple_of(block * cols, cols), cols)
    table = feature_table(params_ref, group, sets).astype(bf16)
    read_ref[...] = jnp.broadcast_to((0.5 * w_out_ref[...].astype(jnp.float32)).T, read_ref.shape)
    readout = jnp.broadcast_to(w_out_ref[...].astype(jnp.float32), (16, WIDTH)).astype(bf16)
    bias_ref[...] = jnp.broadcast_to((0.5 * b_mid_ref[...]).T, bias_ref.shape)

    def span(t):
        return pl.ds(pl.multiple_of(t * ROW_TILE, ROW_TILE), ROW_TILE)

    def step(t, new, old, first=True, second=True, third=True):
        new_hidden, new_mixed = new
        old_hidden, old_mixed = old
        if third:
            pred_out[0:1, span(t - 2)] = dot(readout, new_mixed[...])[0:1]
            mixed_out[:, span(t - 2)] = new_mixed[own, :]
        if first:
            hot, _ = one_hot(t, sets)
            feat = dot(table, hot).astype(bf16)
            feat_out[:, span(t)] = feat
        for c in CHUNKS:
            if second:
                half_mid = dot(turned_ref[c, :], old_hidden[...]) + bias_ref[c, :]
            if first:
                half_in = dot(win_ref[c, :], feat)
            if second:
                wave = jnp.tanh(half_mid)
                turn = half_mid * wave
                old_mixed[c, :] = (half_mid + turn).astype(bf16)
                curve_out[c, span(t - 1)] = (1.0 + wave) * (1.0 + half_mid - turn) * read_ref[c, :]
            if first:
                value = (half_in + half_in * jnp.tanh(half_in)).astype(bf16)
                new_hidden[c, :] = value
                hidden_out[c, span(t)] = value
        if first:
            own_half = dot(win_ref[own, :], feat)
            own_wave = jnp.tanh(own_half)
            own_curve_out[:, span(t)] = (0.5 * (1.0 + own_wave)) * (
                1.0 + own_half * (1.0 - own_wave)
            )

    even, odd = (even_hidden, even_mixed), (odd_hidden, odd_mixed)
    step(0, even, odd, second=False, third=False)
    step(1, odd, even, third=False)

    def two_steps(u, carry):
        step(2 * u + 2, even, odd)
        step(2 * u + 3, odd, even)
        return carry

    lax.fori_loop(0, (tiles - 2) // 2, two_steps, 0)
    buffers = [even, odd]
    for t in range(2 + (tiles - 2) // 2 * 2, tiles + 2):
        step(t, buffers[t % 2], buffers[1 - t % 2], first=t < tiles, second=t <= tiles)


def forward(owner, params, b_mid, w_out, win, turned, sets):
    rows = sets * PAIRS
    cols = WIDTH // 4
    vmem = pl.BlockSpec(memory_space=pltpu.VMEM)
    smem = pl.BlockSpec(memory_space=pltpu.SMEM)
    outs = [
        ((WIDTH, rows), jnp.bfloat16),
        ((WIDTH, rows), jnp.float32),
        ((cols, rows), jnp.float32),
        ((cols, rows), jnp.bfloat16),
        ((FEATURE_ROWS, rows), jnp.bfloat16),
        ((1, rows), jnp.float32),
    ]
    return pl.pallas_call(
        functools.partial(forward_kernel, sets),
        in_specs=[smem] + [vmem] * 5,
        out_specs=[vmem] * len(outs),
        out_shape=[pltpu.VMEM(shape, kind) for shape, kind in outs[:-1]]
        + [jax.ShapeDtypeStruct(*outs[-1])],
        scratch_shapes=[
            pltpu.VMEM((WIDTH, ROW_TILE), jnp.float32),
            pltpu.VMEM((WIDTH, ROW_TILE), jnp.float32),
        ]
        + [pltpu.VMEM((WIDTH, ROW_TILE), jnp.bfloat16)] * 4,
        compiler_params=pltpu.CompilerParams(vmem_limit_bytes=FORWARD_VMEM),
        cost_estimate=pl.CostEstimate(
            flops=2 * rows * WIDTH * (WIDTH + 32), bytes_accessed=4 << 20, transcendentals=0
        ),
        name="forward",
    )(
        owner.reshape(1), in_hbm(params), in_hbm(b_mid.reshape(1, -1)), w_out.reshape(1, -1), win,
        turned,
    )


def backward_kernel(
    inv_sets, owner_ref, sums_ref, near_ref, far_ref, both_ref, hidden_ref, curve_ref, own_curve_ref, mixed_ref, feat_ref,
    pred_ref, w_mid_hbm, b_out_ref, keep_a, send_a, keep_b, send_b,
    left_ref, back_ref, slope_ref, delta_ref, delta_in_ref, own_delta_ref, lines_ref, extra_ref,
    grad_ref, sem,
):
    bf16 = jnp.bfloat16
    sets = sums_ref.shape[0]
    rows = hidden_ref.shape[1]
    groups = 2 * keep_a.shape[0]
    piece_rows = WIDTH // groups
    cols = WIDTH // 4
    owner = owner_ref[0]
    block = 2 * (owner // (2 * groups)) + owner % 2
    own = pl.ds(pl.multiple_of(block * cols, cols), cols)
    fetch = pltpu.make_async_copy(w_mid_hbm.at[own, :], back_ref, sem)
    fetch.start()

    left_ref[...] = jnp.zeros_like(left_ref)
    sums = (sums_ref[...] + near_ref[...]) + (far_ref[...] + both_ref[...])
    for p, piece in enumerate(bf16_pieces(sums)):
        left_ref[p * sets : (p + 1) * sets, :PAIRS] = piece.astype(jnp.float32)
    left = left_ref[...].astype(bf16)
    lines_ref[...] = jnp.zeros_like(lines_ref)
    lines_ref[0:FEATURE_ROWS, :] = feat_ref[...]

    def slopes(t, carry):
        here = pl.ds(pl.multiple_of(t * ROW_TILE, ROW_TILE), ROW_TILE)
        hot, group_set = one_hot(t, sets)
        looked = dot(left, hot)
        target = looked[:sets] + looked[sets : 2 * sets] + looked[2 * sets :]
        member = lax.broadcasted_iota(jnp.int32, (sets, ROW_TILE), 0)
        target = jnp.sum(jnp.where(member == group_set, target, 0.0), axis=0, keepdims=True)
        slope = (pred_ref[0:1, here] + b_out_ref[0] - target) * inv_sets
        slope_ref[0:1, here] = slope
        pieces = [piece.astype(jnp.float32) for piece in bf16_pieces(slope)]
        pieces = jnp.concatenate(pieces + [jnp.zeros((13, ROW_TILE), jnp.float32)], 0)
        lines_ref[FEATURE_ROWS:, here] = pieces.astype(bf16)
        return carry

    lax.fori_loop(0, rows // ROW_TILE, slopes, 0)
    fetch.wait()

    def tile(t, carry):
        here = pl.ds(pl.multiple_of(t * ROW_TILE, ROW_TILE), ROW_TILE)
        slope = slope_ref[0:1, here]
        for c in CHUNKS:
            delta_ref[c, :] = (slope * curve_ref[c, here]).astype(bf16)
        backward = dot(back_ref[...], delta_ref[...])
        delta_in_ref[:, here] = (backward * own_curve_ref[:, here]).astype(bf16)
        own_delta_ref[:, here] = delta_ref[own, :]
        return carry

    lax.fori_loop(0, rows // ROW_TILE, tile, 0)

    for c in CHUNKS:
        grad_ref[c, :] = dot_rows(hidden_ref[c, :], own_delta_ref[...])
    lines = lines_ref[...]
    extra = [dot_rows(delta_in_ref[...], lines).T[0:7]]
    extra.append(dot_rows(own_delta_ref[...], lines).T[6:7])
    extra.append(jnp.sum(dot_rows(mixed_ref[...], lines).T[16:19], axis=0, keepdims=True))
    total = jnp.sum(slope_ref[...], axis=1, keepdims=True)
    extra.append(jnp.broadcast_to(total, (1, cols)))
    extra.append(jnp.zeros((6, cols), jnp.float32))
    extra = jnp.concatenate(extra, 0)
    extra_ref[...] = jnp.zeros_like(extra_ref)
    for j in range(4):
        lanes = slice((j % 2) * LANES, (j % 2 + 1) * LANES)
        extra_ref[j] = extra[8 * (j // 2) : 8 * (j // 2) + 8, lanes]
    group = (owner // 2) % groups
    low, top = group % 2, group // (groups // 2)
    for i in range(groups // 2):
        for a_ref, b_ref, flip in ((keep_a, keep_b, 0), (send_a, send_b, 1)):
            j = 2 * i + (low ^ flip)
            piece = pl.ds(pl.multiple_of(j * piece_rows, piece_rows), piece_rows)
            a_ref[i, 0:piece_rows, :] = grad_ref[piece, 0:LANES]
            a_ref[i, piece_rows:, :] = extra_ref[j]
            j = i + (top ^ flip) * (groups // 2)
            piece = pl.ds(pl.multiple_of(j * piece_rows, piece_rows), piece_rows)
            b_ref[i] = grad_ref[piece, LANES:]


def backward(owner, sums, saved, w_mid, b_out, inv_sets, groups):
    sets = sums[0].shape[0]
    rows = sets * PAIRS
    cols = WIDTH // 4
    vmem = pl.BlockSpec(memory_space=pltpu.VMEM)
    smem = pl.BlockSpec(memory_space=pltpu.SMEM)
    hbm = pl.BlockSpec(memory_space=pltpu.HBM)
    return pl.pallas_call(
        functools.partial(backward_kernel, inv_sets),
        in_specs=[smem] + [vmem] * 10 + [hbm, smem],
        out_specs=[vmem] * 4,
        out_shape=[
            jax.ShapeDtypeStruct((groups // 2, WIDTH // groups + more, LANES), jnp.float32)
            for more in (8, 8, 0, 0)
        ],
        scratch_shapes=[
            pltpu.VMEM((3 * sets, LANES), jnp.float32),
            pltpu.VMEM((cols, WIDTH), jnp.bfloat16),
            pltpu.VMEM((1, rows), jnp.float32),
            pltpu.VMEM((WIDTH, ROW_TILE), jnp.bfloat16),
            pltpu.VMEM((cols, rows), jnp.bfloat16),
            pltpu.VMEM((cols, rows), jnp.bfloat16),
            pltpu.VMEM((2 * FEATURE_ROWS, rows), jnp.bfloat16),
            pltpu.VMEM((max(groups, 4), 8, LANES), jnp.float32),
            pltpu.VMEM((WIDTH, cols), jnp.float32),
            pltpu.SemaphoreType.DMA,
        ],
        compiler_params=pltpu.CompilerParams(vmem_limit_bytes=BACKWARD_VMEM),
        name="backward",
    )(owner.reshape(1), *sums, *saved, in_hbm(w_mid), b_out)


def scaling_kernel(layout, groups, owner_ref, *refs):
    blocks = refs[: len(layout)]
    w_in_ref, b_in_ref, w_mid_ref, b_mid_ref, w_out_ref, b_out_ref, extra_ref, small_ref = refs[
        len(layout) :
    ]
    piece_rows = WIDTH // groups
    cols = WIDTH // 4
    owner = owner_ref[0]
    parts = []
    for ref, (masks, contents) in zip(blocks, layout):
        for i, mask in enumerate(masks):
            device = owner ^ mask
            index = (device >> 1) & (groups - 1)
            column = 2 * (device // (2 * groups)) + (device & 1)
            start = 0
            for content in contents:
                if content == "extra":
                    extra_ref[index, column] = ref[i, start : start + 8, :]
                    start += 8
                else:
                    parts.append((ref, i, start, index, column, content == "right"))
                    start += piece_rows

    total = jnp.zeros((8, LANES), jnp.float32)
    for ref, i, start, index, column, right in parts:
        part = ref[i, start : start + piece_rows, :]
        total = total + jnp.sum((part * part).reshape(-1, 8, LANES), axis=0)
    for column in range(4):
        for j in range(4):
            first = column * cols + (j % 2) * LANES
            small_ref[8 * (j // 2) : 8 * (j // 2) + 8, first : first + LANES] = extra_ref[j, column]
    small = small_ref[...]
    squares = jnp.sum(small * small, axis=1, keepdims=True)
    bias_out = small_ref[9:10, 0:1]
    last = bias_out * bias_out

    def factor(total, entries):
        return lax.rsqrt(total / entries + EPSILON)

    total = jnp.sum(jnp.sum(total, axis=1, keepdims=True), axis=0, keepdims=True)
    scale_mid = factor(total + squares[7:8], WIDTH * WIDTH + WIDTH)
    scale_in = factor(jnp.sum(squares[0:7], axis=0, keepdims=True), 7 * WIDTH)
    scale_out = factor(squares[8:9] + last, WIDTH + 1)
    w_in_ref[...] = small[0:6] * scale_in
    b_in_ref[...] = small[6:7] * scale_in
    b_mid_ref[...] = small[7:8] * scale_mid
    w_out_ref[...] = small[8:9] * scale_out
    b_out_ref[...] = bias_out * scale_out
    for ref, i, start, index, column, right in parts:
        rows = pl.ds(pl.multiple_of(index * piece_rows, piece_rows), piece_rows)
        first = pl.multiple_of(column * cols + (LANES if right else 0), LANES)
        part = ref[i, start : start + piece_rows, :]
        w_mid_ref[rows, pl.ds(first, LANES)] = part * scale_mid


def scaled(owner, groups, received):
    vmem = pl.BlockSpec(memory_space=pltpu.VMEM)
    shapes = [(6, WIDTH), (1, WIDTH), (WIDTH, WIDTH), (1, WIDTH), (1, WIDTH), (1, 1)]
    layout = [(masks, contents) for _, masks, contents in received]
    return pl.pallas_call(
        functools.partial(scaling_kernel, layout, groups),
        in_specs=[pl.BlockSpec(memory_space=pltpu.SMEM)] + [vmem] * len(received),
        out_specs=[vmem] * 6,
        out_shape=[jax.ShapeDtypeStruct(shape, jnp.float32) for shape in shapes],
        scratch_shapes=[
            pltpu.VMEM((max(groups, 4), 4, 8, LANES), jnp.float32),
            pltpu.VMEM((16, WIDTH), jnp.float32),
        ],
        compiler_params=pltpu.CompilerParams(vmem_limit_bytes=32 * 1024 * 1024),
        name="scaling",
    )(owner.reshape(1), *[array for array, _, _ in received])


def swap(array, bit, devices):
    return lax.ppermute(array, "paths", [(i, i ^ bit) for i in range(devices)])


def pick(array, index):
    return lax.dynamic_index_in_dim(array, index, 0, keepdims=False)


def halved(part, left, bit, group, devices):
    axis = len(left) - 1 - left.index(bit)
    shape = part.shape[1:]
    cube = part.reshape((2,) * len(left) + shape)
    mine = (group >> bit) % 2
    keep = lax.dynamic_index_in_dim(cube, mine, axis, keepdims=False)
    send = lax.dynamic_index_in_dim(cube, 1 - mine, axis, keepdims=False)
    send, keep = send.reshape((-1,) + shape), keep.reshape((-1,) + shape)
    return keep + swap(send, 2 << bit, devices)


def on_device(params, increments, w_in, b_in, w_mid, b_mid, w_out, b_out):
    devices = lax.axis_size("paths")
    top = devices // 2
    groups = devices // 4
    total_paths = increments.shape[2] * devices
    set_count = params.shape[0]
    set_dev = set_count // devices
    owner = lax.axis_index("paths")
    core = owner % 2
    high = owner // top
    group = (owner // 2) % groups
    block = 2 * high + core
    turned = params.T

    sums = payoff_sums(turned, increments)
    win, weights = prepare(w_in, b_in, w_mid)
    sums = sums.reshape(2, groups, 2 * set_dev, PAIRS).swapaxes(0, 1)
    sums = sums.reshape(groups, 4 * set_dev, PAIRS)
    lanes = [[2 * j + c + top * h for j in range(groups)] for h in range(2) for c in range(2)]
    parts = lax.all_to_all(sums, "paths", 0, 0, axis_index_groups=lanes, tiled=True)
    parts, win = lax.optimization_barrier((parts, win))
    sums = jnp.sum(parts, axis=0) / total_paths
    sums = [sums] + [swap(sums, mask, devices) for mask in (1, top, top + 1)]
    prices = sum(pick(part.reshape(4, set_dev, PAIRS), block) for part in sums)

    saved = forward(owner, turned, b_mid, w_out, win, weights, 4 * set_dev)
    keep_a, send_a, keep_b, send_b = backward(
        owner, sums, saved, w_mid, b_out, 1.0 / set_count, groups
    )

    bits = [bit for bit in range(groups.bit_length() - 1)]
    part_a = keep_a + swap(send_a, 2, devices)
    part_b = keep_b + swap(send_b, top // 2, devices)
    left_a, left_b = bits[1:], bits[:-1]
    while left_a:
        part_a = halved(part_a, left_a, left_a[0], group, devices)
        part_b = halved(part_b, left_b, left_b[0], group, devices)
        left_a, left_b = left_a[1:], left_b[1:]

    own = jnp.concatenate([part_a, part_b], axis=1)
    far = (0, top // 2, top, top + top // 2)
    whole = jnp.concatenate([own] + [swap(own, mask, devices) for mask in far[1:]], axis=0)
    received = [(whole, far, ("left", "extra", "right"))]
    split = part_a.shape[1]
    held_a, held_b = whole[:, :split], whole[:, split:]
    order = [2 << bit for bit in bits[:-1]]
    masks_a = masks_b = far
    for bit_a, bit_b in zip(order, order[1:] + order[:1]):
        came_a, came_b = swap(held_a, bit_a, devices), swap(held_b, bit_b, devices)
        new_a = tuple(mask ^ bit_a for mask in masks_a)
        new_b = tuple(mask ^ bit_b for mask in masks_b)
        received += [(came_a, new_a, ("left", "extra")), (came_b, new_b, ("right",))]
        if bit_a != order[-1]:
            held_a = jnp.concatenate([held_a, came_a], axis=0)
            held_b = jnp.concatenate([held_b, came_b], axis=0)
        masks_a, masks_b = masks_a + new_a, masks_b + new_b
    received += [
        (swap(array, 1, devices), tuple(mask ^ 1 for mask in masks), contents)
        for array, masks, contents in received
    ]
    result = scaled(owner, groups, received)
    direction_w_in, direction_b_in, direction_w_mid, direction_b_mid, direction_w_out, direction_b_out = result
    return (
        prices,
        direction_w_in,
        direction_b_in.reshape(WIDTH),
        direction_w_mid,
        direction_b_mid.reshape(WIDTH),
        direction_w_out.reshape(WIDTH),
        direction_b_out.reshape(1),
    )


def solution(mesh):
    in_specs = (P(), P(None, None, "paths"), P(), P(), P(), P(), P(), P())
    out_specs = (P("paths", None), P(), P(), P(), P(), P(), P())
    return jax.shard_map(
        on_device, mesh=mesh, in_specs=in_specs, out_specs=out_specs, check_vma=False
    )
```

```python
import functools
import math

import jax
import jax.numpy as jnp
import numpy as np
from jax import lax
from jax.experimental import pallas as pl
from jax.experimental.pallas import tpu as pltpu
from jax.sharding import PartitionSpec as P

STEPS = 64
MATS = 8
STRIKES = 11
PAIRS = 88
WIDTH = 1024
LANES = 128
FEATURE_ROWS = 16
ROW_TILE = 256
FORWARD_VMEM = 24 * 1024 * 1024
BACKWARD_VMEM = 24 * 1024 * 1024
CHUNK = 256
CHUNKS = [slice(start, start + CHUNK) for start in range(0, WIDTH, CHUNK)]
EPSILON = 1e-06


TENORS = (np.arange(MATS, dtype=np.float32) + np.float32(1.0)) / np.float32(MATS)
OFFSETS = np.arange(STRIKES, dtype=np.float32) - np.float32((STRIKES - 1) / 2.0)
LOG_STRIKE = np.float32(0.05) * OFFSETS[None, :] * np.sqrt(TENORS)[:, None]
SET_BLOCK = 256
LOG2E = 1.4426950408889634


def bf16_pieces(value):
    high = value.astype(jnp.bfloat16)
    rest = value - high.astype(jnp.float32)
    mid = rest.astype(jnp.bfloat16)
    low = (rest - mid.astype(jnp.float32)).astype(jnp.bfloat16)
    return high, mid, low


def pricing_kernel(params_ref, inc_ref, out_ref, lags_ref, noise_ref, comp_ref, pay_ref):
    sets = params_ref.shape[1]
    paths = inc_ref.shape[2]
    hurst = params_ref[0:1, :]
    vol_of_vol = params_ref[1:2, :]
    correl = params_ref[2:3, :]
    forward_var = params_ref[3:4, :]
    delta_t = 1.0 / STEPS

    lag = (LANES - lax.broadcasted_iota(jnp.int32, (LANES, 1), 0)).astype(jnp.float32)
    exponent = hurst + 0.5
    here = jnp.exp2(exponent * jnp.log2(lag))
    before = jnp.exp2(exponent * jnp.log2(jnp.maximum(lag - 1.0, 1.0)))
    before = jnp.where(lag > 1.5, before, 0.0)
    front = jnp.sqrt(2.0 * hurst) * jnp.exp2(hurst * math.log2(delta_t)) / exponent
    weights = jnp.where(lag < STEPS - 0.5, (here - before) * front, 0.0).astype(jnp.bfloat16)

    half_scale = vol_of_vol * (0.5 * LOG2E)
    step = lax.broadcasted_iota(jnp.int32, (STEPS, 1), 0).astype(jnp.float32)
    powers = jnp.exp2(2.0 * hurst * jnp.log2(jnp.maximum(step, 1.0) * delta_t))
    comp_ref[...] = jnp.where(step > 0.5, powers * (0.25 * LOG2E * vol_of_vol * vol_of_vol), 0.0)

    root = jnp.sqrt(forward_var * delta_t)
    back = 2.0 / root
    growth = (0.5 * LOG2E) * forward_var * delta_t
    noise_weights = jnp.concatenate(
        [
            jnp.broadcast_to(piece.astype(jnp.float32), (8, sets))
            for value in (correl * back, jnp.sqrt(1.0 - correl * correl) * back)
            for piece in bf16_pieces(value)
        ]
        + [jnp.zeros((LANES - 48, sets), jnp.float32)],
        axis=0,
    ).astype(jnp.bfloat16)

    first = inc_ref[0].astype(jnp.float32)
    second = inc_ref[1].astype(jnp.float32)
    lags_ref[...] = jnp.concatenate([first, jnp.zeros((LANES - STEPS, paths), jnp.float32)], 0).T
    for m in range(MATS):
        rows = slice(8 * m, 8 * m + 8)
        block = jnp.concatenate(
            [first[rows]] * 3 + [second[rows]] * 3 + [jnp.zeros((LANES - 48, paths), jnp.float32)], 0
        )
        noise_ref[m] = block.T.astype(jnp.bfloat16)
    lane = lax.broadcasted_iota(jnp.int32, (paths, LANES), 1)

    def maturity(m, total):
        noise = noise_ref[m]
        for k in range(8):
            i = 8 * m + k
            window = lags_ref[...] if k == 0 else pltpu.roll(lags_ref[...], LANES - k, 1)
            drive = jnp.dot(
                window.astype(jnp.bfloat16), weights, preferred_element_type=jnp.float32
            )
            picked = jnp.where(lane % 8 == k, noise.astype(jnp.float32), 0.0).astype(jnp.bfloat16)
            shock = jnp.dot(picked, noise_weights, preferred_element_type=jnp.float32)
            root_variance = jnp.exp2(drive * half_scale - comp_ref[pl.ds(i, 1), :])
            total = total + root_variance * (shock - root_variance)
        lags_ref[...] = pltpu.roll(lags_ref[...], LANES - 8, 1)
        spot = jnp.exp2(total * growth)
        tenor = jnp.full((8, sets), 1.0, jnp.float32) * ((m + 1).astype(jnp.float32) / MATS)
        spread = jnp.sqrt(tenor)
        for j in range(STRIKES):
            strike = jnp.exp((0.05 * (j - (STRIKES - 1) / 2.0)) * spread)
            gains = jnp.maximum(spot.reshape(paths // 8, 8, sets), strike[None]).sum(axis=0)
            gains = gains - strike * (paths // 8)
            pay_ref[pl.ds(m * STRIKES + j, 1), :] = jnp.sum(gains, axis=0, keepdims=True)
        return total

    lax.fori_loop(0, MATS, maturity, jnp.zeros((paths, sets), jnp.float32))
    paid = pay_ref[...].T[:, :PAIRS]
    blocks, halves, half = out_ref.shape[:3]
    for h in range(halves):
        rows = paid[h * blocks * half : (h + 1) * blocks * half]
        out_ref[:, h] = rows.reshape(blocks, half, PAIRS)


def payoff_sums(params, increments, groups):
    count = params.shape[1]
    paths = increments.shape[2]
    sets = math.gcd(count, SET_BLOCK)
    steps = count // sets
    half = count // groups // 2
    halves = 2 if steps == 1 else 1
    blocks = sets // half // halves
    return pl.pallas_call(
        pricing_kernel,
        grid=(steps,),
        in_specs=[
            pl.BlockSpec((4, sets), lambda b: (0, b)),
            pl.BlockSpec((2, STEPS, paths), lambda b: (0, 0, 0)),
        ],
        out_specs=pl.BlockSpec(
            (blocks, halves, half, PAIRS),
            (lambda b: (0, 0, 0, 0))
            if steps == 1
            else (lambda b: (b % (steps // 2), b // (steps // 2), 0, 0)),
        ),
        out_shape=jax.ShapeDtypeStruct((groups, 2, half, PAIRS), jnp.float32),
        scratch_shapes=[
            pltpu.VMEM((paths, LANES), jnp.float32),
            pltpu.VMEM((MATS, paths, LANES), jnp.bfloat16),
            pltpu.VMEM((STEPS, sets), jnp.float32),
            pltpu.VMEM((LANES, sets), jnp.float32),
        ],
        compiler_params=pltpu.CompilerParams(vmem_limit_bytes=32 * 1024 * 1024),
        name="pricing",
    )(in_hbm(params), in_hbm(increments))


def in_hbm(array):
    return pltpu.with_memory_space_constraint(array, pltpu.HBM)


def dot(left, right):
    return jnp.dot(left, right, preferred_element_type=jnp.float32)


def dot_rows(left, right):
    return lax.dot_general(
        left, right, (((1,), (1,)), ((), ())), preferred_element_type=jnp.float32
    )


def one_hot(t, sets):
    row = t * ROW_TILE + lax.broadcasted_iota(jnp.int32, (1, ROW_TILE), 1)
    group_set = ((row.astype(jnp.float32) + 0.5) * (1.0 / PAIRS)).astype(jnp.int32)
    pair = row - PAIRS * group_set
    code = lax.broadcasted_iota(jnp.int32, (LANES, ROW_TILE), 0)
    hot = jnp.where((code == pair) | (code == group_set + PAIRS), 1.0, 0.0)
    return hot.astype(jnp.bfloat16), group_set


def feature_table(params_ref, group, sets):
    set_count = params_ref.shape[1]
    lane = lax.broadcasted_iota(jnp.int32, (1, LANES), 1)
    maturity = ((lane.astype(jnp.float32) + 0.5) * (1.0 / STRIKES)).astype(jnp.int32)
    offset = (lane - STRIKES * maturity).astype(jnp.float32) - (STRIKES - 1) / 2.0
    spread = jnp.zeros((1, LANES), jnp.float32)
    for m in range(MATS):
        spread = jnp.where(maturity == m, float(np.sqrt(TENORS)[m]), spread)
    strikes = jnp.where(lane < PAIRS, 4.0 * (0.05 * offset * spread), 0.0)
    tenors = jnp.where(lane < PAIRS, (maturity.astype(jnp.float32) + 1.0) / MATS, 0.0)
    ones = jnp.where((lane >= PAIRS) & (lane < PAIRS + sets), 1.0, 0.0)
    wide = jnp.concatenate([params_ref[...], jnp.zeros((4, set_count), jnp.float32)], 0)
    half = sets // 2
    own = jnp.zeros((8, LANES), jnp.float32)
    for high in range(2):
        first = PAIRS + high * half
        start = high * (set_count // 2) + group * half
        moved = pltpu.roll(wide, lax.rem(first + set_count - start, set_count), 1)[:, :LANES]
        own = jnp.where((lane >= first) & (lane < first + half), moved, own)
    scale = [own[0:1] * 4.0, own[1:2], own[2:3], own[3:4] * 20.0]
    pad = jnp.zeros((FEATURE_ROWS - 9, LANES), jnp.float32)
    return jnp.concatenate(scale + [strikes, tenors, ones, ones, ones, pad], 0)


def prepare_kernel(
    sets, owner_ref, params_ref, w_in_hbm, b_in_hbm, w_mid_hbm, win_ref, turned_ref, feat_ref,
    w_in_ref, b_in_ref, w_mid_ref, sems,
):
    copies = [
        pltpu.make_async_copy(source, target, sems.at[i])
        for i, (source, target) in enumerate(
            ((w_in_hbm, w_in_ref), (b_in_hbm, b_in_ref), (w_mid_hbm, w_mid_ref))
        )
    ]
    for copy in copies:
        copy.start()
    devices = params_ref.shape[1] * 4 // sets
    group = (owner_ref[0] // 2) % (devices // 4)
    table = feature_table(params_ref, group, sets).astype(jnp.bfloat16)
    for t in range(feat_ref.shape[1] // ROW_TILE):
        hot, _ = one_hot(t, sets)
        feat = dot(table, hot).astype(jnp.bfloat16)
        feat_ref[:, t * ROW_TILE : (t + 1) * ROW_TILE] = feat
    for copy in copies:
        copy.wait()
    weights_in = w_in_ref[...].astype(jnp.float32)
    bias_in = [piece.astype(jnp.float32) for piece in bf16_pieces(b_in_ref[...])]
    pad = jnp.zeros((FEATURE_ROWS - weights_in.shape[0] - 3, WIDTH), jnp.float32)
    win = (0.5 * jnp.concatenate([weights_in] + bias_in + [pad], 0)).T
    win_ref[...] = win.astype(jnp.bfloat16)
    turned_ref[...] = (0.5 * w_mid_ref[...].astype(jnp.float32)).T.astype(jnp.bfloat16)


def prepare(owner, params, w_in, b_in, w_mid, sets):
    smem = pl.BlockSpec(memory_space=pltpu.SMEM)
    vmem = pl.BlockSpec(memory_space=pltpu.VMEM)
    hbm = pl.BlockSpec(memory_space=pltpu.HBM)
    return pl.pallas_call(
        functools.partial(prepare_kernel, sets),
        in_specs=[smem, vmem] + [hbm] * 3,
        out_specs=[vmem] * 3,
        out_shape=[
            jax.ShapeDtypeStruct((WIDTH, FEATURE_ROWS), jnp.bfloat16),
            jax.ShapeDtypeStruct((WIDTH, WIDTH), jnp.bfloat16),
            jax.ShapeDtypeStruct((FEATURE_ROWS, sets * PAIRS), jnp.bfloat16),
        ],
        scratch_shapes=[
            pltpu.VMEM(w_in.shape, jnp.bfloat16),
            pltpu.VMEM((1, WIDTH), jnp.float32),
            pltpu.VMEM((WIDTH, WIDTH), jnp.bfloat16),
            pltpu.SemaphoreType.DMA((3,)),
        ],
        compiler_params=pltpu.CompilerParams(vmem_limit_bytes=16 * 1024 * 1024),
        name="prepare",
    )(
        owner.reshape(1), in_hbm(params), in_hbm(w_in), in_hbm(b_in.reshape(1, -1)), in_hbm(w_mid)
    )


def forward_kernel(
    owner_ref, b_mid_ref, w_out_ref, win_ref, turned_ref, feat_ref,
    hidden_out, curve_out, mixed_out, pred_out, bias_ref, read_ref,
    even_hidden, odd_hidden, even_mixed, odd_mixed,
):
    bf16 = jnp.bfloat16
    tiles = hidden_out.shape[1] // ROW_TILE
    cols = WIDTH // 4
    owner = owner_ref[0]
    block = 2 * (owner // owner_ref[1]) + owner % 2
    own = pl.ds(pl.multiple_of(block * cols, cols), cols)
    read_ref[...] = jnp.broadcast_to((0.5 * w_out_ref[...].astype(jnp.float32)).T, read_ref.shape)
    readout = jnp.broadcast_to(w_out_ref[...].astype(jnp.float32), (16, WIDTH)).astype(bf16)
    bias_ref[...] = jnp.broadcast_to((0.5 * b_mid_ref[...]).T, bias_ref.shape)

    def span(t):
        return pl.ds(pl.multiple_of(t * ROW_TILE, ROW_TILE), ROW_TILE)

    def step(t, new, old, first=True, second=True, third=True):
        new_hidden, new_mixed = new
        old_hidden, old_mixed = old
        if first:
            feat = feat_ref[:, span(t)]

        def products(c):
            return (
                dot(turned_ref[c, :], old_hidden[...]) if second else None,
                dot(win_ref[c, :], feat) if first else None,
            )

        ahead = products(CHUNKS[0])
        if third:
            predicted = dot(readout, new_mixed[...])
            mixed_out[:, span(t - 2)] = new_mixed[own, :]
        for n, c in enumerate(CHUNKS):
            half_mid, half_in = ahead
            if n + 1 < len(CHUNKS):
                ahead = products(CHUNKS[n + 1])
            if second:
                half_mid = half_mid + bias_ref[c, :]
                wave = jnp.tanh(half_mid)
                turn = half_mid * wave
                old_mixed[c, :] = (half_mid + turn).astype(bf16)
                curve_out[c, span(t - 1)] = (1.0 + wave) * (1.0 + half_mid - turn) * read_ref[c, :]
            if first:
                value = (half_in + half_in * jnp.tanh(half_in)).astype(bf16)
                new_hidden[c, :] = value
                hidden_out[c, span(t)] = value
        if third:
            pred_out[0:1, span(t - 2)] = predicted[0:1]

    even, odd = (even_hidden, even_mixed), (odd_hidden, odd_mixed)
    step(0, even, odd, second=False, third=False)
    step(1, odd, even, third=False)

    def two_steps(u, carry):
        step(2 * u + 2, even, odd)
        step(2 * u + 3, odd, even)
        return carry

    lax.fori_loop(0, (tiles - 2) // 2, two_steps, 0)
    buffers = [even, odd]
    for t in range(2 + (tiles - 2) // 2 * 2, tiles + 2):
        step(t, buffers[t % 2], buffers[1 - t % 2], first=t < tiles, second=t <= tiles)


def forward(place, b_mid, w_out, win, turned, feat):
    rows = feat.shape[1]
    cols = WIDTH // 4
    vmem = pl.BlockSpec(memory_space=pltpu.VMEM)
    smem = pl.BlockSpec(memory_space=pltpu.SMEM)
    outs = [
        ((WIDTH, rows), jnp.bfloat16),
        ((WIDTH, rows), jnp.float32),
        ((cols, rows), jnp.bfloat16),
        ((1, rows), jnp.float32),
    ]
    return pl.pallas_call(
        forward_kernel,
        in_specs=[smem] + [vmem] * 5,
        out_specs=[vmem] * len(outs),
        out_shape=[pltpu.VMEM(shape, kind) for shape, kind in outs[:-1]]
        + [jax.ShapeDtypeStruct(*outs[-1])],
        scratch_shapes=[
            pltpu.VMEM((WIDTH, ROW_TILE), jnp.float32),
            pltpu.VMEM((WIDTH, ROW_TILE), jnp.float32),
        ]
        + [pltpu.VMEM((WIDTH, ROW_TILE), jnp.bfloat16)] * 4,
        compiler_params=pltpu.CompilerParams(vmem_limit_bytes=FORWARD_VMEM),
        cost_estimate=pl.CostEstimate(
            flops=2 * rows * WIDTH * (WIDTH + 32), bytes_accessed=4 << 20, transcendentals=0
        ),
        name="forward",
    )(place, in_hbm(b_mid.reshape(1, -1)), w_out.reshape(1, -1), win, turned, feat)


def backward_kernel(
    inv_sets, owner_ref, sums_ref, near_ref, far_ref, both_ref, hidden_ref, curve_ref, mixed_ref, pred_ref, win_ref,
    feat_ref, w_mid_hbm, b_out_ref, keep_a, send_a, keep_b, send_b,
    left_ref, back_ref, slope_ref, even_delta, odd_delta, delta_in_ref, own_delta_ref, bias_ref,
    read_ref, extra_ref, grad_ref, sem,
):
    bf16 = jnp.bfloat16
    sets = sums_ref.shape[0]
    rows = hidden_ref.shape[1]
    groups = 2 * keep_a.shape[0]
    piece_rows = WIDTH // groups
    cols = WIDTH // 4
    owner = owner_ref[0]
    block = 2 * (owner // (2 * groups)) + owner % 2
    own = pl.ds(pl.multiple_of(block * cols, cols), cols)
    fetch = pltpu.make_async_copy(w_mid_hbm.at[own, :], back_ref, sem)
    fetch.start()

    left_ref[...] = jnp.zeros_like(left_ref)
    sums = (sums_ref[...] + near_ref[...]) + (far_ref[...] + both_ref[...])
    for p, piece in enumerate(bf16_pieces(sums)):
        left_ref[p * sets : (p + 1) * sets, :PAIRS] = piece.astype(jnp.float32)
    left = left_ref[...].astype(bf16)
    tiles = [slice(first, first + ROW_TILE) for first in range(0, rows, ROW_TILE)]
    for t, here in enumerate(tiles):
        hot, group_set = one_hot(t, sets)
        looked = dot(left, hot)
        target = looked[:sets] + looked[sets : 2 * sets] + looked[2 * sets :]
        member = lax.broadcasted_iota(jnp.int32, (sets, ROW_TILE), 0)
        target = jnp.sum(jnp.where(member == group_set, target, 0.0), axis=0, keepdims=True)
        slope_ref[0:1, here] = (pred_ref[0:1, here] + b_out_ref[0] - target) * inv_sets
    fetch.wait()
    for t, here in enumerate(tiles):
        delta_ref = (even_delta, odd_delta)[t % 2]
        slope = slope_ref[0:1, here]
        for c in CHUNKS:
            delta_ref[c, :] = (slope * curve_ref[c, here]).astype(bf16)
        backward = dot(back_ref[...], delta_ref[...])
        own_delta = (slope * curve_ref[own, here]).astype(bf16)
        own_delta_ref[:, here] = own_delta
        bias = own_delta.astype(jnp.float32)
        read = mixed_ref[:, here].astype(jnp.float32) * slope
        bias = bias[:, :LANES] + bias[:, LANES:]
        read = read[:, :LANES] + read[:, LANES:]
        bias_ref[...] = bias if t == 0 else bias_ref[...] + bias
        read_ref[...] = read if t == 0 else read_ref[...] + read
        half = dot(win_ref[own, :], feat_ref[:, here])
        wave = jnp.tanh(half)
        curve = (0.5 * (1.0 + wave)) * (1.0 + half * (1.0 - wave))
        delta_in_ref[:, here] = (backward * curve).astype(bf16)

    for c in CHUNKS:
        grad_ref[c, :] = dot_rows(hidden_ref[c, :], own_delta_ref[...])
    extra = [dot_rows(delta_in_ref[...], feat_ref[...]).T[0:7]]
    extra.append(jnp.sum(bias_ref[...].T, axis=0, keepdims=True))
    extra.append(jnp.sum(read_ref[...].T, axis=0, keepdims=True))
    total = jnp.sum(slope_ref[...], axis=1, keepdims=True)
    extra.append(jnp.broadcast_to(total, (1, cols)))
    extra.append(jnp.zeros((6, cols), jnp.float32))
    extra = jnp.concatenate(extra, 0)
    extra_ref[...] = jnp.zeros_like(extra_ref)
    for j in range(4):
        lanes = slice((j % 2) * LANES, (j % 2 + 1) * LANES)
        extra_ref[j] = extra[8 * (j // 2) : 8 * (j // 2) + 8, lanes]
    group = (owner // 2) % groups
    low, top = group % 2, group // (groups // 2)
    for i in range(groups // 2):
        for a_ref, b_ref, flip in ((keep_a, keep_b, 0), (send_a, send_b, 1)):
            j = 2 * i + (low ^ flip)
            piece = pl.ds(pl.multiple_of(j * piece_rows, piece_rows), piece_rows)
            a_ref[i, 0:piece_rows, :] = grad_ref[piece, 0:LANES]
            a_ref[i, piece_rows:, :] = extra_ref[j]
            j = i + (top ^ flip) * (groups // 2)
            piece = pl.ds(pl.multiple_of(j * piece_rows, piece_rows), piece_rows)
            b_ref[i] = grad_ref[piece, LANES:]


def backward(owner, sums, saved, win, feat, w_mid, b_out, inv_sets, groups):
    sets = sums[0].shape[0]
    rows = sets * PAIRS
    cols = WIDTH // 4
    vmem = pl.BlockSpec(memory_space=pltpu.VMEM)
    smem = pl.BlockSpec(memory_space=pltpu.SMEM)
    hbm = pl.BlockSpec(memory_space=pltpu.HBM)
    return pl.pallas_call(
        functools.partial(backward_kernel, inv_sets),
        in_specs=[smem] + [vmem] * 10 + [hbm, smem],
        out_specs=[vmem] * 4,
        out_shape=[
            jax.ShapeDtypeStruct((groups // 2, WIDTH // groups + more, LANES), jnp.float32)
            for more in (8, 8, 0, 0)
        ],
        scratch_shapes=[
            pltpu.VMEM((3 * sets, LANES), jnp.float32),
            pltpu.VMEM((cols, WIDTH), jnp.bfloat16),
            pltpu.VMEM((1, rows), jnp.float32),
            pltpu.VMEM((WIDTH, ROW_TILE), jnp.bfloat16),
            pltpu.VMEM((WIDTH, ROW_TILE), jnp.bfloat16),
            pltpu.VMEM((cols, rows), jnp.bfloat16),
            pltpu.VMEM((cols, rows), jnp.bfloat16),
            pltpu.VMEM((cols, LANES), jnp.float32),
            pltpu.VMEM((cols, LANES), jnp.float32),
            pltpu.VMEM((max(groups, 4), 8, LANES), jnp.float32),
            pltpu.VMEM((WIDTH, cols), jnp.float32),
            pltpu.SemaphoreType.DMA,
        ],
        compiler_params=pltpu.CompilerParams(vmem_limit_bytes=BACKWARD_VMEM),
        name="backward",
    )(owner.reshape(1), *sums, *saved, win, feat, in_hbm(w_mid), b_out)


def scaling_kernel(layout, groups, owner_ref, *refs):
    blocks = refs[: len(layout)]
    w_in_ref, b_in_ref, w_mid_ref, b_mid_ref, w_out_ref, b_out_ref, extra_ref, small_ref = refs[
        len(layout) :
    ]
    piece_rows = WIDTH // groups
    cols = WIDTH // 4
    owner = owner_ref[0]
    parts = []
    for ref, (masks, contents) in zip(blocks, layout):
        for i, mask in enumerate(masks):
            device = owner ^ mask
            index = (device >> 1) & (groups - 1)
            column = 2 * (device // (2 * groups)) + (device & 1)
            start = 0
            for content in contents:
                if content == "extra":
                    extra_ref[index, column] = ref[i, start : start + 8, :]
                    start += 8
                else:
                    parts.append((ref, i, start, index, column, content == "right"))
                    start += piece_rows

    total = jnp.zeros((8, LANES), jnp.float32)
    for ref, i, start, index, column, right in parts:
        part = ref[i, start : start + piece_rows, :]
        total = total + jnp.sum((part * part).reshape(-1, 8, LANES), axis=0)
    for column in range(4):
        for j in range(4):
            first = column * cols + (j % 2) * LANES
            small_ref[8 * (j // 2) : 8 * (j // 2) + 8, first : first + LANES] = extra_ref[j, column]
    small = small_ref[...]
    squares = jnp.sum(small * small, axis=1, keepdims=True)
    bias_out = small_ref[9:10, 0:1]
    last = bias_out * bias_out

    def factor(total, entries):
        return lax.rsqrt(total / entries + EPSILON)

    total = jnp.sum(jnp.sum(total, axis=1, keepdims=True), axis=0, keepdims=True)
    scale_mid = factor(total + squares[7:8], WIDTH * WIDTH + WIDTH)
    scale_in = factor(jnp.sum(squares[0:7], axis=0, keepdims=True), 7 * WIDTH)
    scale_out = factor(squares[8:9] + last, WIDTH + 1)
    w_in_ref[...] = small[0:6] * scale_in
    b_in_ref[...] = small[6:7] * scale_in
    b_mid_ref[...] = small[7:8] * scale_mid
    w_out_ref[...] = small[8:9] * scale_out
    b_out_ref[...] = bias_out * scale_out
    for ref, i, start, index, column, right in parts:
        rows = pl.ds(pl.multiple_of(index * piece_rows, piece_rows), piece_rows)
        first = pl.multiple_of(column * cols + (LANES if right else 0), LANES)
        part = ref[i, start : start + piece_rows, :]
        w_mid_ref[rows, pl.ds(first, LANES)] = part * scale_mid


def scaled(owner, groups, received):
    vmem = pl.BlockSpec(memory_space=pltpu.VMEM)
    shapes = [(6, WIDTH), (1, WIDTH), (WIDTH, WIDTH), (1, WIDTH), (1, WIDTH), (1, 1)]
    layout = [(masks, contents) for _, masks, contents in received]
    return pl.pallas_call(
        functools.partial(scaling_kernel, layout, groups),
        in_specs=[pl.BlockSpec(memory_space=pltpu.SMEM)] + [vmem] * len(received),
        out_specs=[vmem] * 6,
        out_shape=[jax.ShapeDtypeStruct(shape, jnp.float32) for shape in shapes],
        scratch_shapes=[
            pltpu.VMEM((max(groups, 4), 4, 8, LANES), jnp.float32),
            pltpu.VMEM((16, WIDTH), jnp.float32),
        ],
        compiler_params=pltpu.CompilerParams(vmem_limit_bytes=32 * 1024 * 1024),
        name="scaling",
    )(owner.reshape(1), *[array for array, _, _ in received])


def swap(array, bit, devices):
    return lax.ppermute(array, "paths", [(i, i ^ bit) for i in range(devices)])


def pick(array, index):
    return lax.dynamic_index_in_dim(array, index, 0, keepdims=False)


def halved(part, left, bit, group, devices):
    axis = len(left) - 1 - left.index(bit)
    shape = part.shape[1:]
    cube = part.reshape((2,) * len(left) + shape)
    mine = (group >> bit) % 2
    keep = lax.dynamic_index_in_dim(cube, mine, axis, keepdims=False)
    send = lax.dynamic_index_in_dim(cube, 1 - mine, axis, keepdims=False)
    send, keep = send.reshape((-1,) + shape), keep.reshape((-1,) + shape)
    return keep + swap(send, 2 << bit, devices)


def on_device(params, increments, w_in, b_in, w_mid, b_mid, w_out, b_out):
    devices = lax.axis_size("paths")
    top = devices // 2
    groups = devices // 4
    total_paths = increments.shape[2] * devices
    set_count = params.shape[0]
    set_dev = set_count // devices
    owner = lax.axis_index("paths")
    core = owner % 2
    high = owner // top
    group = (owner // 2) % groups
    block = 2 * high + core
    turned = params.T

    sums = payoff_sums(turned, increments, groups).reshape(groups, 4 * set_dev, PAIRS)
    win, weights, feat = prepare(owner, turned, w_in, b_in, w_mid, 4 * set_dev)
    lanes = [[2 * j + c + top * h for j in range(groups)] for h in range(2) for c in range(2)]
    parts = lax.all_to_all(sums, "paths", 0, 0, axis_index_groups=lanes, tiled=True)
    parts, win = lax.optimization_barrier((parts, win))
    sums = jnp.sum(parts, axis=0) / total_paths
    sums = [sums] + [swap(sums, mask, devices) for mask in (1, top, top + 1)]
    prices = sum(pick(part.reshape(4, set_dev, PAIRS), block) for part in sums)

    place = jnp.stack([owner, jnp.int32(top)])
    saved = forward(place, b_mid, w_out, win, weights, feat)
    keep_a, send_a, keep_b, send_b = backward(
        owner, sums, saved, win, feat, w_mid, b_out, 1.0 / set_count, groups
    )

    bits = [bit for bit in range(groups.bit_length() - 1)]
    part_a = keep_a + swap(send_a, 2, devices)
    part_b = keep_b + swap(send_b, top // 2, devices)
    left_a, left_b = bits[1:], bits[:-1]
    while left_a:
        part_a = halved(part_a, left_a, left_a[0], group, devices)
        part_b = halved(part_b, left_b, left_b[0], group, devices)
        left_a, left_b = left_a[1:], left_b[1:]

    own = jnp.concatenate([part_a, part_b], axis=1)
    far = (0, top // 2, top, top + top // 2)
    whole = jnp.concatenate([own] + [swap(own, mask, devices) for mask in far[1:]], axis=0)
    received = [(whole, far, ("left", "extra", "right"))]
    split = part_a.shape[1]
    held_a, held_b = whole[:, :split], whole[:, split:]
    order = [2 << bit for bit in bits[:-1]]
    masks_a = masks_b = far
    for bit_a, bit_b in zip(order, order[1:] + order[:1]):
        came_a, came_b = swap(held_a, bit_a, devices), swap(held_b, bit_b, devices)
        new_a = tuple(mask ^ bit_a for mask in masks_a)
        new_b = tuple(mask ^ bit_b for mask in masks_b)
        received += [(came_a, new_a, ("left", "extra")), (came_b, new_b, ("right",))]
        if bit_a != order[-1]:
            held_a = jnp.concatenate([held_a, came_a], axis=0)
            held_b = jnp.concatenate([held_b, came_b], axis=0)
        masks_a, masks_b = masks_a + new_a, masks_b + new_b
    received += [
        (swap(array, 1, devices), tuple(mask ^ 1 for mask in masks), contents)
        for array, masks, contents in received
    ]
    result = scaled(owner, groups, received)
    direction_w_in, direction_b_in, direction_w_mid, direction_b_mid, direction_w_out, direction_b_out = result
    return (
        prices,
        direction_w_in,
        direction_b_in.reshape(WIDTH),
        direction_w_mid,
        direction_b_mid.reshape(WIDTH),
        direction_w_out.reshape(WIDTH),
        direction_b_out.reshape(1),
    )


def solution(mesh):
    in_specs = (P(), P(None, None, "paths"), P(), P(), P(), P(), P(), P())
    out_specs = (P("paths", None), P(), P(), P(), P(), P(), P())
    return jax.shard_map(
        on_device, mesh=mesh, in_specs=in_specs, out_specs=out_specs, check_vma=False
    )
```

```python
import functools
import math

import jax
import jax.numpy as jnp
import numpy as np
from jax import lax
from jax.experimental import pallas as pl
from jax.experimental.pallas import tpu as pltpu
from jax.sharding import PartitionSpec as P

STEPS = 64
MATS = 8
STRIKES = 11
PAIRS = 88
WIDTH = 1024
LANES = 128
FEATURE_ROWS = 16
ROW_TILE = 256
FORWARD_VMEM = 24 * 1024 * 1024
BACKWARD_VMEM = 24 * 1024 * 1024
CHUNK = 256
CHUNKS = [slice(start, start + CHUNK) for start in range(0, WIDTH, CHUNK)]
EPSILON = 1e-06


TENORS = (np.arange(MATS, dtype=np.float32) + np.float32(1.0)) / np.float32(MATS)
OFFSETS = np.arange(STRIKES, dtype=np.float32) - np.float32((STRIKES - 1) / 2.0)
LOG_STRIKE = np.float32(0.05) * OFFSETS[None, :] * np.sqrt(TENORS)[:, None]
SET_BLOCK = 256
LOG2E = 1.4426950408889634


def bf16_pieces(value):
    high = value.astype(jnp.bfloat16)
    rest = value - high.astype(jnp.float32)
    mid = rest.astype(jnp.bfloat16)
    low = (rest - mid.astype(jnp.float32)).astype(jnp.bfloat16)
    return high, mid, low


def pricing_kernel(params_ref, inc_ref, out_ref, lags_ref, noise_ref, comp_ref, pay_ref):
    sets = params_ref.shape[1]
    paths = inc_ref.shape[2]
    hurst = params_ref[0:1, :]
    vol_of_vol = params_ref[1:2, :]
    correl = params_ref[2:3, :]
    forward_var = params_ref[3:4, :]
    delta_t = 1.0 / STEPS

    lag = (LANES - lax.broadcasted_iota(jnp.int32, (LANES, 1), 0)).astype(jnp.float32)
    exponent = hurst + 0.5
    here = jnp.exp2(exponent * jnp.log2(lag))
    before = jnp.exp2(exponent * jnp.log2(jnp.maximum(lag - 1.0, 1.0)))
    before = jnp.where(lag > 1.5, before, 0.0)
    front = jnp.sqrt(2.0 * hurst) * jnp.exp2(hurst * math.log2(delta_t)) / exponent
    weights = jnp.where(lag < STEPS - 0.5, (here - before) * front, 0.0).astype(jnp.bfloat16)

    half_scale = vol_of_vol * (0.5 * LOG2E)
    step = lax.broadcasted_iota(jnp.int32, (STEPS, 1), 0).astype(jnp.float32)
    powers = jnp.exp2(2.0 * hurst * jnp.log2(jnp.maximum(step, 1.0) * delta_t))
    comp_ref[...] = jnp.where(step > 0.5, powers * (0.25 * LOG2E * vol_of_vol * vol_of_vol), 0.0)

    root = jnp.sqrt(forward_var * delta_t)
    back = 2.0 / root
    growth = (0.5 * LOG2E) * forward_var * delta_t
    noise_weights = jnp.concatenate(
        [
            jnp.broadcast_to(piece.astype(jnp.float32), (8, sets))
            for value in (correl * back, jnp.sqrt(1.0 - correl * correl) * back)
            for piece in bf16_pieces(value)
        ]
        + [jnp.zeros((LANES - 48, sets), jnp.float32)],
        axis=0,
    ).astype(jnp.bfloat16)

    first = inc_ref[0].astype(jnp.float32)
    second = inc_ref[1].astype(jnp.float32)
    lags_ref[...] = jnp.concatenate([first, jnp.zeros((LANES - STEPS, paths), jnp.float32)], 0).T
    for m in range(MATS):
        rows = slice(8 * m, 8 * m + 8)
        block = jnp.concatenate(
            [first[rows]] * 3 + [second[rows]] * 3 + [jnp.zeros((LANES - 48, paths), jnp.float32)], 0
        )
        noise_ref[m] = block.T.astype(jnp.bfloat16)
    lane = lax.broadcasted_iota(jnp.int32, (paths, LANES), 1)

    def maturity(m, total):
        noise = noise_ref[m]
        for k in range(8):
            i = 8 * m + k
            window = lags_ref[...] if k == 0 else pltpu.roll(lags_ref[...], LANES - k, 1)
            drive = jnp.dot(
                window.astype(jnp.bfloat16), weights, preferred_element_type=jnp.float32
            )
            picked = jnp.where(lane % 8 == k, noise.astype(jnp.float32), 0.0).astype(jnp.bfloat16)
            shock = jnp.dot(picked, noise_weights, preferred_element_type=jnp.float32)
            root_variance = jnp.exp2(drive * half_scale - comp_ref[pl.ds(i, 1), :])
            total = total + root_variance * (shock - root_variance)
        lags_ref[...] = pltpu.roll(lags_ref[...], LANES - 8, 1)
        spot = jnp.exp2(total * growth)
        tenor = jnp.full((8, sets), 1.0, jnp.float32) * ((m + 1).astype(jnp.float32) / MATS)
        spread = jnp.sqrt(tenor)
        for j in range(STRIKES):
            strike = jnp.exp((0.05 * (j - (STRIKES - 1) / 2.0)) * spread)
            gains = jnp.maximum(spot.reshape(paths // 8, 8, sets), strike[None]).sum(axis=0)
            gains = gains - strike * (paths // 8)
            pay_ref[pl.ds(m * STRIKES + j, 1), :] = jnp.sum(gains, axis=0, keepdims=True)
        return total

    lax.fori_loop(0, MATS, maturity, jnp.zeros((paths, sets), jnp.float32))
    paid = pay_ref[...].T[:, :PAIRS]
    blocks, halves, half = out_ref.shape[:3]
    for h in range(halves):
        rows = paid[h * blocks * half : (h + 1) * blocks * half]
        out_ref[:, h] = rows.reshape(blocks, half, PAIRS)


def payoff_sums(params, increments, groups):
    count = params.shape[1]
    paths = increments.shape[2]
    sets = math.gcd(count, SET_BLOCK)
    steps = count // sets
    half = count // groups // 2
    halves = 2 if steps == 1 else 1
    blocks = sets // half // halves
    return pl.pallas_call(
        pricing_kernel,
        grid=(steps,),
        in_specs=[
            pl.BlockSpec((4, sets), lambda b: (0, b)),
            pl.BlockSpec((2, STEPS, paths), lambda b: (0, 0, 0)),
        ],
        out_specs=pl.BlockSpec(
            (blocks, halves, half, PAIRS),
            (lambda b: (0, 0, 0, 0))
            if steps == 1
            else (lambda b: (b % (steps // 2), b // (steps // 2), 0, 0)),
        ),
        out_shape=jax.ShapeDtypeStruct((groups, 2, half, PAIRS), jnp.float32),
        scratch_shapes=[
            pltpu.VMEM((paths, LANES), jnp.float32),
            pltpu.VMEM((MATS, paths, LANES), jnp.bfloat16),
            pltpu.VMEM((STEPS, sets), jnp.float32),
            pltpu.VMEM((LANES, sets), jnp.float32),
        ],
        compiler_params=pltpu.CompilerParams(vmem_limit_bytes=32 * 1024 * 1024),
        name="pricing",
    )(in_hbm(params), in_hbm(increments))


def in_hbm(array):
    return pltpu.with_memory_space_constraint(array, pltpu.HBM)


def dot(left, right):
    return jnp.dot(left, right, preferred_element_type=jnp.float32)


def dot_rows(left, right):
    return lax.dot_general(
        left, right, (((1,), (1,)), ((), ())), preferred_element_type=jnp.float32
    )


def one_hot(t, sets):
    row = t * ROW_TILE + lax.broadcasted_iota(jnp.int32, (1, ROW_TILE), 1)
    group_set = ((row.astype(jnp.float32) + 0.5) * (1.0 / PAIRS)).astype(jnp.int32)
    pair = row - PAIRS * group_set
    code = lax.broadcasted_iota(jnp.int32, (LANES, ROW_TILE), 0)
    hot = jnp.where((code == pair) | (code == group_set + PAIRS), 1.0, 0.0)
    return hot.astype(jnp.bfloat16), group_set


def feature_table(params_ref, group, sets):
    set_count = params_ref.shape[1]
    lane = lax.broadcasted_iota(jnp.int32, (1, LANES), 1)
    maturity = ((lane.astype(jnp.float32) + 0.5) * (1.0 / STRIKES)).astype(jnp.int32)
    offset = (lane - STRIKES * maturity).astype(jnp.float32) - (STRIKES - 1) / 2.0
    spread = jnp.zeros((1, LANES), jnp.float32)
    for m in range(MATS):
        spread = jnp.where(maturity == m, float(np.sqrt(TENORS)[m]), spread)
    strikes = jnp.where(lane < PAIRS, 4.0 * (0.05 * offset * spread), 0.0)
    tenors = jnp.where(lane < PAIRS, (maturity.astype(jnp.float32) + 1.0) / MATS, 0.0)
    ones = jnp.where((lane >= PAIRS) & (lane < PAIRS + sets), 1.0, 0.0)
    wide = jnp.concatenate([params_ref[...], jnp.zeros((4, set_count), jnp.float32)], 0)
    half = sets // 2
    own = jnp.zeros((8, LANES), jnp.float32)
    for high in range(2):
        first = PAIRS + high * half
        start = high * (set_count // 2) + group * half
        moved = pltpu.roll(wide, lax.rem(first + set_count - start, set_count), 1)[:, :LANES]
        own = jnp.where((lane >= first) & (lane < first + half), moved, own)
    scale = [own[0:1] * 4.0, own[1:2], own[2:3], own[3:4] * 20.0]
    pad = jnp.zeros((FEATURE_ROWS - 9, LANES), jnp.float32)
    return jnp.concatenate(scale + [strikes, tenors, ones, ones, ones, pad], 0)


def prepare_kernel(
    sets, owner_ref, params_ref, w_in_hbm, b_in_hbm, w_mid_hbm, win_ref, turned_ref, feat_ref,
    w_in_ref, b_in_ref, w_mid_ref, sems,
):
    copies = [
        pltpu.make_async_copy(source, target, sems.at[i])
        for i, (source, target) in enumerate(
            ((w_in_hbm, w_in_ref), (b_in_hbm, b_in_ref), (w_mid_hbm, w_mid_ref))
        )
    ]
    for copy in copies:
        copy.start()
    devices = params_ref.shape[1] * 4 // sets
    group = (owner_ref[0] // 2) % (devices // 4)
    table = feature_table(params_ref, group, sets).astype(jnp.bfloat16)
    for t in range(feat_ref.shape[1] // ROW_TILE):
        hot, _ = one_hot(t, sets)
        feat = dot(table, hot).astype(jnp.bfloat16)
        feat_ref[:, t * ROW_TILE : (t + 1) * ROW_TILE] = feat
    for copy in copies:
        copy.wait()
    weights_in = w_in_ref[...].astype(jnp.float32)
    bias_in = [piece.astype(jnp.float32) for piece in bf16_pieces(b_in_ref[...])]
    pad = jnp.zeros((FEATURE_ROWS - weights_in.shape[0] - 3, WIDTH), jnp.float32)
    win = (0.5 * jnp.concatenate([weights_in] + bias_in + [pad], 0)).T
    win_ref[...] = win.astype(jnp.bfloat16)
    turned_ref[...] = (0.5 * w_mid_ref[...].astype(jnp.float32)).T.astype(jnp.bfloat16)


def prepare(owner, params, w_in, b_in, w_mid, sets):
    smem = pl.BlockSpec(memory_space=pltpu.SMEM)
    vmem = pl.BlockSpec(memory_space=pltpu.VMEM)
    hbm = pl.BlockSpec(memory_space=pltpu.HBM)
    return pl.pallas_call(
        functools.partial(prepare_kernel, sets),
        in_specs=[smem, vmem] + [hbm] * 3,
        out_specs=[vmem] * 3,
        out_shape=[
            jax.ShapeDtypeStruct((WIDTH, FEATURE_ROWS), jnp.bfloat16),
            jax.ShapeDtypeStruct((WIDTH, WIDTH), jnp.bfloat16),
            jax.ShapeDtypeStruct((FEATURE_ROWS, sets * PAIRS), jnp.bfloat16),
        ],
        scratch_shapes=[
            pltpu.VMEM(w_in.shape, jnp.bfloat16),
            pltpu.VMEM((1, WIDTH), jnp.float32),
            pltpu.VMEM((WIDTH, WIDTH), jnp.bfloat16),
            pltpu.SemaphoreType.DMA((3,)),
        ],
        compiler_params=pltpu.CompilerParams(vmem_limit_bytes=16 * 1024 * 1024),
        name="prepare",
    )(
        owner.reshape(1), in_hbm(params), in_hbm(w_in), in_hbm(b_in.reshape(1, -1)), in_hbm(w_mid)
    )


def forward_kernel(
    owner_ref, b_mid_ref, w_out_ref, win_ref, turned_ref, feat_ref,
    hidden_out, curve_out, mixed_out, pred_out, bias_ref, read_ref,
    even_hidden, odd_hidden, even_mixed, odd_mixed,
):
    bf16 = jnp.bfloat16
    tiles = hidden_out.shape[1] // ROW_TILE
    cols = WIDTH // 4
    owner = owner_ref[0]
    block = 2 * (owner // owner_ref[1]) + owner % 2
    own = pl.ds(pl.multiple_of(block * cols, cols), cols)
    read_ref[...] = jnp.broadcast_to((0.5 * w_out_ref[...].astype(jnp.float32)).T, read_ref.shape)
    readout = jnp.broadcast_to(w_out_ref[...].astype(jnp.float32), (16, WIDTH)).astype(bf16)
    bias_ref[...] = jnp.broadcast_to((0.5 * b_mid_ref[...]).T, bias_ref.shape)

    def span(t):
        return pl.ds(pl.multiple_of(t * ROW_TILE, ROW_TILE), ROW_TILE)

    def step(t, new, old, first=True, second=True, third=True):
        new_hidden, new_mixed = new
        old_hidden, old_mixed = old
        if first:
            feat = feat_ref[:, span(t)]

        def products(c):
            return (
                dot(turned_ref[c, :], old_hidden[...]) if second else None,
                dot(win_ref[c, :], feat) if first else None,
            )

        ahead = products(CHUNKS[0])
        if third:
            predicted = dot(readout, new_mixed[...])
            mixed_out[:, span(t - 2)] = new_mixed[own, :]
        for n, c in enumerate(CHUNKS):
            half_mid, half_in = ahead
            if n + 1 < len(CHUNKS):
                ahead = products(CHUNKS[n + 1])
            if second:
                half_mid = half_mid + bias_ref[c, :]
                wave = jnp.tanh(half_mid)
                turn = half_mid * wave
                old_mixed[c, :] = (half_mid + turn).astype(bf16)
                curve_out[c, span(t - 1)] = (1.0 + wave) * (1.0 + half_mid - turn) * read_ref[c, :]
            if first:
                value = (half_in + half_in * jnp.tanh(half_in)).astype(bf16)
                new_hidden[c, :] = value
                hidden_out[c, span(t)] = value
        if third:
            pred_out[0:1, span(t - 2)] = predicted[0:1]

    even, odd = (even_hidden, even_mixed), (odd_hidden, odd_mixed)
    step(0, even, odd, second=False, third=False)
    step(1, odd, even, third=False)

    def two_steps(u, carry):
        step(2 * u + 2, even, odd)
        step(2 * u + 3, odd, even)
        return carry

    lax.fori_loop(0, (tiles - 2) // 2, two_steps, 0)
    buffers = [even, odd]
    for t in range(2 + (tiles - 2) // 2 * 2, tiles + 2):
        step(t, buffers[t % 2], buffers[1 - t % 2], first=t < tiles, second=t <= tiles)


def forward(place, b_mid, w_out, win, turned, feat):
    rows = feat.shape[1]
    cols = WIDTH // 4
    vmem = pl.BlockSpec(memory_space=pltpu.VMEM)
    smem = pl.BlockSpec(memory_space=pltpu.SMEM)
    outs = [
        ((WIDTH, rows), jnp.bfloat16),
        ((WIDTH, rows), jnp.float32),
        ((cols, rows), jnp.bfloat16),
        ((1, rows), jnp.float32),
    ]
    return pl.pallas_call(
        forward_kernel,
        in_specs=[smem] + [vmem] * 5,
        out_specs=[vmem] * len(outs),
        out_shape=[pltpu.VMEM(shape, kind) for shape, kind in outs[:-1]]
        + [jax.ShapeDtypeStruct(*outs[-1])],
        scratch_shapes=[
            pltpu.VMEM((WIDTH, ROW_TILE), jnp.float32),
            pltpu.VMEM((WIDTH, ROW_TILE), jnp.float32),
        ]
        + [pltpu.VMEM((WIDTH, ROW_TILE), jnp.bfloat16)] * 4,
        compiler_params=pltpu.CompilerParams(vmem_limit_bytes=FORWARD_VMEM),
        cost_estimate=pl.CostEstimate(
            flops=2 * rows * WIDTH * (WIDTH + 32), bytes_accessed=4 << 20, transcendentals=0
        ),
        name="forward",
    )(place, in_hbm(b_mid.reshape(1, -1)), w_out.reshape(1, -1), win, turned, feat)


def backward_kernel(
    inv_sets, owner_ref, sums_ref, near_ref, far_ref, both_ref, hidden_ref, curve_ref, mixed_ref, pred_ref, win_ref,
    feat_ref, w_mid_hbm, b_out_ref, keep_a, send_a, keep_b, send_b, prices_ref,
    left_ref, back_ref, slope_ref, even_delta, odd_delta, delta_in_ref, own_delta_ref, bias_ref,
    read_ref, extra_ref, grad_ref, sem,
):
    bf16 = jnp.bfloat16
    sets = sums_ref.shape[0]
    rows = hidden_ref.shape[1]
    groups = 2 * keep_a.shape[0]
    piece_rows = WIDTH // groups
    cols = WIDTH // 4
    owner = owner_ref[0]
    block = 2 * (owner // (2 * groups)) + owner % 2
    own = pl.ds(pl.multiple_of(block * cols, cols), cols)
    fetch = pltpu.make_async_copy(w_mid_hbm.at[own, :], back_ref, sem)
    fetch.start()

    left_ref[...] = jnp.zeros_like(left_ref)
    sums = (sums_ref[...] + near_ref[...]) + (far_ref[...] + both_ref[...])
    set_dev = sets // 4
    prices = sums[:set_dev]
    for b in range(1, 4):
        prices = jnp.where(block == b, sums[b * set_dev : (b + 1) * set_dev], prices)
    prices_ref[...] = prices
    for p, piece in enumerate(bf16_pieces(sums)):
        left_ref[p * sets : (p + 1) * sets, :PAIRS] = piece.astype(jnp.float32)
    left = left_ref[...].astype(bf16)
    tiles = [slice(first, first + ROW_TILE) for first in range(0, rows, ROW_TILE)]
    for t, here in enumerate(tiles):
        hot, group_set = one_hot(t, sets)
        looked = dot(left, hot)
        target = looked[:sets] + looked[sets : 2 * sets] + looked[2 * sets :]
        member = lax.broadcasted_iota(jnp.int32, (sets, ROW_TILE), 0)
        target = jnp.sum(jnp.where(member == group_set, target, 0.0), axis=0, keepdims=True)
        slope_ref[0:1, here] = (pred_ref[0:1, here] + b_out_ref[0] - target) * inv_sets
    fetch.wait()
    for t, here in enumerate(tiles):
        delta_ref = (even_delta, odd_delta)[t % 2]
        slope = slope_ref[0:1, here]
        for c in CHUNKS:
            delta_ref[c, :] = (slope * curve_ref[c, here]).astype(bf16)
        backward = dot(back_ref[...], delta_ref[...])
        own_delta = (slope * curve_ref[own, here]).astype(bf16)
        own_delta_ref[:, here] = own_delta
        bias = own_delta.astype(jnp.float32)
        read = mixed_ref[:, here].astype(jnp.float32) * slope
        bias = bias[:, :LANES] + bias[:, LANES:]
        read = read[:, :LANES] + read[:, LANES:]
        bias_ref[...] = bias if t == 0 else bias_ref[...] + bias
        read_ref[...] = read if t == 0 else read_ref[...] + read
        half = dot(win_ref[own, :], feat_ref[:, here])
        wave = jnp.tanh(half)
        curve = (0.5 * (1.0 + wave)) * (1.0 + half * (1.0 - wave))
        delta_in_ref[:, here] = (backward * curve).astype(bf16)

    for c in CHUNKS:
        grad_ref[c, :] = dot_rows(hidden_ref[c, :], own_delta_ref[...])
    extra = [dot_rows(delta_in_ref[...], feat_ref[...]).T[0:7]]
    extra.append(jnp.sum(bias_ref[...].T, axis=0, keepdims=True))
    extra.append(jnp.sum(read_ref[...].T, axis=0, keepdims=True))
    total = jnp.sum(slope_ref[...], axis=1, keepdims=True)
    extra.append(jnp.broadcast_to(total, (1, cols)))
    extra.append(jnp.zeros((6, cols), jnp.float32))
    extra = jnp.concatenate(extra, 0)
    extra_ref[...] = jnp.zeros_like(extra_ref)
    for j in range(4):
        lanes = slice((j % 2) * LANES, (j % 2 + 1) * LANES)
        extra_ref[j] = extra[8 * (j // 2) : 8 * (j // 2) + 8, lanes]
    group = (owner // 2) % groups
    low, top = group % 2, group // (groups // 2)
    for i in range(groups // 2):
        for a_ref, b_ref, flip in ((keep_a, keep_b, 0), (send_a, send_b, 1)):
            j = 2 * i + (low ^ flip)
            piece = pl.ds(pl.multiple_of(j * piece_rows, piece_rows), piece_rows)
            a_ref[i, 0:piece_rows, :] = grad_ref[piece, 0:LANES]
            a_ref[i, piece_rows:, :] = extra_ref[j]
            j = i + (top ^ flip) * (groups // 2)
            piece = pl.ds(pl.multiple_of(j * piece_rows, piece_rows), piece_rows)
            b_ref[i] = grad_ref[piece, LANES:]


def backward(owner, sums, saved, win, feat, w_mid, b_out, inv_sets, groups):
    sets = sums[0].shape[0]
    rows = sets * PAIRS
    cols = WIDTH // 4
    vmem = pl.BlockSpec(memory_space=pltpu.VMEM)
    smem = pl.BlockSpec(memory_space=pltpu.SMEM)
    hbm = pl.BlockSpec(memory_space=pltpu.HBM)
    return pl.pallas_call(
        functools.partial(backward_kernel, inv_sets),
        in_specs=[smem] + [vmem] * 10 + [hbm, smem],
        out_specs=[vmem] * 5,
        out_shape=[
            jax.ShapeDtypeStruct((groups // 2, WIDTH // groups + more, LANES), jnp.float32)
            for more in (8, 8, 0, 0)
        ]
        + [jax.ShapeDtypeStruct((sets // 4, PAIRS), jnp.float32)],
        scratch_shapes=[
            pltpu.VMEM((3 * sets, LANES), jnp.float32),
            pltpu.VMEM((cols, WIDTH), jnp.bfloat16),
            pltpu.VMEM((1, rows), jnp.float32),
            pltpu.VMEM((WIDTH, ROW_TILE), jnp.bfloat16),
            pltpu.VMEM((WIDTH, ROW_TILE), jnp.bfloat16),
            pltpu.VMEM((cols, rows), jnp.bfloat16),
            pltpu.VMEM((cols, rows), jnp.bfloat16),
            pltpu.VMEM((cols, LANES), jnp.float32),
            pltpu.VMEM((cols, LANES), jnp.float32),
            pltpu.VMEM((max(groups, 4), 8, LANES), jnp.float32),
            pltpu.VMEM((WIDTH, cols), jnp.float32),
            pltpu.SemaphoreType.DMA,
        ],
        compiler_params=pltpu.CompilerParams(vmem_limit_bytes=BACKWARD_VMEM),
        name="backward",
    )(owner.reshape(1), *sums, *saved, win, feat, in_hbm(w_mid), b_out)


def scaling_kernel(layout, groups, owner_ref, *refs):
    blocks = refs[: len(layout)]
    w_in_ref, b_in_ref, w_mid_ref, b_mid_ref, w_out_ref, b_out_ref, extra_ref, small_ref = refs[
        len(layout) :
    ]
    piece_rows = WIDTH // groups
    cols = WIDTH // 4
    owner = owner_ref[0]
    parts = []
    for ref, (masks, contents) in zip(blocks, layout):
        for i, mask in enumerate(masks):
            device = owner ^ mask
            index = (device >> 1) & (groups - 1)
            column = 2 * (device // (2 * groups)) + (device & 1)
            start = 0
            for content in contents:
                if content == "extra":
                    extra_ref[index, column] = ref[i, start : start + 8, :]
                    start += 8
                else:
                    parts.append((ref, i, start, index, column, content == "right"))
                    start += piece_rows

    total = jnp.zeros((8, LANES), jnp.float32)
    for ref, i, start, index, column, right in parts:
        part = ref[i, start : start + piece_rows, :]
        total = total + jnp.sum((part * part).reshape(-1, 8, LANES), axis=0)
    for column in range(4):
        for j in range(4):
            first = column * cols + (j % 2) * LANES
            small_ref[8 * (j // 2) : 8 * (j // 2) + 8, first : first + LANES] = extra_ref[j, column]
    small = small_ref[...]
    squares = jnp.sum(small * small, axis=1, keepdims=True)
    bias_out = small_ref[9:10, 0:1]
    last = bias_out * bias_out

    def factor(total, entries):
        return lax.rsqrt(total / entries + EPSILON)

    total = jnp.sum(jnp.sum(total, axis=1, keepdims=True), axis=0, keepdims=True)
    scale_mid = factor(total + squares[7:8], WIDTH * WIDTH + WIDTH)
    scale_in = factor(jnp.sum(squares[0:7], axis=0, keepdims=True), 7 * WIDTH)
    scale_out = factor(squares[8:9] + last, WIDTH + 1)
    w_in_ref[...] = small[0:6] * scale_in
    b_in_ref[...] = small[6:7] * scale_in
    b_mid_ref[...] = small[7:8] * scale_mid
    w_out_ref[...] = small[8:9] * scale_out
    b_out_ref[...] = bias_out * scale_out
    for ref, i, start, index, column, right in parts:
        rows = pl.ds(pl.multiple_of(index * piece_rows, piece_rows), piece_rows)
        first = pl.multiple_of(column * cols + (LANES if right else 0), LANES)
        part = ref[i, start : start + piece_rows, :]
        w_mid_ref[rows, pl.ds(first, LANES)] = part * scale_mid


def scaled(owner, groups, received):
    vmem = pl.BlockSpec(memory_space=pltpu.VMEM)
    shapes = [(6, WIDTH), (1, WIDTH), (WIDTH, WIDTH), (1, WIDTH), (1, WIDTH), (1, 1)]
    layout = [(masks, contents) for _, masks, contents in received]
    return pl.pallas_call(
        functools.partial(scaling_kernel, layout, groups),
        in_specs=[pl.BlockSpec(memory_space=pltpu.SMEM)] + [vmem] * len(received),
        out_specs=[vmem] * 6,
        out_shape=[jax.ShapeDtypeStruct(shape, jnp.float32) for shape in shapes],
        scratch_shapes=[
            pltpu.VMEM((max(groups, 4), 4, 8, LANES), jnp.float32),
            pltpu.VMEM((16, WIDTH), jnp.float32),
        ],
        compiler_params=pltpu.CompilerParams(vmem_limit_bytes=32 * 1024 * 1024),
        name="scaling",
    )(owner.reshape(1), *[array for array, _, _ in received])


def swap(array, bit, devices):
    return lax.ppermute(array, "paths", [(i, i ^ bit) for i in range(devices)])


def pick(array, index):
    return lax.dynamic_index_in_dim(array, index, 0, keepdims=False)


def halved(part, left, bit, group, devices):
    axis = len(left) - 1 - left.index(bit)
    shape = part.shape[1:]
    cube = part.reshape((2,) * len(left) + shape)
    mine = (group >> bit) % 2
    keep = lax.dynamic_index_in_dim(cube, mine, axis, keepdims=False)
    send = lax.dynamic_index_in_dim(cube, 1 - mine, axis, keepdims=False)
    send, keep = send.reshape((-1,) + shape), keep.reshape((-1,) + shape)
    return keep + swap(send, 2 << bit, devices)


def on_device(params, increments, w_in, b_in, w_mid, b_mid, w_out, b_out):
    devices = lax.axis_size("paths")
    top = devices // 2
    groups = devices // 4
    total_paths = increments.shape[2] * devices
    set_count = params.shape[0]
    set_dev = set_count // devices
    owner = lax.axis_index("paths")
    core = owner % 2
    high = owner // top
    group = (owner // 2) % groups
    block = 2 * high + core
    turned = params.T

    sums = payoff_sums(turned, increments, groups).reshape(groups, 4 * set_dev, PAIRS)
    win, weights, feat = prepare(owner, turned, w_in, b_in, w_mid, 4 * set_dev)
    lanes = [[2 * j + c + top * h for j in range(groups)] for h in range(2) for c in range(2)]
    parts = lax.all_to_all(sums, "paths", 0, 0, axis_index_groups=lanes, tiled=True)
    parts, win = lax.optimization_barrier((parts, win))
    sums = jnp.sum(parts, axis=0) / total_paths
    sums = [sums] + [swap(sums, mask, devices) for mask in (1, top, top + 1)]

    place = jnp.stack([owner, jnp.int32(top)])
    saved = forward(place, b_mid, w_out, win, weights, feat)
    keep_a, send_a, keep_b, send_b, prices = backward(
        owner, sums, saved, win, feat, w_mid, b_out, 1.0 / set_count, groups
    )

    bits = [bit for bit in range(groups.bit_length() - 1)]
    part_a = keep_a + swap(send_a, 2, devices)
    part_b = keep_b + swap(send_b, top // 2, devices)
    left_a, left_b = bits[1:], bits[:-1]
    while left_a:
        part_a = halved(part_a, left_a, left_a[0], group, devices)
        part_b = halved(part_b, left_b, left_b[0], group, devices)
        left_a, left_b = left_a[1:], left_b[1:]

    own = jnp.concatenate([part_a, part_b], axis=1)
    far = (0, top // 2, top, top + top // 2)
    whole = jnp.concatenate([own] + [swap(own, mask, devices) for mask in far[1:]], axis=0)
    received = [(whole, far, ("left", "extra", "right"))]
    split = part_a.shape[1]
    held_a, held_b = whole[:, :split], whole[:, split:]
    order = [2 << bit for bit in bits[:-1]]
    masks_a = masks_b = far
    for bit_a, bit_b in zip(order, order[1:] + order[:1]):
        came_a, came_b = swap(held_a, bit_a, devices), swap(held_b, bit_b, devices)
        new_a = tuple(mask ^ bit_a for mask in masks_a)
        new_b = tuple(mask ^ bit_b for mask in masks_b)
        if bit_a == order[-1]:
            near = [swap(array, 1, devices) for array, _, _ in received]
            came_a, came_b, *near = lax.optimization_barrier((came_a, came_b, *near))
        received += [(came_a, new_a, ("left", "extra")), (came_b, new_b, ("right",))]
        if bit_a != order[-1]:
            held_a = jnp.concatenate([held_a, came_a], axis=0)
            held_b = jnp.concatenate([held_b, came_b], axis=0)
        masks_a, masks_b = masks_a + new_a, masks_b + new_b
    near += [swap(array, 1, devices) for array, _, _ in received[len(near) :]]
    received += [
        (array, tuple(mask ^ 1 for mask in masks), contents)
        for array, (_, masks, contents) in zip(near, received)
    ]
    result = scaled(owner, groups, received)
    direction_w_in, direction_b_in, direction_w_mid, direction_b_mid, direction_w_out, direction_b_out = result
    return (
        prices,
        direction_w_in,
        direction_b_in.reshape(WIDTH),
        direction_w_mid,
        direction_b_mid.reshape(WIDTH),
        direction_w_out.reshape(WIDTH),
        direction_b_out.reshape(1),
    )


def solution(mesh):
    in_specs = (P(), P(None, None, "paths"), P(), P(), P(), P(), P(), P())
    out_specs = (P("paths", None), P(), P(), P(), P(), P(), P())
    return jax.shard_map(
        on_device, mesh=mesh, in_specs=in_specs, out_specs=out_specs, check_vma=False
    )
```

```python
import functools
import math

import jax
import jax.numpy as jnp
import numpy as np
from jax import lax
from jax.experimental import pallas as pl
from jax.experimental.pallas import tpu as pltpu
from jax.sharding import PartitionSpec as P

STEPS = 64
MATS = 8
STRIKES = 11
PAIRS = 88
WIDTH = 1024
LANES = 128
FEATURE_ROWS = 16
ROW_TILE = 256
FORWARD_VMEM = 24 * 1024 * 1024
BACKWARD_VMEM = 24 * 1024 * 1024
CHUNK = 256
CHUNKS = [slice(start, start + CHUNK) for start in range(0, WIDTH, CHUNK)]
EPSILON = 1e-06


TENORS = (np.arange(MATS, dtype=np.float32) + np.float32(1.0)) / np.float32(MATS)
OFFSETS = np.arange(STRIKES, dtype=np.float32) - np.float32((STRIKES - 1) / 2.0)
LOG_STRIKE = np.float32(0.05) * OFFSETS[None, :] * np.sqrt(TENORS)[:, None]
SET_BLOCK = 256
LOG2E = 1.4426950408889634


def bf16_pieces(value):
    high = value.astype(jnp.bfloat16)
    rest = value - high.astype(jnp.float32)
    mid = rest.astype(jnp.bfloat16)
    low = (rest - mid.astype(jnp.float32)).astype(jnp.bfloat16)
    return high, mid, low


def pricing_kernel(params_ref, inc_ref, out_ref, lags_ref, noise_ref, comp_ref, pay_ref):
    sets = params_ref.shape[1]
    paths = inc_ref.shape[2]
    hurst = params_ref[0:1, :]
    vol_of_vol = params_ref[1:2, :]
    correl = params_ref[2:3, :]
    forward_var = params_ref[3:4, :]
    delta_t = 1.0 / STEPS

    lag = (LANES - lax.broadcasted_iota(jnp.int32, (LANES, 1), 0)).astype(jnp.float32)
    exponent = hurst + 0.5
    here = jnp.exp2(exponent * jnp.log2(lag))
    before = jnp.exp2(exponent * jnp.log2(jnp.maximum(lag - 1.0, 1.0)))
    before = jnp.where(lag > 1.5, before, 0.0)
    front = jnp.sqrt(2.0 * hurst) * jnp.exp2(hurst * math.log2(delta_t)) / exponent
    weights = jnp.where(lag < STEPS - 0.5, (here - before) * front, 0.0).astype(jnp.bfloat16)

    half_scale = vol_of_vol * (0.5 * LOG2E)
    step = lax.broadcasted_iota(jnp.int32, (STEPS, 1), 0).astype(jnp.float32)
    powers = jnp.exp2(2.0 * hurst * jnp.log2(jnp.maximum(step, 1.0) * delta_t))
    comp_ref[...] = jnp.where(step > 0.5, powers * (0.25 * LOG2E * vol_of_vol * vol_of_vol), 0.0)

    root = jnp.sqrt(forward_var * delta_t)
    back = 2.0 / root
    growth = (0.5 * LOG2E) * forward_var * delta_t
    noise_weights = jnp.concatenate(
        [
            jnp.broadcast_to(piece.astype(jnp.float32), (8, sets))
            for value in (correl * back, jnp.sqrt(1.0 - correl * correl) * back)
            for piece in bf16_pieces(value)
        ]
        + [jnp.zeros((LANES - 48, sets), jnp.float32)],
        axis=0,
    ).astype(jnp.bfloat16)

    first = inc_ref[0].astype(jnp.float32)
    second = inc_ref[1].astype(jnp.float32)
    lags_ref[...] = jnp.concatenate([first, jnp.zeros((LANES - STEPS, paths), jnp.float32)], 0).T
    for m in range(MATS):
        rows = slice(8 * m, 8 * m + 8)
        block = jnp.concatenate(
            [first[rows]] * 3 + [second[rows]] * 3 + [jnp.zeros((LANES - 48, paths), jnp.float32)], 0
        )
        noise_ref[m] = block.T.astype(jnp.bfloat16)
    lane = lax.broadcasted_iota(jnp.int32, (paths, LANES), 1)

    def maturity(m, total):
        noise = noise_ref[m]
        for k in range(8):
            i = 8 * m + k
            window = lags_ref[...] if k == 0 else pltpu.roll(lags_ref[...], LANES - k, 1)
            drive = jnp.dot(
                window.astype(jnp.bfloat16), weights, preferred_element_type=jnp.float32
            )
            picked = jnp.where(lane % 8 == k, noise.astype(jnp.float32), 0.0).astype(jnp.bfloat16)
            shock = jnp.dot(picked, noise_weights, preferred_element_type=jnp.float32)
            root_variance = jnp.exp2(drive * half_scale - comp_ref[pl.ds(i, 1), :])
            total = total + root_variance * (shock - root_variance)
        lags_ref[...] = pltpu.roll(lags_ref[...], LANES - 8, 1)
        spot = jnp.exp2(total * growth)
        tenor = jnp.full((8, sets), 1.0, jnp.float32) * ((m + 1).astype(jnp.float32) / MATS)
        spread = jnp.sqrt(tenor)
        for j in range(STRIKES):
            strike = jnp.exp((0.05 * (j - (STRIKES - 1) / 2.0)) * spread)
            gains = jnp.maximum(spot.reshape(paths // 8, 8, sets), strike[None]).sum(axis=0)
            gains = gains - strike * (paths // 8)
            pay_ref[pl.ds(m * STRIKES + j, 1), :] = jnp.sum(gains, axis=0, keepdims=True)
        return total

    lax.fori_loop(0, MATS, maturity, jnp.zeros((paths, sets), jnp.float32))
    paid = pay_ref[...].T[:, :PAIRS]
    blocks, halves, half = out_ref.shape[:3]
    for h in range(halves):
        rows = paid[h * blocks * half : (h + 1) * blocks * half]
        out_ref[:, h] = rows.reshape(blocks, half, PAIRS)


def payoff_sums(params, increments, groups):
    count = params.shape[1]
    paths = increments.shape[2]
    sets = math.gcd(count, SET_BLOCK)
    steps = count // sets
    half = count // groups // 2
    halves = 2 if steps == 1 else 1
    blocks = sets // half // halves
    return pl.pallas_call(
        pricing_kernel,
        grid=(steps,),
        in_specs=[
            pl.BlockSpec((4, sets), lambda b: (0, b)),
            pl.BlockSpec((2, STEPS, paths), lambda b: (0, 0, 0)),
        ],
        out_specs=pl.BlockSpec(
            (blocks, halves, half, PAIRS),
            (lambda b: (0, 0, 0, 0))
            if steps == 1
            else (lambda b: (b % (steps // 2), b // (steps // 2), 0, 0)),
        ),
        out_shape=jax.ShapeDtypeStruct((groups, 2, half, PAIRS), jnp.float32),
        scratch_shapes=[
            pltpu.VMEM((paths, LANES), jnp.float32),
            pltpu.VMEM((MATS, paths, LANES), jnp.bfloat16),
            pltpu.VMEM((STEPS, sets), jnp.float32),
            pltpu.VMEM((LANES, sets), jnp.float32),
        ],
        compiler_params=pltpu.CompilerParams(vmem_limit_bytes=32 * 1024 * 1024),
        name="pricing",
    )(in_hbm(params), in_hbm(increments))


def in_hbm(array):
    return pltpu.with_memory_space_constraint(array, pltpu.HBM)


def dot(left, right):
    return jnp.dot(left, right, preferred_element_type=jnp.float32)


def dot_rows(left, right):
    return lax.dot_general(
        left, right, (((1,), (1,)), ((), ())), preferred_element_type=jnp.float32
    )


def one_hot(t, sets):
    row = t * ROW_TILE + lax.broadcasted_iota(jnp.int32, (1, ROW_TILE), 1)
    group_set = ((row.astype(jnp.float32) + 0.5) * (1.0 / PAIRS)).astype(jnp.int32)
    pair = row - PAIRS * group_set
    code = lax.broadcasted_iota(jnp.int32, (LANES, ROW_TILE), 0)
    hot = jnp.where((code == pair) | (code == group_set + PAIRS), 1.0, 0.0)
    return hot.astype(jnp.bfloat16), group_set


def feature_table(params_ref, group, sets):
    set_count = params_ref.shape[1]
    lane = lax.broadcasted_iota(jnp.int32, (1, LANES), 1)
    maturity = ((lane.astype(jnp.float32) + 0.5) * (1.0 / STRIKES)).astype(jnp.int32)
    offset = (lane - STRIKES * maturity).astype(jnp.float32) - (STRIKES - 1) / 2.0
    spread = jnp.zeros((1, LANES), jnp.float32)
    for m in range(MATS):
        spread = jnp.where(maturity == m, float(np.sqrt(TENORS)[m]), spread)
    strikes = jnp.where(lane < PAIRS, 4.0 * (0.05 * offset * spread), 0.0)
    tenors = jnp.where(lane < PAIRS, (maturity.astype(jnp.float32) + 1.0) / MATS, 0.0)
    ones = jnp.where((lane >= PAIRS) & (lane < PAIRS + sets), 1.0, 0.0)
    wide = jnp.concatenate([params_ref[...], jnp.zeros((4, set_count), jnp.float32)], 0)
    half = sets // 2
    own = jnp.zeros((8, LANES), jnp.float32)
    for high in range(2):
        first = PAIRS + high * half
        start = high * (set_count // 2) + group * half
        moved = pltpu.roll(wide, lax.rem(first + set_count - start, set_count), 1)[:, :LANES]
        own = jnp.where((lane >= first) & (lane < first + half), moved, own)
    scale = [own[0:1] * 4.0, own[1:2], own[2:3], own[3:4] * 20.0]
    pad = jnp.zeros((FEATURE_ROWS - 9, LANES), jnp.float32)
    return jnp.concatenate(scale + [strikes, tenors, ones, ones, ones, pad], 0)


def prepare_kernel(
    sets, owner_ref, params_ref, w_in_hbm, b_in_hbm, w_mid_hbm, win_ref, turned_ref, feat_ref,
    w_in_ref, b_in_ref, w_mid_ref, sems,
):
    copies = [
        pltpu.make_async_copy(source, target, sems.at[i])
        for i, (source, target) in enumerate(
            ((w_in_hbm, w_in_ref), (b_in_hbm, b_in_ref), (w_mid_hbm, w_mid_ref))
        )
    ]
    for copy in copies:
        copy.start()
    devices = params_ref.shape[1] * 4 // sets
    group = (owner_ref[0] // 2) % (devices // 4)
    table = feature_table(params_ref, group, sets).astype(jnp.bfloat16)
    for t in range(feat_ref.shape[1] // ROW_TILE):
        hot, _ = one_hot(t, sets)
        feat = dot(table, hot).astype(jnp.bfloat16)
        feat_ref[:, t * ROW_TILE : (t + 1) * ROW_TILE] = feat
    for copy in copies:
        copy.wait()
    weights_in = w_in_ref[...].astype(jnp.float32)
    bias_in = [piece.astype(jnp.float32) for piece in bf16_pieces(b_in_ref[...])]
    pad = jnp.zeros((FEATURE_ROWS - weights_in.shape[0] - 3, WIDTH), jnp.float32)
    win = (0.5 * jnp.concatenate([weights_in] + bias_in + [pad], 0)).T
    win_ref[...] = win.astype(jnp.bfloat16)
    turned_ref[...] = (0.5 * w_mid_ref[...].astype(jnp.float32)).T.astype(jnp.bfloat16)


def prepare(owner, params, w_in, b_in, w_mid, sets):
    smem = pl.BlockSpec(memory_space=pltpu.SMEM)
    vmem = pl.BlockSpec(memory_space=pltpu.VMEM)
    hbm = pl.BlockSpec(memory_space=pltpu.HBM)
    return pl.pallas_call(
        functools.partial(prepare_kernel, sets),
        in_specs=[smem, vmem] + [hbm] * 3,
        out_specs=[vmem] * 3,
        out_shape=[
            jax.ShapeDtypeStruct((WIDTH, FEATURE_ROWS), jnp.bfloat16),
            jax.ShapeDtypeStruct((WIDTH, WIDTH), jnp.bfloat16),
            jax.ShapeDtypeStruct((FEATURE_ROWS, sets * PAIRS), jnp.bfloat16),
        ],
        scratch_shapes=[
            pltpu.VMEM(w_in.shape, jnp.bfloat16),
            pltpu.VMEM((1, WIDTH), jnp.float32),
            pltpu.VMEM((WIDTH, WIDTH), jnp.bfloat16),
            pltpu.SemaphoreType.DMA((3,)),
        ],
        compiler_params=pltpu.CompilerParams(vmem_limit_bytes=16 * 1024 * 1024),
        name="prepare",
    )(
        owner.reshape(1), in_hbm(params), in_hbm(w_in), in_hbm(b_in.reshape(1, -1)), in_hbm(w_mid)
    )


def forward_kernel(
    owner_ref, b_mid_ref, w_out_ref, win_ref, turned_ref, feat_ref,
    hidden_out, curve_out, mixed_out, pred_out, bias_ref, read_ref,
    even_hidden, odd_hidden, even_mixed, odd_mixed,
):
    bf16 = jnp.bfloat16
    tiles = hidden_out.shape[1] // ROW_TILE
    cols = WIDTH // 4
    owner = owner_ref[0]
    block = 2 * (owner // owner_ref[1]) + owner % 2
    own = pl.ds(pl.multiple_of(block * cols, cols), cols)
    read_ref[...] = jnp.broadcast_to((0.5 * w_out_ref[...].astype(jnp.float32)).T, read_ref.shape)
    readout = jnp.broadcast_to(w_out_ref[...].astype(jnp.float32), (16, WIDTH)).astype(bf16)
    bias_ref[...] = jnp.broadcast_to((0.5 * b_mid_ref[...]).T, bias_ref.shape)

    def span(t):
        return pl.ds(pl.multiple_of(t * ROW_TILE, ROW_TILE), ROW_TILE)

    def step(t, new, old, first=True, second=True, third=True):
        new_hidden, new_mixed = new
        old_hidden, old_mixed = old
        if first:
            feat = feat_ref[:, span(t)]

        def products(c):
            return (
                dot(turned_ref[c, :], old_hidden[...]) if second else None,
                dot(win_ref[c, :], feat) if first else None,
            )

        ahead = products(CHUNKS[0])
        if third:
            predicted = dot(readout, new_mixed[...])
            mixed_out[:, span(t - 2)] = new_mixed[own, :]
        for n, c in enumerate(CHUNKS):
            half_mid, half_in = ahead
            if n + 1 < len(CHUNKS):
                ahead = products(CHUNKS[n + 1])
            if second:
                half_mid = half_mid + bias_ref[c, :]
                wave = jnp.tanh(half_mid)
                turn = half_mid * wave
                old_mixed[c, :] = (half_mid + turn).astype(bf16)
                curve_out[c, span(t - 1)] = (1.0 + wave) * (1.0 + half_mid - turn) * read_ref[c, :]
            if first:
                value = (half_in + half_in * jnp.tanh(half_in)).astype(bf16)
                new_hidden[c, :] = value
                hidden_out[c, span(t)] = value
        if third:
            pred_out[0:1, span(t - 2)] = predicted[0:1]

    even, odd = (even_hidden, even_mixed), (odd_hidden, odd_mixed)
    step(0, even, odd, second=False, third=False)
    step(1, odd, even, third=False)

    def two_steps(u, carry):
        step(2 * u + 2, even, odd)
        step(2 * u + 3, odd, even)
        return carry

    lax.fori_loop(0, (tiles - 2) // 2, two_steps, 0)
    buffers = [even, odd]
    for t in range(2 + (tiles - 2) // 2 * 2, tiles + 2):
        step(t, buffers[t % 2], buffers[1 - t % 2], first=t < tiles, second=t <= tiles)


def forward(place, b_mid, w_out, win, turned, feat):
    rows = feat.shape[1]
    cols = WIDTH // 4
    vmem = pl.BlockSpec(memory_space=pltpu.VMEM)
    smem = pl.BlockSpec(memory_space=pltpu.SMEM)
    outs = [
        ((WIDTH, rows), jnp.bfloat16),
        ((WIDTH, rows), jnp.float32),
        ((cols, rows), jnp.bfloat16),
        ((1, rows), jnp.float32),
    ]
    return pl.pallas_call(
        forward_kernel,
        in_specs=[smem] + [vmem] * 5,
        out_specs=[vmem] * len(outs),
        out_shape=[pltpu.VMEM(shape, kind) for shape, kind in outs[:-1]]
        + [jax.ShapeDtypeStruct(*outs[-1])],
        scratch_shapes=[
            pltpu.VMEM((WIDTH, ROW_TILE), jnp.float32),
            pltpu.VMEM((WIDTH, ROW_TILE), jnp.float32),
        ]
        + [pltpu.VMEM((WIDTH, ROW_TILE), jnp.bfloat16)] * 4,
        compiler_params=pltpu.CompilerParams(vmem_limit_bytes=FORWARD_VMEM),
        cost_estimate=pl.CostEstimate(
            flops=2 * rows * WIDTH * (WIDTH + 32), bytes_accessed=4 << 20, transcendentals=0
        ),
        name="forward",
    )(place, in_hbm(b_mid.reshape(1, -1)), w_out.reshape(1, -1), win, turned, feat)


def backward_kernel(
    inv_sets, owner_ref, sums_ref, near_ref, far_ref, both_ref, hidden_ref, curve_ref, mixed_ref, pred_ref, win_ref,
    feat_ref, w_mid_hbm, b_out_ref, keep_x, send_x, keep_y, send_y, keep_z, send_z, prices_ref,
    left_ref, back_ref, slope_ref, even_delta, odd_delta, delta_in_ref, own_delta_ref, bias_ref,
    read_ref, pieces_ref, sem,
):
    bf16 = jnp.bfloat16
    sets = sums_ref.shape[0]
    rows = hidden_ref.shape[1]
    groups = pieces_ref.shape[0]
    piece_rows = WIDTH // groups
    cols = WIDTH // 4
    owner = owner_ref[0]
    block = 2 * (owner // (2 * groups)) + owner % 2
    own = pl.ds(pl.multiple_of(block * cols, cols), cols)
    fetch = pltpu.make_async_copy(w_mid_hbm.at[own, :], back_ref, sem)
    fetch.start()

    left_ref[...] = jnp.zeros_like(left_ref)
    sums = (sums_ref[...] + near_ref[...]) + (far_ref[...] + both_ref[...])
    set_dev = sets // 4
    prices = sums[:set_dev]
    for b in range(1, 4):
        prices = jnp.where(block == b, sums[b * set_dev : (b + 1) * set_dev], prices)
    prices_ref[...] = prices
    for p, piece in enumerate(bf16_pieces(sums)):
        left_ref[p * sets : (p + 1) * sets, :PAIRS] = piece.astype(jnp.float32)
    left = left_ref[...].astype(bf16)
    tiles = [slice(first, first + ROW_TILE) for first in range(0, rows, ROW_TILE)]
    for t, here in enumerate(tiles):
        hot, group_set = one_hot(t, sets)
        looked = dot(left, hot)
        target = looked[:sets] + looked[sets : 2 * sets] + looked[2 * sets :]
        member = lax.broadcasted_iota(jnp.int32, (sets, ROW_TILE), 0)
        target = jnp.sum(jnp.where(member == group_set, target, 0.0), axis=0, keepdims=True)
        slope_ref[0:1, here] = (pred_ref[0:1, here] + b_out_ref[0] - target) * inv_sets
    fetch.wait()
    for t, here in enumerate(tiles):
        delta_ref = (even_delta, odd_delta)[t % 2]
        slope = slope_ref[0:1, here]
        for c in CHUNKS:
            delta_ref[c, :] = (slope * curve_ref[c, here]).astype(bf16)
        backward = dot(back_ref[...], delta_ref[...])
        own_delta = (slope * curve_ref[own, here]).astype(bf16)
        own_delta_ref[:, here] = own_delta
        bias = own_delta.astype(jnp.float32)
        read = mixed_ref[:, here].astype(jnp.float32) * slope
        bias = bias[:, :LANES] + bias[:, LANES:]
        read = read[:, :LANES] + read[:, LANES:]
        bias_ref[...] = bias if t == 0 else bias_ref[...] + bias
        read_ref[...] = read if t == 0 else read_ref[...] + read
        half = dot(win_ref[own, :], feat_ref[:, here])
        wave = jnp.tanh(half)
        curve = (0.5 * (1.0 + wave)) * (1.0 + half * (1.0 - wave))
        delta_in_ref[:, here] = (backward * curve).astype(bf16)

    for c in CHUNKS:
        total = dot_rows(hidden_ref[c, :], own_delta_ref[...])
        for first in range(0, CHUNK, piece_rows):
            j = (c.start + first) // piece_rows
            part = total[first : first + piece_rows]
            pieces_ref[j, 0:piece_rows, :] = part[:, :LANES]
            pieces_ref[j, piece_rows + 8 :, :] = part[:, LANES:]
    extra = [dot_rows(delta_in_ref[...], feat_ref[...]).T[0:7]]
    extra.append(jnp.sum(bias_ref[...].T, axis=0, keepdims=True))
    extra.append(jnp.sum(read_ref[...].T, axis=0, keepdims=True))
    total = jnp.sum(slope_ref[...], axis=1, keepdims=True)
    extra.append(jnp.broadcast_to(total, (1, cols)))
    extra.append(jnp.zeros((6, cols), jnp.float32))
    extra = jnp.concatenate(extra, 0)
    for j in range(groups):
        lanes = slice((j % 2) * LANES, (j % 2 + 1) * LANES)
        part = extra[8 * (j // 2) : 8 * (j // 2) + 8, lanes] if j < 4 else jnp.zeros((8, LANES))
        pieces_ref[j, piece_rows : piece_rows + 8, :] = part
    group = (owner // 2) % groups
    cuts = part_cuts(groups)
    for bit, (keep, send) in enumerate(((keep_x, send_x), (keep_y, send_y), (keep_z, send_z))):
        mine = (group // 2**bit) % 2
        for i in range(groups // 2):
            base = (i >> bit << (bit + 1)) + (i & (2**bit - 1))
            keep[i] = pieces_ref[base + mine * 2**bit, cuts[bit] : cuts[bit + 1], :]
            send[i] = pieces_ref[base + (1 - mine) * 2**bit, cuts[bit] : cuts[bit + 1], :]


def part_cuts(groups):
    rows = 2 * (WIDTH // groups) + 8
    third = rows // 24 * 8
    return (0, third, 2 * third, rows)


def backward(owner, sums, saved, win, feat, w_mid, b_out, inv_sets, groups):
    sets = sums[0].shape[0]
    cuts = part_cuts(groups)
    rows = sets * PAIRS
    cols = WIDTH // 4
    vmem = pl.BlockSpec(memory_space=pltpu.VMEM)
    smem = pl.BlockSpec(memory_space=pltpu.SMEM)
    hbm = pl.BlockSpec(memory_space=pltpu.HBM)
    return pl.pallas_call(
        functools.partial(backward_kernel, inv_sets),
        in_specs=[smem] + [vmem] * 10 + [hbm, smem],
        out_specs=[vmem] * 7,
        out_shape=[
            jax.ShapeDtypeStruct((groups // 2, stop - start, LANES), jnp.float32)
            for start, stop in zip(cuts, cuts[1:])
            for _ in range(2)
        ]
        + [jax.ShapeDtypeStruct((sets // 4, PAIRS), jnp.float32)],
        scratch_shapes=[
            pltpu.VMEM((3 * sets, LANES), jnp.float32),
            pltpu.VMEM((cols, WIDTH), jnp.bfloat16),
            pltpu.VMEM((1, rows), jnp.float32),
            pltpu.VMEM((WIDTH, ROW_TILE), jnp.bfloat16),
            pltpu.VMEM((WIDTH, ROW_TILE), jnp.bfloat16),
            pltpu.VMEM((cols, rows), jnp.bfloat16),
            pltpu.VMEM((cols, rows), jnp.bfloat16),
            pltpu.VMEM((cols, LANES), jnp.float32),
            pltpu.VMEM((cols, LANES), jnp.float32),
            pltpu.VMEM((groups, 2 * (WIDTH // groups) + 8, LANES), jnp.float32),
            pltpu.SemaphoreType.DMA,
        ],
        compiler_params=pltpu.CompilerParams(vmem_limit_bytes=BACKWARD_VMEM),
        name="backward",
    )(owner.reshape(1), *sums, *saved, win, feat, in_hbm(w_mid), b_out)


def scaling_kernel(layout, groups, owner_ref, *refs):
    blocks = refs[: len(layout)]
    w_in_ref, b_in_ref, w_mid_ref, b_mid_ref, w_out_ref, b_out_ref, extra_ref, small_ref = refs[
        len(layout) :
    ]
    piece_rows = WIDTH // groups
    cols = WIDTH // 4
    owner = owner_ref[0]
    parts = []
    for ref, (masks, contents) in zip(blocks, layout):
        for i, mask in enumerate(masks):
            device = owner ^ mask
            index = (device >> 1) & (groups - 1)
            column = 2 * (device // (2 * groups)) + (device & 1)
            start = 0
            for content in contents:
                if content == "extra":
                    extra_ref[index, column] = ref[i, start : start + 8, :]
                    start += 8
                else:
                    parts.append((ref, i, start, index, column, content == "right"))
                    start += piece_rows

    total = jnp.zeros((8, LANES), jnp.float32)
    for ref, i, start, index, column, right in parts:
        part = ref[i, start : start + piece_rows, :]
        total = total + jnp.sum((part * part).reshape(-1, 8, LANES), axis=0)
    for column in range(4):
        for j in range(4):
            first = column * cols + (j % 2) * LANES
            small_ref[8 * (j // 2) : 8 * (j // 2) + 8, first : first + LANES] = extra_ref[j, column]
    small = small_ref[...]
    squares = jnp.sum(small * small, axis=1, keepdims=True)
    bias_out = small_ref[9:10, 0:1]
    last = bias_out * bias_out

    def factor(total, entries):
        return lax.rsqrt(total / entries + EPSILON)

    total = jnp.sum(jnp.sum(total, axis=1, keepdims=True), axis=0, keepdims=True)
    scale_mid = factor(total + squares[7:8], WIDTH * WIDTH + WIDTH)
    scale_in = factor(jnp.sum(squares[0:7], axis=0, keepdims=True), 7 * WIDTH)
    scale_out = factor(squares[8:9] + last, WIDTH + 1)
    w_in_ref[...] = small[0:6] * scale_in
    b_in_ref[...] = small[6:7] * scale_in
    b_mid_ref[...] = small[7:8] * scale_mid
    w_out_ref[...] = small[8:9] * scale_out
    b_out_ref[...] = bias_out * scale_out
    for ref, i, start, index, column, right in parts:
        rows = pl.ds(pl.multiple_of(index * piece_rows, piece_rows), piece_rows)
        first = pl.multiple_of(column * cols + (LANES if right else 0), LANES)
        part = ref[i, start : start + piece_rows, :]
        w_mid_ref[rows, pl.ds(first, LANES)] = part * scale_mid


def scaled(owner, groups, received):
    vmem = pl.BlockSpec(memory_space=pltpu.VMEM)
    shapes = [(6, WIDTH), (1, WIDTH), (WIDTH, WIDTH), (1, WIDTH), (1, WIDTH), (1, 1)]
    layout = [(masks, contents) for _, masks, contents in received]
    return pl.pallas_call(
        functools.partial(scaling_kernel, layout, groups),
        in_specs=[pl.BlockSpec(memory_space=pltpu.SMEM)] + [vmem] * len(received),
        out_specs=[vmem] * 6,
        out_shape=[jax.ShapeDtypeStruct(shape, jnp.float32) for shape in shapes],
        scratch_shapes=[
            pltpu.VMEM((max(groups, 4), 4, 8, LANES), jnp.float32),
            pltpu.VMEM((16, WIDTH), jnp.float32),
        ],
        compiler_params=pltpu.CompilerParams(vmem_limit_bytes=32 * 1024 * 1024),
        name="scaling",
    )(owner.reshape(1), *[array for array, _, _ in received])


def swap(array, bit, devices):
    return lax.ppermute(array, "paths", [(i, i ^ bit) for i in range(devices)])


def pick(array, index):
    return lax.dynamic_index_in_dim(array, index, 0, keepdims=False)


def halved(part, left, bit, group, devices):
    axis = len(left) - 1 - left.index(bit)
    shape = part.shape[1:]
    cube = part.reshape((2,) * len(left) + shape)
    mine = (group >> bit) % 2
    keep = lax.dynamic_index_in_dim(cube, mine, axis, keepdims=False)
    send = lax.dynamic_index_in_dim(cube, 1 - mine, axis, keepdims=False)
    send, keep = send.reshape((-1,) + shape), keep.reshape((-1,) + shape)
    return keep + swap(send, 2 << bit, devices)


def on_device(params, increments, w_in, b_in, w_mid, b_mid, w_out, b_out):
    devices = lax.axis_size("paths")
    top = devices // 2
    groups = devices // 4
    total_paths = increments.shape[2] * devices
    set_count = params.shape[0]
    set_dev = set_count // devices
    owner = lax.axis_index("paths")
    core = owner % 2
    high = owner // top
    group = (owner // 2) % groups
    block = 2 * high + core
    turned = params.T

    sums = payoff_sums(turned, increments, groups).reshape(groups, 4 * set_dev, PAIRS)
    win, weights, feat = prepare(owner, turned, w_in, b_in, w_mid, 4 * set_dev)
    lanes = [[2 * j + c + top * h for j in range(groups)] for h in range(2) for c in range(2)]
    parts = lax.all_to_all(sums, "paths", 0, 0, axis_index_groups=lanes, tiled=True)
    parts, win = lax.optimization_barrier((parts, win))
    sums = jnp.sum(parts, axis=0) / total_paths
    sums = [sums] + [swap(sums, mask, devices) for mask in (1, top, top + 1)]

    place = jnp.stack([owner, jnp.int32(top)])
    saved = forward(place, b_mid, w_out, win, weights, feat)
    *parts, prices = backward(
        owner, sums, saved, win, feat, w_mid, b_out, 1.0 / set_count, groups
    )

    bits = [bit for bit in range(groups.bit_length() - 1)]
    orders = [bits[first:] + bits[:first] for first in range(3)]
    parts = [
        parts[2 * n] + swap(parts[2 * n + 1], 2 << order[0], devices)
        for n, order in enumerate(orders)
    ]
    for step in range(1, len(bits)):
        parts = [
            halved(part, sorted(order[step:]), order[step], group, devices)
            for part, order in zip(parts, orders)
        ]

    own = jnp.concatenate(parts, axis=1)
    far = (0, top // 2, top, top + top // 2)
    whole = jnp.concatenate([own] + [swap(own, mask, devices) for mask in far[1:]], axis=0)
    received = [(whole, far, ("left", "extra", "right"))]
    split = WIDTH // groups + 8
    held_a, held_b = whole[:, :split], whole[:, split:]
    order = [2 << bit for bit in bits[:-1]]
    masks_a = masks_b = far
    for bit_a, bit_b in zip(order, order[1:] + order[:1]):
        came_a, came_b = swap(held_a, bit_a, devices), swap(held_b, bit_b, devices)
        new_a = tuple(mask ^ bit_a for mask in masks_a)
        new_b = tuple(mask ^ bit_b for mask in masks_b)
        if bit_a == order[-1]:
            near = [swap(array, 1, devices) for array, _, _ in received]
            came_a, came_b, *near = lax.optimization_barrier((came_a, came_b, *near))
        received += [(came_a, new_a, ("left", "extra")), (came_b, new_b, ("right",))]
        if bit_a != order[-1]:
            held_a = jnp.concatenate([held_a, came_a], axis=0)
            held_b = jnp.concatenate([held_b, came_b], axis=0)
        masks_a, masks_b = masks_a + new_a, masks_b + new_b
    near += [swap(array, 1, devices) for array, _, _ in received[len(near) :]]
    received += [
        (array, tuple(mask ^ 1 for mask in masks), contents)
        for array, (_, masks, contents) in zip(near, received)
    ]
    result = scaled(owner, groups, received)
    direction_w_in, direction_b_in, direction_w_mid, direction_b_mid, direction_w_out, direction_b_out = result
    return (
        prices,
        direction_w_in,
        direction_b_in.reshape(WIDTH),
        direction_w_mid,
        direction_b_mid.reshape(WIDTH),
        direction_w_out.reshape(WIDTH),
        direction_b_out.reshape(1),
    )


def solution(mesh):
    in_specs = (P(), P(None, None, "paths"), P(), P(), P(), P(), P(), P())
    out_specs = (P("paths", None), P(), P(), P(), P(), P(), P())
    return jax.shard_map(
        on_device, mesh=mesh, in_specs=in_specs, out_specs=out_specs, check_vma=False
    )
```

```python
import functools
import math

import jax
import jax.numpy as jnp
import numpy as np
from jax import lax
from jax.experimental import pallas as pl
from jax.experimental.pallas import tpu as pltpu
from jax.sharding import PartitionSpec as P

STEPS = 64
MATS = 8
STRIKES = 11
PAIRS = 88
WIDTH = 1024
LANES = 128
FEATURE_ROWS = 16
ROW_TILE = 256
FORWARD_VMEM = 24 * 1024 * 1024
BACKWARD_VMEM = 24 * 1024 * 1024
CHUNK = 512
CHUNKS = [slice(start, start + CHUNK) for start in range(0, WIDTH, CHUNK)]
EPSILON = 1e-06


TENORS = (np.arange(MATS, dtype=np.float32) + np.float32(1.0)) / np.float32(MATS)
OFFSETS = np.arange(STRIKES, dtype=np.float32) - np.float32((STRIKES - 1) / 2.0)
LOG_STRIKE = np.float32(0.05) * OFFSETS[None, :] * np.sqrt(TENORS)[:, None]
SET_BLOCK = 256
LOG2E = 1.4426950408889634


def bf16_pieces(value):
    high = value.astype(jnp.bfloat16)
    rest = value - high.astype(jnp.float32)
    mid = rest.astype(jnp.bfloat16)
    low = (rest - mid.astype(jnp.float32)).astype(jnp.bfloat16)
    return high, mid, low


def pricing_kernel(params_ref, inc_ref, out_ref, lags_ref, noise_ref, comp_ref, pay_ref):
    sets = params_ref.shape[1]
    paths = inc_ref.shape[2]
    hurst = params_ref[0:1, :]
    vol_of_vol = params_ref[1:2, :]
    correl = params_ref[2:3, :]
    forward_var = params_ref[3:4, :]
    delta_t = 1.0 / STEPS

    lag = (LANES - lax.broadcasted_iota(jnp.int32, (LANES, 1), 0)).astype(jnp.float32)
    exponent = hurst + 0.5
    here = jnp.exp2(exponent * jnp.log2(lag))
    before = jnp.exp2(exponent * jnp.log2(jnp.maximum(lag - 1.0, 1.0)))
    before = jnp.where(lag > 1.5, before, 0.0)
    front = jnp.sqrt(2.0 * hurst) * jnp.exp2(hurst * math.log2(delta_t)) / exponent
    weights = jnp.where(lag < STEPS - 0.5, (here - before) * front, 0.0).astype(jnp.bfloat16)

    half_scale = vol_of_vol * (0.5 * LOG2E)
    step = lax.broadcasted_iota(jnp.int32, (STEPS, 1), 0).astype(jnp.float32)
    powers = jnp.exp2(2.0 * hurst * jnp.log2(jnp.maximum(step, 1.0) * delta_t))
    comp_ref[...] = jnp.where(step > 0.5, powers * (0.25 * LOG2E * vol_of_vol * vol_of_vol), 0.0)

    root = jnp.sqrt(forward_var * delta_t)
    back = 2.0 / root
    growth = (0.5 * LOG2E) * forward_var * delta_t
    noise_weights = jnp.concatenate(
        [
            jnp.broadcast_to(piece.astype(jnp.float32), (8, sets))
            for value in (correl * back, jnp.sqrt(1.0 - correl * correl) * back)
            for piece in bf16_pieces(value)
        ]
        + [jnp.zeros((LANES - 48, sets), jnp.float32)],
        axis=0,
    ).astype(jnp.bfloat16)

    first = inc_ref[0].astype(jnp.float32)
    second = inc_ref[1].astype(jnp.float32)
    lags_ref[...] = jnp.concatenate([first, jnp.zeros((LANES - STEPS, paths), jnp.float32)], 0).T
    for m in range(MATS):
        rows = slice(8 * m, 8 * m + 8)
        block = jnp.concatenate(
            [first[rows]] * 3 + [second[rows]] * 3 + [jnp.zeros((LANES - 48, paths), jnp.float32)], 0
        )
        noise_ref[m] = block.T.astype(jnp.bfloat16)
    lane = lax.broadcasted_iota(jnp.int32, (paths, LANES), 1)

    def maturity(m, total):
        noise = noise_ref[m]
        for k in range(8):
            i = 8 * m + k
            window = lags_ref[...] if k == 0 else pltpu.roll(lags_ref[...], LANES - k, 1)
            drive = jnp.dot(
                window.astype(jnp.bfloat16), weights, preferred_element_type=jnp.float32
            )
            picked = jnp.where(lane % 8 == k, noise.astype(jnp.float32), 0.0).astype(jnp.bfloat16)
            shock = jnp.dot(picked, noise_weights, preferred_element_type=jnp.float32)
            root_variance = jnp.exp2(drive * half_scale - comp_ref[pl.ds(i, 1), :])
            total = total + root_variance * (shock - root_variance)
        lags_ref[...] = pltpu.roll(lags_ref[...], LANES - 8, 1)
        spot = jnp.exp2(total * growth)
        tenor = jnp.full((8, sets), 1.0, jnp.float32) * ((m + 1).astype(jnp.float32) / MATS)
        spread = jnp.sqrt(tenor)
        for j in range(STRIKES):
            strike = jnp.exp((0.05 * (j - (STRIKES - 1) / 2.0)) * spread)
            gains = jnp.maximum(spot.reshape(paths // 8, 8, sets), strike[None]).sum(axis=0)
            gains = gains - strike * (paths // 8)
            pay_ref[pl.ds(m * STRIKES + j, 1), :] = jnp.sum(gains, axis=0, keepdims=True)
        return total

    lax.fori_loop(0, MATS, maturity, jnp.zeros((paths, sets), jnp.float32))
    paid = pay_ref[...].T[:, :PAIRS]
    blocks, halves, half = out_ref.shape[:3]
    for h in range(halves):
        rows = paid[h * blocks * half : (h + 1) * blocks * half]
        out_ref[:, h] = rows.reshape(blocks, half, PAIRS)


def payoff_sums(params, increments, groups):
    count = params.shape[1]
    paths = increments.shape[2]
    sets = math.gcd(count, SET_BLOCK)
    steps = count // sets
    half = count // groups // 2
    halves = 2 if steps == 1 else 1
    blocks = sets // half // halves
    return pl.pallas_call(
        pricing_kernel,
        grid=(steps,),
        in_specs=[
            pl.BlockSpec((4, sets), lambda b: (0, b)),
            pl.BlockSpec((2, STEPS, paths), lambda b: (0, 0, 0)),
        ],
        out_specs=pl.BlockSpec(
            (blocks, halves, half, PAIRS),
            (lambda b: (0, 0, 0, 0))
            if steps == 1
            else (lambda b: (b % (steps // 2), b // (steps // 2), 0, 0)),
        ),
        out_shape=jax.ShapeDtypeStruct((groups, 2, half, PAIRS), jnp.float32),
        scratch_shapes=[
            pltpu.VMEM((paths, LANES), jnp.float32),
            pltpu.VMEM((MATS, paths, LANES), jnp.bfloat16),
            pltpu.VMEM((STEPS, sets), jnp.float32),
            pltpu.VMEM((LANES, sets), jnp.float32),
        ],
        compiler_params=pltpu.CompilerParams(vmem_limit_bytes=32 * 1024 * 1024),
        name="pricing",
    )(in_hbm(params), in_hbm(increments))


def in_hbm(array):
    return pltpu.with_memory_space_constraint(array, pltpu.HBM)


def dot(left, right):
    return jnp.dot(left, right, preferred_element_type=jnp.float32)


def dot_rows(left, right):
    return lax.dot_general(
        left, right, (((1,), (1,)), ((), ())), preferred_element_type=jnp.float32
    )


def one_hot(t, sets):
    row = t * ROW_TILE + lax.broadcasted_iota(jnp.int32, (1, ROW_TILE), 1)
    group_set = ((row.astype(jnp.float32) + 0.5) * (1.0 / PAIRS)).astype(jnp.int32)
    pair = row - PAIRS * group_set
    code = lax.broadcasted_iota(jnp.int32, (LANES, ROW_TILE), 0)
    hot = jnp.where((code == pair) | (code == group_set + PAIRS), 1.0, 0.0)
    return hot.astype(jnp.bfloat16), group_set


def feature_table(params_ref, group, sets):
    set_count = params_ref.shape[1]
    lane = lax.broadcasted_iota(jnp.int32, (1, LANES), 1)
    maturity = ((lane.astype(jnp.float32) + 0.5) * (1.0 / STRIKES)).astype(jnp.int32)
    offset = (lane - STRIKES * maturity).astype(jnp.float32) - (STRIKES - 1) / 2.0
    spread = jnp.zeros((1, LANES), jnp.float32)
    for m in range(MATS):
        spread = jnp.where(maturity == m, float(np.sqrt(TENORS)[m]), spread)
    strikes = jnp.where(lane < PAIRS, 4.0 * (0.05 * offset * spread), 0.0)
    tenors = jnp.where(lane < PAIRS, (maturity.astype(jnp.float32) + 1.0) / MATS, 0.0)
    ones = jnp.where((lane >= PAIRS) & (lane < PAIRS + sets), 1.0, 0.0)
    wide = jnp.concatenate([params_ref[...], jnp.zeros((4, set_count), jnp.float32)], 0)
    half = sets // 2
    own = jnp.zeros((8, LANES), jnp.float32)
    for high in range(2):
        first = PAIRS + high * half
        start = high * (set_count // 2) + group * half
        moved = pltpu.roll(wide, lax.rem(first + set_count - start, set_count), 1)[:, :LANES]
        own = jnp.where((lane >= first) & (lane < first + half), moved, own)
    scale = [own[0:1] * 4.0, own[1:2], own[2:3], own[3:4] * 20.0]
    pad = jnp.zeros((FEATURE_ROWS - 9, LANES), jnp.float32)
    return jnp.concatenate(scale + [strikes, tenors, ones, ones, ones, pad], 0)


def prepare_kernel(
    sets, owner_ref, params_ref, w_in_hbm, b_in_hbm, w_mid_hbm, win_ref, turned_ref, feat_ref,
    w_in_ref, b_in_ref, w_mid_ref, sems,
):
    copies = [
        pltpu.make_async_copy(source, target, sems.at[i])
        for i, (source, target) in enumerate(
            ((w_in_hbm, w_in_ref), (b_in_hbm, b_in_ref), (w_mid_hbm, w_mid_ref))
        )
    ]
    for copy in copies:
        copy.start()
    devices = params_ref.shape[1] * 4 // sets
    group = (owner_ref[0] // 2) % (devices // 4)
    table = feature_table(params_ref, group, sets).astype(jnp.bfloat16)
    for t in range(feat_ref.shape[1] // ROW_TILE):
        hot, _ = one_hot(t, sets)
        feat = dot(table, hot).astype(jnp.bfloat16)
        feat_ref[:, t * ROW_TILE : (t + 1) * ROW_TILE] = feat
    for copy in copies:
        copy.wait()
    weights_in = w_in_ref[...].astype(jnp.float32)
    bias_in = [piece.astype(jnp.float32) for piece in bf16_pieces(b_in_ref[...])]
    pad = jnp.zeros((FEATURE_ROWS - weights_in.shape[0] - 3, WIDTH), jnp.float32)
    win = (0.5 * jnp.concatenate([weights_in] + bias_in + [pad], 0)).T
    win_ref[...] = win.astype(jnp.bfloat16)
    turned_ref[...] = (0.5 * w_mid_ref[...].astype(jnp.float32)).T.astype(jnp.bfloat16)


def prepare(owner, params, w_in, b_in, w_mid, sets):
    smem = pl.BlockSpec(memory_space=pltpu.SMEM)
    vmem = pl.BlockSpec(memory_space=pltpu.VMEM)
    hbm = pl.BlockSpec(memory_space=pltpu.HBM)
    return pl.pallas_call(
        functools.partial(prepare_kernel, sets),
        in_specs=[smem, vmem] + [hbm] * 3,
        out_specs=[vmem] * 3,
        out_shape=[
            jax.ShapeDtypeStruct((WIDTH, FEATURE_ROWS), jnp.bfloat16),
            jax.ShapeDtypeStruct((WIDTH, WIDTH), jnp.bfloat16),
            jax.ShapeDtypeStruct((FEATURE_ROWS, sets * PAIRS), jnp.bfloat16),
        ],
        scratch_shapes=[
            pltpu.VMEM(w_in.shape, jnp.bfloat16),
            pltpu.VMEM((1, WIDTH), jnp.float32),
            pltpu.VMEM((WIDTH, WIDTH), jnp.bfloat16),
            pltpu.SemaphoreType.DMA((3,)),
        ],
        compiler_params=pltpu.CompilerParams(vmem_limit_bytes=16 * 1024 * 1024),
        name="prepare",
    )(
        owner.reshape(1), in_hbm(params), in_hbm(w_in), in_hbm(b_in.reshape(1, -1)), in_hbm(w_mid)
    )


def forward_kernel(
    owner_ref, b_mid_ref, w_out_ref, win_ref, turned_ref, feat_ref,
    hidden_out, curve_out, mixed_out, pred_out, bias_ref, read_ref,
    even_hidden, odd_hidden, even_mixed, odd_mixed,
):
    bf16 = jnp.bfloat16
    tiles = hidden_out.shape[1] // ROW_TILE
    cols = WIDTH // 4
    owner = owner_ref[0]
    block = 2 * (owner // owner_ref[1]) + owner % 2
    own = pl.ds(pl.multiple_of(block * cols, cols), cols)
    read_ref[...] = jnp.broadcast_to((0.5 * w_out_ref[...].astype(jnp.float32)).T, read_ref.shape)
    readout = jnp.broadcast_to(w_out_ref[...].astype(jnp.float32), (16, WIDTH)).astype(bf16)
    bias_ref[...] = jnp.broadcast_to((0.5 * b_mid_ref[...]).T, bias_ref.shape)

    def wide(column):
        return jnp.concatenate([column] * (ROW_TILE // LANES), axis=1)

    def span(t):
        return pl.ds(pl.multiple_of(t * ROW_TILE, ROW_TILE), ROW_TILE)

    def step(t, new, old, first=True, second=True, third=True):
        new_hidden, new_mixed = new
        old_hidden, old_mixed = old
        if first:
            feat = feat_ref[:, span(t)]

        def products(c):
            return (
                dot(turned_ref[c, :], old_hidden[...]) if second else None,
                dot(win_ref[c, :], feat) if first else None,
            )

        ahead = products(CHUNKS[0])
        if third:
            predicted = dot(readout, new_mixed[...])
            mixed_out[:, span(t - 2)] = new_mixed[own, :]
        for n, c in enumerate(CHUNKS):
            half_mid, half_in = ahead
            if n + 1 < len(CHUNKS):
                ahead = products(CHUNKS[n + 1])
            if second:
                half_mid = half_mid + wide(bias_ref[c, :])
                wave = jnp.tanh(half_mid)
                turn = half_mid * wave
                old_mixed[c, :] = (half_mid + turn).astype(bf16)
                curve_out[c, span(t - 1)] = (1.0 + wave) * (1.0 + half_mid - turn) * wide(read_ref[c, :])
            if first:
                value = (half_in + half_in * jnp.tanh(half_in)).astype(bf16)
                new_hidden[c, :] = value
                hidden_out[c, span(t)] = value
        if third:
            pred_out[0:1, span(t - 2)] = predicted[0:1]

    even, odd = (even_hidden, even_mixed), (odd_hidden, odd_mixed)
    step(0, even, odd, second=False, third=False)
    step(1, odd, even, third=False)

    def two_steps(u, carry):
        step(2 * u + 2, even, odd)
        step(2 * u + 3, odd, even)
        return carry

    lax.fori_loop(0, (tiles - 2) // 2, two_steps, 0)
    buffers = [even, odd]
    for t in range(2 + (tiles - 2) // 2 * 2, tiles + 2):
        step(t, buffers[t % 2], buffers[1 - t % 2], first=t < tiles, second=t <= tiles)


def forward(place, b_mid, w_out, win, turned, feat):
    rows = feat.shape[1]
    cols = WIDTH // 4
    vmem = pl.BlockSpec(memory_space=pltpu.VMEM)
    smem = pl.BlockSpec(memory_space=pltpu.SMEM)
    outs = [
        ((WIDTH, rows), jnp.bfloat16),
        ((WIDTH, rows), jnp.float32),
        ((cols, rows), jnp.bfloat16),
        ((1, rows), jnp.float32),
    ]
    return pl.pallas_call(
        forward_kernel,
        in_specs=[smem] + [vmem] * 5,
        out_specs=[vmem] * len(outs),
        out_shape=[pltpu.VMEM(shape, kind) for shape, kind in outs[:-1]]
        + [jax.ShapeDtypeStruct(*outs[-1])],
        scratch_shapes=[
            pltpu.VMEM((WIDTH, LANES), jnp.float32),
            pltpu.VMEM((WIDTH, LANES), jnp.float32),
        ]
        + [pltpu.VMEM((WIDTH, ROW_TILE), jnp.bfloat16)] * 4,
        compiler_params=pltpu.CompilerParams(vmem_limit_bytes=FORWARD_VMEM),
        cost_estimate=pl.CostEstimate(
            flops=2 * rows * WIDTH * (WIDTH + 32), bytes_accessed=4 << 20, transcendentals=0
        ),
        name="forward",
    )(place, in_hbm(b_mid.reshape(1, -1)), w_out.reshape(1, -1), win, turned, feat)


def backward_kernel(
    inv_sets, owner_ref, sums_ref, near_ref, far_ref, both_ref, hidden_ref, curve_ref, mixed_ref, pred_ref, win_ref,
    feat_ref, w_mid_hbm, b_out_ref, keep_x, send_x, keep_y, send_y, keep_z, send_z, prices_ref,
    left_ref, back_ref, slope_ref, even_delta, odd_delta, delta_in_ref, own_delta_ref, bias_ref,
    read_ref, pieces_ref, sem,
):
    bf16 = jnp.bfloat16
    sets = sums_ref.shape[0]
    rows = hidden_ref.shape[1]
    groups = pieces_ref.shape[0]
    piece_rows = WIDTH // groups
    cols = WIDTH // 4
    owner = owner_ref[0]
    block = 2 * (owner // (2 * groups)) + owner % 2
    own = pl.ds(pl.multiple_of(block * cols, cols), cols)
    fetch = pltpu.make_async_copy(w_mid_hbm.at[own, :], back_ref, sem)
    fetch.start()

    left_ref[...] = jnp.zeros_like(left_ref)
    sums = (sums_ref[...] + near_ref[...]) + (far_ref[...] + both_ref[...])
    set_dev = sets // 4
    prices = sums[:set_dev]
    for b in range(1, 4):
        prices = jnp.where(block == b, sums[b * set_dev : (b + 1) * set_dev], prices)
    prices_ref[...] = prices
    for p, piece in enumerate(bf16_pieces(sums)):
        left_ref[p * sets : (p + 1) * sets, :PAIRS] = piece.astype(jnp.float32)
    left = left_ref[...].astype(bf16)
    tiles = [slice(first, first + ROW_TILE) for first in range(0, rows, ROW_TILE)]
    for t, here in enumerate(tiles):
        hot, group_set = one_hot(t, sets)
        looked = dot(left, hot)
        target = looked[:sets] + looked[sets : 2 * sets] + looked[2 * sets :]
        member = lax.broadcasted_iota(jnp.int32, (sets, ROW_TILE), 0)
        target = jnp.sum(jnp.where(member == group_set, target, 0.0), axis=0, keepdims=True)
        slope_ref[0:1, here] = (pred_ref[0:1, here] + b_out_ref[0] - target) * inv_sets
    fetch.wait()
    for t, here in enumerate(tiles):
        delta_ref = (even_delta, odd_delta)[t % 2]
        slope = slope_ref[0:1, here]
        for c in CHUNKS:
            delta_ref[c, :] = (slope * curve_ref[c, here]).astype(bf16)
        backward = dot(back_ref[...], delta_ref[...])
        own_delta = (slope * curve_ref[own, here]).astype(bf16)
        own_delta_ref[:, here] = own_delta
        bias = own_delta.astype(jnp.float32)
        read = mixed_ref[:, here].astype(jnp.float32) * slope
        bias = bias[:, :LANES] + bias[:, LANES:]
        read = read[:, :LANES] + read[:, LANES:]
        bias_ref[...] = bias if t == 0 else bias_ref[...] + bias
        read_ref[...] = read if t == 0 else read_ref[...] + read
        half = dot(win_ref[own, :], feat_ref[:, here])
        wave = jnp.tanh(half)
        curve = (0.5 * (1.0 + wave)) * (1.0 + half * (1.0 - wave))
        delta_in_ref[:, here] = (backward * curve).astype(bf16)

    for c in CHUNKS:
        total = dot_rows(hidden_ref[c, :], own_delta_ref[...])
        for first in range(0, CHUNK, piece_rows):
            j = (c.start + first) // piece_rows
            part = total[first : first + piece_rows]
            pieces_ref[j, 0:piece_rows, :] = part[:, :LANES]
            pieces_ref[j, piece_rows + 8 :, :] = part[:, LANES:]
    extra = [dot_rows(delta_in_ref[...], feat_ref[...]).T[0:7]]
    extra.append(jnp.sum(bias_ref[...].T, axis=0, keepdims=True))
    extra.append(jnp.sum(read_ref[...].T, axis=0, keepdims=True))
    total = jnp.sum(slope_ref[...], axis=1, keepdims=True)
    extra.append(jnp.broadcast_to(total, (1, cols)))
    extra.append(jnp.zeros((6, cols), jnp.float32))
    extra = jnp.concatenate(extra, 0)
    for j in range(groups):
        lanes = slice((j % 2) * LANES, (j % 2 + 1) * LANES)
        part = extra[8 * (j // 2) : 8 * (j // 2) + 8, lanes] if j < 4 else jnp.zeros((8, LANES))
        pieces_ref[j, piece_rows : piece_rows + 8, :] = part
    group = (owner // 2) % groups
    cuts = part_cuts(groups)
    for bit, (keep, send) in enumerate(((keep_x, send_x), (keep_y, send_y), (keep_z, send_z))):
        mine = (group // 2**bit) % 2
        for i in range(groups // 2):
            base = (i >> bit << (bit + 1)) + (i & (2**bit - 1))
            keep[i] = pieces_ref[base + mine * 2**bit, cuts[bit] : cuts[bit + 1], :]
            send[i] = pieces_ref[base + (1 - mine) * 2**bit, cuts[bit] : cuts[bit + 1], :]


def part_cuts(groups):
    rows = 2 * (WIDTH // groups) + 8
    third = rows // 24 * 8
    return (0, third, 2 * third, rows)


def backward(owner, sums, saved, win, feat, w_mid, b_out, inv_sets, groups):
    sets = sums[0].shape[0]
    cuts = part_cuts(groups)
    rows = sets * PAIRS
    cols = WIDTH // 4
    vmem = pl.BlockSpec(memory_space=pltpu.VMEM)
    smem = pl.BlockSpec(memory_space=pltpu.SMEM)
    hbm = pl.BlockSpec(memory_space=pltpu.HBM)
    return pl.pallas_call(
        functools.partial(backward_kernel, inv_sets),
        in_specs=[smem] + [vmem] * 10 + [hbm, smem],
        out_specs=[vmem] * 7,
        out_shape=[
            jax.ShapeDtypeStruct((groups // 2, stop - start, LANES), jnp.float32)
            for start, stop in zip(cuts, cuts[1:])
            for _ in range(2)
        ]
        + [jax.ShapeDtypeStruct((sets // 4, PAIRS), jnp.float32)],
        scratch_shapes=[
            pltpu.VMEM((3 * sets, LANES), jnp.float32),
            pltpu.VMEM((cols, WIDTH), jnp.bfloat16),
            pltpu.VMEM((1, rows), jnp.float32),
            pltpu.VMEM((WIDTH, ROW_TILE), jnp.bfloat16),
            pltpu.VMEM((WIDTH, ROW_TILE), jnp.bfloat16),
            pltpu.VMEM((cols, rows), jnp.bfloat16),
            pltpu.VMEM((cols, rows), jnp.bfloat16),
            pltpu.VMEM((cols, LANES), jnp.float32),
            pltpu.VMEM((cols, LANES), jnp.float32),
            pltpu.VMEM((groups, 2 * (WIDTH // groups) + 8, LANES), jnp.float32),
            pltpu.SemaphoreType.DMA,
        ],
        compiler_params=pltpu.CompilerParams(vmem_limit_bytes=BACKWARD_VMEM),
        name="backward",
    )(owner.reshape(1), *sums, *saved, win, feat, in_hbm(w_mid), b_out)


def scaling_kernel(layout, groups, owner_ref, *refs):
    blocks = refs[: len(layout)]
    w_in_ref, b_in_ref, w_mid_ref, b_mid_ref, w_out_ref, b_out_ref, extra_ref, small_ref = refs[
        len(layout) :
    ]
    piece_rows = WIDTH // groups
    cols = WIDTH // 4
    owner = owner_ref[0]
    parts = []
    for ref, (masks, contents) in zip(blocks, layout):
        for i, mask in enumerate(masks):
            device = owner ^ mask
            index = (device >> 1) & (groups - 1)
            column = 2 * (device // (2 * groups)) + (device & 1)
            start = 0
            for content in contents:
                if content == "extra":
                    extra_ref[index, column] = ref[i, start : start + 8, :]
                    start += 8
                else:
                    parts.append((ref, i, start, index, column, content == "right"))
                    start += piece_rows

    total = jnp.zeros((8, LANES), jnp.float32)
    for ref, i, start, index, column, right in parts:
        part = ref[i, start : start + piece_rows, :]
        total = total + jnp.sum((part * part).reshape(-1, 8, LANES), axis=0)
    for column in range(4):
        for j in range(4):
            first = column * cols + (j % 2) * LANES
            small_ref[8 * (j // 2) : 8 * (j // 2) + 8, first : first + LANES] = extra_ref[j, column]
    small = small_ref[...]
    squares = jnp.sum(small * small, axis=1, keepdims=True)
    bias_out = small_ref[9:10, 0:1]
    last = bias_out * bias_out

    def factor(total, entries):
        return lax.rsqrt(total / entries + EPSILON)

    total = jnp.sum(jnp.sum(total, axis=1, keepdims=True), axis=0, keepdims=True)
    scale_mid = factor(total + squares[7:8], WIDTH * WIDTH + WIDTH)
    scale_in = factor(jnp.sum(squares[0:7], axis=0, keepdims=True), 7 * WIDTH)
    scale_out = factor(squares[8:9] + last, WIDTH + 1)
    w_in_ref[...] = small[0:6] * scale_in
    b_in_ref[...] = small[6:7] * scale_in
    b_mid_ref[...] = small[7:8] * scale_mid
    w_out_ref[...] = small[8:9] * scale_out
    b_out_ref[...] = bias_out * scale_out
    for ref, i, start, index, column, right in parts:
        rows = pl.ds(pl.multiple_of(index * piece_rows, piece_rows), piece_rows)
        first = pl.multiple_of(column * cols + (LANES if right else 0), LANES)
        part = ref[i, start : start + piece_rows, :]
        w_mid_ref[rows, pl.ds(first, LANES)] = part * scale_mid


def scaled(owner, groups, received):
    vmem = pl.BlockSpec(memory_space=pltpu.VMEM)
    shapes = [(6, WIDTH), (1, WIDTH), (WIDTH, WIDTH), (1, WIDTH), (1, WIDTH), (1, 1)]
    layout = [(masks, contents) for _, masks, contents in received]
    return pl.pallas_call(
        functools.partial(scaling_kernel, layout, groups),
        in_specs=[pl.BlockSpec(memory_space=pltpu.SMEM)] + [vmem] * len(received),
        out_specs=[vmem] * 6,
        out_shape=[jax.ShapeDtypeStruct(shape, jnp.float32) for shape in shapes],
        scratch_shapes=[
            pltpu.VMEM((max(groups, 4), 4, 8, LANES), jnp.float32),
            pltpu.VMEM((16, WIDTH), jnp.float32),
        ],
        compiler_params=pltpu.CompilerParams(vmem_limit_bytes=32 * 1024 * 1024),
        name="scaling",
    )(owner.reshape(1), *[array for array, _, _ in received])


def swap(array, bit, devices):
    return lax.ppermute(array, "paths", [(i, i ^ bit) for i in range(devices)])


def pick(array, index):
    return lax.dynamic_index_in_dim(array, index, 0, keepdims=False)


def halved(part, left, bit, group, devices):
    axis = len(left) - 1 - left.index(bit)
    shape = part.shape[1:]
    cube = part.reshape((2,) * len(left) + shape)
    mine = (group >> bit) % 2
    keep = lax.dynamic_index_in_dim(cube, mine, axis, keepdims=False)
    send = lax.dynamic_index_in_dim(cube, 1 - mine, axis, keepdims=False)
    send, keep = send.reshape((-1,) + shape), keep.reshape((-1,) + shape)
    return keep + swap(send, 2 << bit, devices)


def on_device(params, increments, w_in, b_in, w_mid, b_mid, w_out, b_out):
    devices = lax.axis_size("paths")
    top = devices // 2
    groups = devices // 4
    total_paths = increments.shape[2] * devices
    set_count = params.shape[0]
    set_dev = set_count // devices
    owner = lax.axis_index("paths")
    core = owner % 2
    high = owner // top
    group = (owner // 2) % groups
    block = 2 * high + core
    turned = params.T

    sums = payoff_sums(turned, increments, groups).reshape(groups, 4 * set_dev, PAIRS)
    win, weights, feat = prepare(owner, turned, w_in, b_in, w_mid, 4 * set_dev)
    lanes = [[2 * j + c + top * h for j in range(groups)] for h in range(2) for c in range(2)]
    parts = lax.all_to_all(sums, "paths", 0, 0, axis_index_groups=lanes, tiled=True)
    parts, win = lax.optimization_barrier((parts, win))
    sums = jnp.sum(parts, axis=0) / total_paths
    sums = [sums] + [swap(sums, mask, devices) for mask in (1, top, top + 1)]

    place = jnp.stack([owner, jnp.int32(top)])
    saved = forward(place, b_mid, w_out, win, weights, feat)
    *parts, prices = backward(
        owner, sums, saved, win, feat, w_mid, b_out, 1.0 / set_count, groups
    )

    bits = [bit for bit in range(groups.bit_length() - 1)]
    orders = [bits[first:] + bits[:first] for first in range(3)]
    parts = [
        parts[2 * n] + swap(parts[2 * n + 1], 2 << order[0], devices)
        for n, order in enumerate(orders)
    ]
    for step in range(1, len(bits)):
        parts = [
            halved(part, sorted(order[step:]), order[step], group, devices)
            for part, order in zip(parts, orders)
        ]

    own = jnp.concatenate(parts, axis=1)
    far = (0, top + top // 2, top, top // 2)
    whole = jnp.concatenate([own] + [swap(own, mask, devices) for mask in far[1:]], axis=0)
    received = [(whole, far, ("left", "extra", "right"))]
    split = WIDTH // groups + 8
    held_a, held_b = whole[:, :split], whole[:, split:]
    order = [2 << bit for bit in bits[:-1]]
    masks_a = masks_b = far
    for bit_a, bit_b in zip(order, order[1:] + order[:1]):
        came_a, came_b = swap(held_a, bit_a, devices), swap(held_b, bit_b, devices)
        new_a = tuple(mask ^ bit_a for mask in masks_a)
        new_b = tuple(mask ^ bit_b for mask in masks_b)
        if bit_a == order[-1]:
            near = [swap(array, 1, devices) for array, _, _ in received]
            came_a, came_b, *near = lax.optimization_barrier((came_a, came_b, *near))
        received += [(came_a, new_a, ("left", "extra")), (came_b, new_b, ("right",))]
        if bit_a != order[-1]:
            held_a = jnp.concatenate([held_a, came_a], axis=0)
            held_b = jnp.concatenate([held_b, came_b], axis=0)
        masks_a, masks_b = masks_a + new_a, masks_b + new_b
    near += [swap(array, 1, devices) for array, _, _ in received[len(near) :]]
    received += [
        (array, tuple(mask ^ 1 for mask in masks), contents)
        for array, (_, masks, contents) in zip(near, received)
    ]
    result = scaled(owner, groups, received)
    direction_w_in, direction_b_in, direction_w_mid, direction_b_mid, direction_w_out, direction_b_out = result
    return (
        prices,
        direction_w_in,
        direction_b_in.reshape(WIDTH),
        direction_w_mid,
        direction_b_mid.reshape(WIDTH),
        direction_w_out.reshape(WIDTH),
        direction_b_out.reshape(1),
    )


def solution(mesh):
    in_specs = (P(), P(None, None, "paths"), P(), P(), P(), P(), P(), P())
    out_specs = (P("paths", None), P(), P(), P(), P(), P(), P())
    return jax.shard_map(
        on_device, mesh=mesh, in_specs=in_specs, out_specs=out_specs, check_vma=False
    )
```

```python
import functools
import math

import jax
import jax.numpy as jnp
import numpy as np
from jax import lax
from jax.experimental import pallas as pl
from jax.experimental.pallas import tpu as pltpu
from jax.sharding import PartitionSpec as P

STEPS = 64
MATS = 8
STRIKES = 11
PAIRS = 88
WIDTH = 1024
LANES = 128
FEATURE_ROWS = 16
ROW_TILE = 256
FORWARD_VMEM = 24 * 1024 * 1024
BACKWARD_VMEM = 24 * 1024 * 1024
CHUNK = 512
CHUNKS = [slice(start, start + CHUNK) for start in range(0, WIDTH, CHUNK)]
EPSILON = 1e-06


TENORS = (np.arange(MATS, dtype=np.float32) + np.float32(1.0)) / np.float32(MATS)
OFFSETS = np.arange(STRIKES, dtype=np.float32) - np.float32((STRIKES - 1) / 2.0)
LOG_STRIKE = np.float32(0.05) * OFFSETS[None, :] * np.sqrt(TENORS)[:, None]
SET_BLOCK = 256
LOG2E = 1.4426950408889634


def bf16_pieces(value):
    high = value.astype(jnp.bfloat16)
    rest = value - high.astype(jnp.float32)
    mid = rest.astype(jnp.bfloat16)
    low = (rest - mid.astype(jnp.float32)).astype(jnp.bfloat16)
    return high, mid, low


def pricing_kernel(params_ref, inc_ref, out_ref, lags_ref, noise_ref, comp_ref, pay_ref):
    sets = params_ref.shape[1]
    paths = inc_ref.shape[2]
    hurst = params_ref[0:1, :]
    vol_of_vol = params_ref[1:2, :]
    correl = params_ref[2:3, :]
    forward_var = params_ref[3:4, :]
    delta_t = 1.0 / STEPS

    lag = (LANES - lax.broadcasted_iota(jnp.int32, (LANES, 1), 0)).astype(jnp.float32)
    exponent = hurst + 0.5
    here = jnp.exp2(exponent * jnp.log2(lag))
    before = jnp.exp2(exponent * jnp.log2(jnp.maximum(lag - 1.0, 1.0)))
    before = jnp.where(lag > 1.5, before, 0.0)
    front = jnp.sqrt(2.0 * hurst) * jnp.exp2(hurst * math.log2(delta_t)) / exponent
    weights = jnp.where(lag < STEPS - 0.5, (here - before) * front, 0.0).astype(jnp.bfloat16)

    half_scale = vol_of_vol * (0.5 * LOG2E)
    step = lax.broadcasted_iota(jnp.int32, (STEPS, 1), 0).astype(jnp.float32)
    powers = jnp.exp2(2.0 * hurst * jnp.log2(jnp.maximum(step, 1.0) * delta_t))
    comp_ref[...] = jnp.where(step > 0.5, powers * (0.25 * LOG2E * vol_of_vol * vol_of_vol), 0.0)

    root = jnp.sqrt(forward_var * delta_t)
    back = 2.0 / root
    growth = (0.5 * LOG2E) * forward_var * delta_t
    noise_weights = jnp.concatenate(
        [
            jnp.broadcast_to(piece.astype(jnp.float32), (8, sets))
            for value in (correl * back, jnp.sqrt(1.0 - correl * correl) * back)
            for piece in bf16_pieces(value)
        ]
        + [jnp.zeros((LANES - 48, sets), jnp.float32)],
        axis=0,
    ).astype(jnp.bfloat16)

    first = inc_ref[0].astype(jnp.float32)
    second = inc_ref[1].astype(jnp.float32)
    lags_ref[...] = jnp.concatenate([first, jnp.zeros((LANES - STEPS, paths), jnp.float32)], 0).T
    for m in range(MATS):
        rows = slice(8 * m, 8 * m + 8)
        block = jnp.concatenate(
            [first[rows]] * 3 + [second[rows]] * 3 + [jnp.zeros((LANES - 48, paths), jnp.float32)], 0
        )
        noise_ref[m] = block.T.astype(jnp.bfloat16)
    lane = lax.broadcasted_iota(jnp.int32, (paths, LANES), 1)

    def maturity(m, total):
        noise = noise_ref[m].astype(jnp.float32)
        lags = lags_ref[...]
        for first in range(0, 8, 4):
            steps = range(first, first + 4)
            windows = [lags if k == 0 else pltpu.roll(lags, LANES - k, 1) for k in steps]
            windows = jnp.concatenate(windows, 0).astype(jnp.bfloat16)
            drives = jnp.dot(windows, weights, preferred_element_type=jnp.float32)
            picked = [jnp.where(lane % 8 == k, noise, 0.0) for k in steps]
            picked = jnp.concatenate(picked, 0).astype(jnp.bfloat16)
            shocks = jnp.dot(picked, noise_weights, preferred_element_type=jnp.float32)
            for n, k in enumerate(steps):
                here = slice(n * paths, (n + 1) * paths)
                lift = drives[here] * half_scale - comp_ref[pl.ds(8 * m + k, 1), :]
                root_variance = jnp.exp2(lift)
                total = total + root_variance * (shocks[here] - root_variance)
        lags_ref[...] = pltpu.roll(lags_ref[...], LANES - 8, 1)
        spot = jnp.exp2(total * growth)
        tenor = jnp.full((8, sets), 1.0, jnp.float32) * ((m + 1).astype(jnp.float32) / MATS)
        spread = jnp.sqrt(tenor)
        for j in range(STRIKES):
            strike = jnp.exp((0.05 * (j - (STRIKES - 1) / 2.0)) * spread)
            gains = jnp.maximum(spot.reshape(paths // 8, 8, sets), strike[None]).sum(axis=0)
            gains = gains - strike * (paths // 8)
            pay_ref[pl.ds(m * STRIKES + j, 1), :] = jnp.sum(gains, axis=0, keepdims=True)
        return total

    lax.fori_loop(0, MATS, maturity, jnp.zeros((paths, sets), jnp.float32))
    paid = pay_ref[...].T[:, :PAIRS]
    blocks, halves, half = out_ref.shape[:3]
    for h in range(halves):
        rows = paid[h * blocks * half : (h + 1) * blocks * half]
        out_ref[:, h] = rows.reshape(blocks, half, PAIRS)


def payoff_sums(params, increments, groups):
    count = params.shape[1]
    paths = increments.shape[2]
    sets = math.gcd(count, SET_BLOCK)
    steps = count // sets
    half = count // groups // 2
    halves = 2 if steps == 1 else 1
    blocks = sets // half // halves
    return pl.pallas_call(
        pricing_kernel,
        grid=(steps,),
        in_specs=[
            pl.BlockSpec((4, sets), lambda b: (0, b)),
            pl.BlockSpec((2, STEPS, paths), lambda b: (0, 0, 0)),
        ],
        out_specs=pl.BlockSpec(
            (blocks, halves, half, PAIRS),
            (lambda b: (0, 0, 0, 0))
            if steps == 1
            else (lambda b: (b % (steps // 2), b // (steps // 2), 0, 0)),
        ),
        out_shape=jax.ShapeDtypeStruct((groups, 2, half, PAIRS), jnp.float32),
        scratch_shapes=[
            pltpu.VMEM((paths, LANES), jnp.float32),
            pltpu.VMEM((MATS, paths, LANES), jnp.bfloat16),
            pltpu.VMEM((STEPS, sets), jnp.float32),
            pltpu.VMEM((LANES, sets), jnp.float32),
        ],
        compiler_params=pltpu.CompilerParams(vmem_limit_bytes=32 * 1024 * 1024),
        name="pricing",
    )(in_hbm(params), in_hbm(increments))


def in_hbm(array):
    return pltpu.with_memory_space_constraint(array, pltpu.HBM)


def dot(left, right):
    return jnp.dot(left, right, preferred_element_type=jnp.float32)


def dot_rows(left, right):
    return lax.dot_general(
        left, right, (((1,), (1,)), ((), ())), preferred_element_type=jnp.float32
    )


def one_hot(t, sets):
    row = t * ROW_TILE + lax.broadcasted_iota(jnp.int32, (1, ROW_TILE), 1)
    group_set = ((row.astype(jnp.float32) + 0.5) * (1.0 / PAIRS)).astype(jnp.int32)
    pair = row - PAIRS * group_set
    code = lax.broadcasted_iota(jnp.int32, (LANES, ROW_TILE), 0)
    hot = jnp.where((code == pair) | (code == group_set + PAIRS), 1.0, 0.0)
    return hot.astype(jnp.bfloat16), group_set


def feature_table(params_ref, group, sets):
    set_count = params_ref.shape[1]
    lane = lax.broadcasted_iota(jnp.int32, (1, LANES), 1)
    maturity = ((lane.astype(jnp.float32) + 0.5) * (1.0 / STRIKES)).astype(jnp.int32)
    offset = (lane - STRIKES * maturity).astype(jnp.float32) - (STRIKES - 1) / 2.0
    spread = jnp.zeros((1, LANES), jnp.float32)
    for m in range(MATS):
        spread = jnp.where(maturity == m, float(np.sqrt(TENORS)[m]), spread)
    strikes = jnp.where(lane < PAIRS, 4.0 * (0.05 * offset * spread), 0.0)
    tenors = jnp.where(lane < PAIRS, (maturity.astype(jnp.float32) + 1.0) / MATS, 0.0)
    ones = jnp.where((lane >= PAIRS) & (lane < PAIRS + sets), 1.0, 0.0)
    wide = jnp.concatenate([params_ref[...], jnp.zeros((4, set_count), jnp.float32)], 0)
    half = sets // 2
    own = jnp.zeros((8, LANES), jnp.float32)
    for high in range(2):
        first = PAIRS + high * half
        start = high * (set_count // 2) + group * half
        moved = pltpu.roll(wide, lax.rem(first + set_count - start, set_count), 1)[:, :LANES]
        own = jnp.where((lane >= first) & (lane < first + half), moved, own)
    scale = [own[0:1] * 4.0, own[1:2], own[2:3], own[3:4] * 20.0]
    pad = jnp.zeros((FEATURE_ROWS - 9, LANES), jnp.float32)
    return jnp.concatenate(scale + [strikes, tenors, ones, ones, ones, pad], 0)


def prepare_kernel(
    sets, owner_ref, params_ref, w_in_hbm, b_in_hbm, w_mid_hbm, b_mid_ref, win_ref, turned_ref, feat_ref, bias_ref,
    w_in_ref, b_in_ref, w_mid_ref, sems,
):
    copies = [
        pltpu.make_async_copy(source, target, sems.at[i])
        for i, (source, target) in enumerate(
            ((w_in_hbm, w_in_ref), (b_in_hbm, b_in_ref), (w_mid_hbm, w_mid_ref))
        )
    ]
    for copy in copies:
        copy.start()
    devices = params_ref.shape[1] * 4 // sets
    group = (owner_ref[0] // 2) % (devices // 4)
    table = feature_table(params_ref, group, sets).astype(jnp.bfloat16)
    for t in range(feat_ref.shape[1] // ROW_TILE):
        hot, _ = one_hot(t, sets)
        feat = dot(table, hot).astype(jnp.bfloat16)
        feat_ref[:, t * ROW_TILE : (t + 1) * ROW_TILE] = feat
    bias_ref[...] = jnp.broadcast_to((0.5 * b_mid_ref[...]).T, bias_ref.shape)
    for copy in copies:
        copy.wait()
    weights_in = w_in_ref[...].astype(jnp.float32)
    bias_in = [piece.astype(jnp.float32) for piece in bf16_pieces(b_in_ref[...])]
    pad = jnp.zeros((FEATURE_ROWS - weights_in.shape[0] - 3, WIDTH), jnp.float32)
    win = (0.5 * jnp.concatenate([weights_in] + bias_in + [pad], 0)).T
    win_ref[...] = win.astype(jnp.bfloat16)
    turned_ref[...] = (0.5 * w_mid_ref[...].astype(jnp.float32)).T.astype(jnp.bfloat16)


def prepare(owner, params, w_in, b_in, w_mid, b_mid, sets):
    smem = pl.BlockSpec(memory_space=pltpu.SMEM)
    vmem = pl.BlockSpec(memory_space=pltpu.VMEM)
    hbm = pl.BlockSpec(memory_space=pltpu.HBM)
    return pl.pallas_call(
        functools.partial(prepare_kernel, sets),
        in_specs=[smem, vmem] + [hbm] * 3 + [vmem],
        out_specs=[vmem] * 4,
        out_shape=[
            jax.ShapeDtypeStruct((WIDTH, FEATURE_ROWS), jnp.bfloat16),
            jax.ShapeDtypeStruct((WIDTH, WIDTH), jnp.bfloat16),
            jax.ShapeDtypeStruct((FEATURE_ROWS, sets * PAIRS), jnp.bfloat16),
            jax.ShapeDtypeStruct((WIDTH, LANES), jnp.float32),
        ],
        scratch_shapes=[
            pltpu.VMEM(w_in.shape, jnp.bfloat16),
            pltpu.VMEM((1, WIDTH), jnp.float32),
            pltpu.VMEM((WIDTH, WIDTH), jnp.bfloat16),
            pltpu.SemaphoreType.DMA((3,)),
        ],
        compiler_params=pltpu.CompilerParams(vmem_limit_bytes=16 * 1024 * 1024),
        name="prepare",
    )(
        owner.reshape(1), in_hbm(params), in_hbm(w_in), in_hbm(b_in.reshape(1, -1)), in_hbm(w_mid),
        in_hbm(b_mid.reshape(1, -1)),
    )


def forward_kernel(
    owner_ref, bias_ref, w_out_ref, win_ref, turned_ref, feat_ref,
    hidden_out, curve_out, mixed_out, pred_out, read_ref,
    even_hidden, odd_hidden, even_mixed, odd_mixed,
):
    bf16 = jnp.bfloat16
    tiles = hidden_out.shape[1] // ROW_TILE
    cols = WIDTH // 4
    owner = owner_ref[0]
    block = 2 * (owner // owner_ref[1]) + owner % 2
    own = pl.ds(pl.multiple_of(block * cols, cols), cols)
    read_ref[...] = jnp.broadcast_to((0.5 * w_out_ref[...].astype(jnp.float32)).T, read_ref.shape)
    readout = jnp.broadcast_to(w_out_ref[...].astype(jnp.float32), (16, WIDTH)).astype(bf16)

    def wide(column):
        return jnp.concatenate([column] * (ROW_TILE // LANES), axis=1)

    def span(t):
        return pl.ds(pl.multiple_of(t * ROW_TILE, ROW_TILE), ROW_TILE)

    def step(t, new, old, first=True, second=True, third=True):
        new_hidden, new_mixed = new
        old_hidden, old_mixed = old
        if first:
            feat = feat_ref[:, span(t)]

        def products(c):
            return (
                dot(turned_ref[c, :], old_hidden[...]) if second else None,
                dot(win_ref[c, :], feat) if first else None,
            )

        ahead = products(CHUNKS[0])
        if third:
            predicted = dot(readout, new_mixed[...])
            mixed_out[:, span(t - 2)] = new_mixed[own, :]
        for n, c in enumerate(CHUNKS):
            half_mid, half_in = ahead
            if n + 1 < len(CHUNKS):
                ahead = products(CHUNKS[n + 1])
            if second:
                half_mid = half_mid + wide(bias_ref[c, :])
                wave = jnp.tanh(half_mid)
                turn = half_mid * wave
                old_mixed[c, :] = (half_mid + turn).astype(bf16)
                curve_out[c, span(t - 1)] = (1.0 + wave) * (1.0 + half_mid - turn) * wide(read_ref[c, :])
            if first:
                value = (half_in + half_in * jnp.tanh(half_in)).astype(bf16)
                new_hidden[c, :] = value
                hidden_out[c, span(t)] = value
        if third:
            pred_out[0:1, span(t - 2)] = predicted[0:1]

    even, odd = (even_hidden, even_mixed), (odd_hidden, odd_mixed)
    step(0, even, odd, second=False, third=False)
    step(1, odd, even, third=False)

    def two_steps(u, carry):
        step(2 * u + 2, even, odd)
        step(2 * u + 3, odd, even)
        return carry

    lax.fori_loop(0, (tiles - 2) // 2, two_steps, 0)
    buffers = [even, odd]
    for t in range(2 + (tiles - 2) // 2 * 2, tiles + 2):
        step(t, buffers[t % 2], buffers[1 - t % 2], first=t < tiles, second=t <= tiles)


def forward(place, bias, w_out, win, turned, feat):
    rows = feat.shape[1]
    cols = WIDTH // 4
    vmem = pl.BlockSpec(memory_space=pltpu.VMEM)
    smem = pl.BlockSpec(memory_space=pltpu.SMEM)
    outs = [
        ((WIDTH, rows), jnp.bfloat16),
        ((WIDTH, rows), jnp.float32),
        ((cols, rows), jnp.bfloat16),
        ((1, rows), jnp.float32),
    ]
    return pl.pallas_call(
        forward_kernel,
        in_specs=[smem] + [vmem] * 5,
        out_specs=[vmem] * len(outs),
        out_shape=[pltpu.VMEM(shape, kind) for shape, kind in outs[:-1]]
        + [jax.ShapeDtypeStruct(*outs[-1])],
        scratch_shapes=[
            pltpu.VMEM((WIDTH, LANES), jnp.float32),
        ]
        + [pltpu.VMEM((WIDTH, ROW_TILE), jnp.bfloat16)] * 4,
        compiler_params=pltpu.CompilerParams(vmem_limit_bytes=FORWARD_VMEM),
        cost_estimate=pl.CostEstimate(
            flops=2 * rows * WIDTH * (WIDTH + 32), bytes_accessed=4 << 20, transcendentals=0
        ),
        name="forward",
    )(place, bias, w_out.reshape(1, -1), win, turned, feat)


def backward_kernel(
    inv_sets, owner_ref, sums_ref, near_ref, far_ref, both_ref, hidden_ref, curve_ref, mixed_ref, pred_ref, win_ref,
    feat_ref, w_mid_hbm, b_out_ref, keep_x, send_x, keep_y, send_y, keep_z, send_z, prices_ref,
    left_ref, back_ref, slope_ref, even_delta, odd_delta, delta_in_ref, own_delta_ref, bias_ref,
    read_ref, pieces_ref, sem,
):
    bf16 = jnp.bfloat16
    sets = sums_ref.shape[0]
    rows = hidden_ref.shape[1]
    groups = pieces_ref.shape[0]
    piece_rows = WIDTH // groups
    cols = WIDTH // 4
    owner = owner_ref[0]
    block = 2 * (owner // (2 * groups)) + owner % 2
    own = pl.ds(pl.multiple_of(block * cols, cols), cols)
    fetch = pltpu.make_async_copy(w_mid_hbm.at[own, :], back_ref, sem)
    fetch.start()

    left_ref[...] = jnp.zeros_like(left_ref)
    sums = (sums_ref[...] + near_ref[...]) + (far_ref[...] + both_ref[...])
    set_dev = sets // 4
    prices = sums[:set_dev]
    for b in range(1, 4):
        prices = jnp.where(block == b, sums[b * set_dev : (b + 1) * set_dev], prices)
    prices_ref[...] = prices
    for p, piece in enumerate(bf16_pieces(sums)):
        left_ref[p * sets : (p + 1) * sets, :PAIRS] = piece.astype(jnp.float32)
    left = left_ref[...].astype(bf16)
    tiles = [slice(first, first + ROW_TILE) for first in range(0, rows, ROW_TILE)]
    for t, here in enumerate(tiles):
        hot, group_set = one_hot(t, sets)
        looked = dot(left, hot)
        target = looked[:sets] + looked[sets : 2 * sets] + looked[2 * sets :]
        member = lax.broadcasted_iota(jnp.int32, (sets, ROW_TILE), 0)
        target = jnp.sum(jnp.where(member == group_set, target, 0.0), axis=0, keepdims=True)
        slope_ref[0:1, here] = (pred_ref[0:1, here] + b_out_ref[0] - target) * inv_sets
    fetch.wait()
    for t, here in enumerate(tiles):
        delta_ref = (even_delta, odd_delta)[t % 2]
        slope = slope_ref[0:1, here]
        for c in CHUNKS:
            delta_ref[c, :] = (slope * curve_ref[c, here]).astype(bf16)
        backward = dot(back_ref[...], delta_ref[...])
        own_delta = (slope * curve_ref[own, here]).astype(bf16)
        own_delta_ref[:, here] = own_delta
        bias = own_delta.astype(jnp.float32)
        read = mixed_ref[:, here].astype(jnp.float32) * slope
        bias = bias[:, :LANES] + bias[:, LANES:]
        read = read[:, :LANES] + read[:, LANES:]
        bias_ref[...] = bias if t == 0 else bias_ref[...] + bias
        read_ref[...] = read if t == 0 else read_ref[...] + read
        half = dot(win_ref[own, :], feat_ref[:, here])
        wave = jnp.tanh(half)
        curve = (0.5 * (1.0 + wave)) * (1.0 + half * (1.0 - wave))
        delta_in_ref[:, here] = (backward * curve).astype(bf16)

    for c in CHUNKS:
        total = dot_rows(hidden_ref[c, :], own_delta_ref[...])
        for first in range(0, CHUNK, piece_rows):
            j = (c.start + first) // piece_rows
            part = total[first : first + piece_rows]
            pieces_ref[j, 0:piece_rows, :] = part[:, :LANES]
            pieces_ref[j, piece_rows + 8 :, :] = part[:, LANES:]
    extra = [dot_rows(delta_in_ref[...], feat_ref[...]).T[0:7]]
    extra.append(jnp.sum(bias_ref[...].T, axis=0, keepdims=True))
    extra.append(jnp.sum(read_ref[...].T, axis=0, keepdims=True))
    total = jnp.sum(slope_ref[...], axis=1, keepdims=True)
    extra.append(jnp.broadcast_to(total, (1, cols)))
    extra.append(jnp.zeros((6, cols), jnp.float32))
    extra = jnp.concatenate(extra, 0)
    for j in range(groups):
        lanes = slice((j % 2) * LANES, (j % 2 + 1) * LANES)
        part = extra[8 * (j // 2) : 8 * (j // 2) + 8, lanes] if j < 4 else jnp.zeros((8, LANES))
        pieces_ref[j, piece_rows : piece_rows + 8, :] = part
    group = (owner // 2) % groups
    cuts = part_cuts(groups)
    for bit, (keep, send) in enumerate(((keep_x, send_x), (keep_y, send_y), (keep_z, send_z))):
        mine = (group // 2**bit) % 2
        for i in range(groups // 2):
            base = (i >> bit << (bit + 1)) + (i & (2**bit - 1))
            keep[i] = pieces_ref[base + mine * 2**bit, cuts[bit] : cuts[bit + 1], :]
            send[i] = pieces_ref[base + (1 - mine) * 2**bit, cuts[bit] : cuts[bit + 1], :]


def part_cuts(groups):
    rows = 2 * (WIDTH // groups) + 8
    third = rows // 24 * 8
    return (0, third, 2 * third, rows)


def backward(owner, sums, saved, win, feat, w_mid, b_out, inv_sets, groups):
    sets = sums[0].shape[0]
    cuts = part_cuts(groups)
    rows = sets * PAIRS
    cols = WIDTH // 4
    vmem = pl.BlockSpec(memory_space=pltpu.VMEM)
    smem = pl.BlockSpec(memory_space=pltpu.SMEM)
    hbm = pl.BlockSpec(memory_space=pltpu.HBM)
    return pl.pallas_call(
        functools.partial(backward_kernel, inv_sets),
        in_specs=[smem] + [vmem] * 10 + [hbm, smem],
        out_specs=[vmem] * 7,
        out_shape=[
            jax.ShapeDtypeStruct((groups // 2, stop - start, LANES), jnp.float32)
            for start, stop in zip(cuts, cuts[1:])
            for _ in range(2)
        ]
        + [jax.ShapeDtypeStruct((sets // 4, PAIRS), jnp.float32)],
        scratch_shapes=[
            pltpu.VMEM((3 * sets, LANES), jnp.float32),
            pltpu.VMEM((cols, WIDTH), jnp.bfloat16),
            pltpu.VMEM((1, rows), jnp.float32),
            pltpu.VMEM((WIDTH, ROW_TILE), jnp.bfloat16),
            pltpu.VMEM((WIDTH, ROW_TILE), jnp.bfloat16),
            pltpu.VMEM((cols, rows), jnp.bfloat16),
            pltpu.VMEM((cols, rows), jnp.bfloat16),
            pltpu.VMEM((cols, LANES), jnp.float32),
            pltpu.VMEM((cols, LANES), jnp.float32),
            pltpu.VMEM((groups, 2 * (WIDTH // groups) + 8, LANES), jnp.float32),
            pltpu.SemaphoreType.DMA,
        ],
        compiler_params=pltpu.CompilerParams(vmem_limit_bytes=BACKWARD_VMEM),
        name="backward",
    )(owner.reshape(1), *sums, *saved, win, feat, in_hbm(w_mid), b_out)


def scaling_kernel(layout, groups, owner_ref, *refs):
    blocks = refs[: len(layout)]
    w_in_ref, b_in_ref, w_mid_ref, b_mid_ref, w_out_ref, b_out_ref, extra_ref, small_ref = refs[
        len(layout) :
    ]
    piece_rows = WIDTH // groups
    cols = WIDTH // 4
    owner = owner_ref[0]
    parts = []
    for ref, (masks, contents) in zip(blocks, layout):
        for i, mask in enumerate(masks):
            device = owner ^ mask
            index = (device >> 1) & (groups - 1)
            column = 2 * (device // (2 * groups)) + (device & 1)
            start = 0
            for content in contents:
                if content == "extra":
                    extra_ref[index, column] = ref[i, start : start + 8, :]
                    start += 8
                else:
                    parts.append((ref, i, start, index, column, content == "right"))
                    start += piece_rows

    total = jnp.zeros((8, LANES), jnp.float32)
    for ref, i, start, index, column, right in parts:
        part = ref[i, start : start + piece_rows, :]
        total = total + jnp.sum((part * part).reshape(-1, 8, LANES), axis=0)
    for column in range(4):
        for j in range(4):
            first = column * cols + (j % 2) * LANES
            small_ref[8 * (j // 2) : 8 * (j // 2) + 8, first : first + LANES] = extra_ref[j, column]
    small = small_ref[...]
    squares = jnp.sum(small * small, axis=1, keepdims=True)
    bias_out = small_ref[9:10, 0:1]
    last = bias_out * bias_out

    def factor(total, entries):
        return lax.rsqrt(total / entries + EPSILON)

    total = jnp.sum(jnp.sum(total, axis=1, keepdims=True), axis=0, keepdims=True)
    scale_mid = factor(total + squares[7:8], WIDTH * WIDTH + WIDTH)
    scale_in = factor(jnp.sum(squares[0:7], axis=0, keepdims=True), 7 * WIDTH)
    scale_out = factor(squares[8:9] + last, WIDTH + 1)
    w_in_ref[...] = small[0:6] * scale_in
    b_in_ref[...] = small[6:7] * scale_in
    b_mid_ref[...] = small[7:8] * scale_mid
    w_out_ref[...] = small[8:9] * scale_out
    b_out_ref[...] = bias_out * scale_out
    for ref, i, start, index, column, right in parts:
        rows = pl.ds(pl.multiple_of(index * piece_rows, piece_rows), piece_rows)
        first = pl.multiple_of(column * cols + (LANES if right else 0), LANES)
        part = ref[i, start : start + piece_rows, :]
        w_mid_ref[rows, pl.ds(first, LANES)] = part * scale_mid


def scaled(owner, groups, received):
    vmem = pl.BlockSpec(memory_space=pltpu.VMEM)
    shapes = [(6, WIDTH), (1, WIDTH), (WIDTH, WIDTH), (1, WIDTH), (1, WIDTH), (1, 1)]
    layout = [(masks, contents) for _, masks, contents in received]
    return pl.pallas_call(
        functools.partial(scaling_kernel, layout, groups),
        in_specs=[pl.BlockSpec(memory_space=pltpu.SMEM)] + [vmem] * len(received),
        out_specs=[vmem] * 6,
        out_shape=[jax.ShapeDtypeStruct(shape, jnp.float32) for shape in shapes],
        scratch_shapes=[
            pltpu.VMEM((max(groups, 4), 4, 8, LANES), jnp.float32),
            pltpu.VMEM((16, WIDTH), jnp.float32),
        ],
        compiler_params=pltpu.CompilerParams(vmem_limit_bytes=32 * 1024 * 1024),
        name="scaling",
    )(owner.reshape(1), *[array for array, _, _ in received])


def swap(array, bit, devices):
    return lax.ppermute(array, "paths", [(i, i ^ bit) for i in range(devices)])


def pick(array, index):
    return lax.dynamic_index_in_dim(array, index, 0, keepdims=False)


def halved(part, left, bit, group, devices):
    axis = len(left) - 1 - left.index(bit)
    shape = part.shape[1:]
    cube = part.reshape((2,) * len(left) + shape)
    mine = (group >> bit) % 2
    keep = lax.dynamic_index_in_dim(cube, mine, axis, keepdims=False)
    send = lax.dynamic_index_in_dim(cube, 1 - mine, axis, keepdims=False)
    send, keep = send.reshape((-1,) + shape), keep.reshape((-1,) + shape)
    return keep + swap(send, 2 << bit, devices)


def on_device(params, increments, w_in, b_in, w_mid, b_mid, w_out, b_out):
    devices = lax.axis_size("paths")
    top = devices // 2
    groups = devices // 4
    total_paths = increments.shape[2] * devices
    set_count = params.shape[0]
    set_dev = set_count // devices
    owner = lax.axis_index("paths")
    core = owner % 2
    high = owner // top
    group = (owner // 2) % groups
    block = 2 * high + core
    turned = params.T

    sums = payoff_sums(turned, increments, groups).reshape(groups, 4 * set_dev, PAIRS)
    win, weights, feat, bias = prepare(owner, turned, w_in, b_in, w_mid, b_mid, 4 * set_dev)
    lanes = [[2 * j + c + top * h for j in range(groups)] for h in range(2) for c in range(2)]
    parts = lax.all_to_all(sums, "paths", 0, 0, axis_index_groups=lanes, tiled=True)
    parts, win = lax.optimization_barrier((parts, win))
    sums = jnp.sum(parts, axis=0) / total_paths
    sums = [sums] + [swap(sums, mask, devices) for mask in (1, top, top + 1)]

    place = jnp.stack([owner, jnp.int32(top)])
    saved = forward(place, bias, w_out, win, weights, feat)
    *parts, prices = backward(
        owner, sums, saved, win, feat, w_mid, b_out, 1.0 / set_count, groups
    )

    bits = [bit for bit in range(groups.bit_length() - 1)]
    orders = [bits[first:] + bits[:first] for first in range(3)]
    parts = [
        parts[2 * n] + swap(parts[2 * n + 1], 2 << order[0], devices)
        for n, order in enumerate(orders)
    ]
    for step in range(1, len(bits)):
        parts = [
            halved(part, sorted(order[step:]), order[step], group, devices)
            for part, order in zip(parts, orders)
        ]

    own = jnp.concatenate(parts, axis=1)
    far = (0, top + top // 2, top, top // 2)
    whole = jnp.concatenate([own] + [swap(own, mask, devices) for mask in far[1:]], axis=0)
    received = [(whole, far, ("left", "extra", "right"))]
    split = WIDTH // groups + 8
    held_a, held_b = whole[:, :split], whole[:, split:]
    order = [2 << bit for bit in bits[:-1]]
    masks_a = masks_b = far
    for bit_a, bit_b in zip(order, order[1:] + order[:1]):
        came_a, came_b = swap(held_a, bit_a, devices), swap(held_b, bit_b, devices)
        new_a = tuple(mask ^ bit_a for mask in masks_a)
        new_b = tuple(mask ^ bit_b for mask in masks_b)
        if bit_a == order[-1]:
            near = [swap(array, 1, devices) for array, _, _ in received]
            came_a, came_b, *near = lax.optimization_barrier((came_a, came_b, *near))
        received += [(came_a, new_a, ("left", "extra")), (came_b, new_b, ("right",))]
        if bit_a != order[-1]:
            held_a = jnp.concatenate([held_a, came_a], axis=0)
            held_b = jnp.concatenate([held_b, came_b], axis=0)
        masks_a, masks_b = masks_a + new_a, masks_b + new_b
    near += [swap(array, 1, devices) for array, _, _ in received[len(near) :]]
    received += [
        (array, tuple(mask ^ 1 for mask in masks), contents)
        for array, (_, masks, contents) in zip(near, received)
    ]
    result = scaled(owner, groups, received)
    direction_w_in, direction_b_in, direction_w_mid, direction_b_mid, direction_w_out, direction_b_out = result
    return (
        prices,
        direction_w_in,
        direction_b_in.reshape(WIDTH),
        direction_w_mid,
        direction_b_mid.reshape(WIDTH),
        direction_w_out.reshape(WIDTH),
        direction_b_out.reshape(1),
    )


def solution(mesh):
    in_specs = (P(), P(None, None, "paths"), P(), P(), P(), P(), P(), P())
    out_specs = (P("paths", None), P(), P(), P(), P(), P(), P())
    return jax.shard_map(
        on_device, mesh=mesh, in_specs=in_specs, out_specs=out_specs, check_vma=False
    )
```
